32 devices in a mesh: gx: 16 (over z, y, core), gy: 2 (over x).
Axes of the slice: x: 2, y: 2, z: 4, core: 2. Of those that a mesh axis runs over, the one named last changes fastest.
Arguments:
- source: float32 [64, 64, 256], P('gx', 'gy'), may hold values from -96 to 96
- region: int32 [64, 64, 256], P('gx', 'gy'), may hold values from 0 to 63
- permeability: float32 [64], replicated, may hold values from 0.1 to 10
- owners: int32 [16, 2], P('gx'), may hold values from 0 to 1
Outputs:
- pressure: float32 [64, 64, 256], P('gx', 'gy')
The draws below stay inside these ranges and needn't reach their ends.
All inputs are finite; a program needn't handle non-finite values.
Results may differ from the reference program's by a relative error of at most 0.0001.
Values sent between devices are 32-bit elements; how exact they have to be, the bound alone decides.
A program may use at most 64 MiB of HBM per device.

```python
import math
import jax
import jax.numpy as jnp

CX = 4
CY = 32
REGIONS = 64
PRE_SWEEPS = 2
POST_SWEEPS = 2
COARSE_SWEEPS = 6
NX = 64
NY = 64
NZ = 256
N_GX = 16
N_GY = 2


def with_ends(array, own_key, least, top_value):
    place = [jax.random.randint(jax.random.fold_in(own_key, axis), (), 0, length) for axis, length in enumerate(array.shape)]
    main_axis = array.shape.index(max(array.shape))
    next_to = place[:main_axis] + [(place[main_axis] + 1) % array.shape[main_axis]] + place[main_axis + 1:]
    return array.at[tuple(place)].set(least).at[tuple(next_to)].set(top_value)


def steps_of(rng, extent, pieces, low, largest):
    factor_of = 1.0
    for dim, blocks in pieces:
        draws = jax.random.uniform(jax.random.fold_in(jax.random.fold_in(rng, 6), dim), (blocks,), jnp.float32, low / len(pieces), largest / len(pieces))
        factor_of = factor_of * jnp.repeat(jnp.exp(draws), extent[dim] // blocks).reshape((-1,) + (1,) * (len(extent) - 1 - dim))
    return factor_of


def centred(own_key, dims, width, limit, shards=(), kind=jnp.bfloat16):
    loudness = steps_of(own_key, dims, shards, -0.22, 0.18) if shards else 1.0
    array = jax.random.normal(own_key, dims, jnp.float32) * width * loudness
    return jnp.minimum(jnp.maximum(array, -limit), limit).astype(kind)


def setup_inputs(seed: int = 0) -> dict:
    seeds = jax.random.split(jax.random.key(seed), 5)
    return {
        "source": centred(seeds[0], (NX, NY, NZ), 16.0, 96.0, ((0, 16), (1, 2)), jnp.float32),
        "region": with_ends(jax.random.randint(seeds[1], (NX, NY, NZ), 0, REGIONS), jax.random.fold_in(seeds[1], 1), 0, REGIONS - 1).astype(jnp.int32),
        "permeability": jnp.clip(jnp.exp(jax.random.uniform(seeds[2], (REGIONS,), jnp.float32, math.log(0.1), math.log(10.0))), 0.1, 10.0),
        "owners": with_ends(jax.random.randint(seeds[3], (N_GX, N_GY), 0, N_GY), jax.random.fold_in(seeds[3], 1), 0, N_GY - 1).astype(jnp.int32),
    }


RELAX_WEIGHT = 0.6
MASS_TERM = 0.1


def stencil_sum(padded):
    blended = 0.5 * padded[:-2] + padded[1:-1] + 0.5 * padded[2:]
    blended = 0.5 * blended[:, :-2] + blended[:, 1:-1] + 0.5 * blended[:, 2:]
    blended = 0.5 * blended[:, :, :-2] + blended[:, :, 1:-1] + 0.5 * blended[:, :, 2:]
    return 2.0 * (blended - padded[1:-1, 1:-1, 1:-1])


def pad_all(values):
    return jnp.pad(values, 1)


def operate(values, conduct, cond_pad, diagonal, factor, extend):
    value_pad = extend(values)
    return diagonal * values - factor * (conduct * stencil_sum(value_pad) + stencil_sum(cond_pad * value_pad))


def coarsen(values):
    size_x, size_y, size_z = values.shape
    return values.reshape(size_x // 2, 2, size_y // 2, 2, size_z // 2, 2).mean(axis=(1, 3, 5))


def local_ratio(numer, denom):
    return jnp.sum(numer) / jnp.maximum(jnp.sum(denom), 1.0)


def coarse_sweeps(residual, conduct, cond_pad, region_mask, extend, totals):
    diagonal = MASS_TERM + 0.125 * (14.0 * conduct + stencil_sum(cond_pad))
    correction = jnp.zeros_like(residual)
    for iteration in range(COARSE_SWEEPS):
        applied = operate(correction, conduct, cond_pad, diagonal, 0.125, extend)
        correction = region_mask * (correction + RELAX_WEIGHT * (residual - applied) / diagonal)
    applied = operate(correction, conduct, cond_pad, diagonal, 0.125, extend)
    ratio = totals(region_mask * (residual - applied), region_mask * diagonal)
    return correction + region_mask * ratio


def solve_region(residual, conduct, region_mask):
    return coarse_sweeps(residual, conduct, jnp.pad(conduct, 1), region_mask, pad_all, local_ratio)


def reference(source, region, permeability, owners):
    conduct = permeability[region]
    cond_pad = jnp.pad(conduct, 1)
    diagonal = MASS_TERM + 0.5 * (14.0 * conduct + stencil_sum(cond_pad))
    pressure = jnp.zeros_like(source)
    for iteration in range(PRE_SWEEPS):
        applied = operate(pressure, conduct, cond_pad, diagonal, 0.5, pad_all)
        pressure = pressure + RELAX_WEIGHT * (source - applied) / diagonal
    residual = source - operate(pressure, conduct, cond_pad, diagonal, 0.5, pad_all)
    coarse_res = coarsen(residual)
    coarse_cond = coarsen(conduct)
    size_x, size_y, size_z = coarse_res.shape
    slab_res = coarse_res.reshape(N_GX, CX // 2, size_y, size_z)
    slab_cond = coarse_cond.reshape(N_GX, CX // 2, size_y, size_z)
    owner_cells = jnp.repeat(owners, CY // 2, axis=1)
    correction = jnp.zeros_like(slab_res)
    for member in range(N_GY):
        region_mask = (owner_cells == member).astype(jnp.float32)[:, None, :, None]
        full_mask = jnp.broadcast_to(region_mask, slab_res.shape)
        correction = correction + jax.vmap(solve_region)(slab_res * region_mask, slab_cond * region_mask, full_mask)
    correction = correction.reshape(size_x, size_y, size_z)
    fine_corr = jnp.broadcast_to(correction[:, None, :, None, :, None], (size_x, 2, size_y, 2, size_z, 2)).reshape(source.shape)
    pressure = pressure + fine_corr
    for iteration in range(POST_SWEEPS):
        applied = operate(pressure, conduct, cond_pad, diagonal, 0.5, pad_all)
        pressure = pressure + RELAX_WEIGHT * (source - applied) / diagonal
    return pressure
```

```python
import functools

import jax
import jax.numpy as jnp
from jax import lax
from jax.experimental import pallas as pl
from jax.experimental.pallas import tpu as pltpu
from jax.sharding import PartitionSpec as P

POST_SWEEPS = 2
COARSE_SWEEPS = 6
RELAX_WEIGHT = 0.6
MASS_TERM = 0.1

MESH = pl.DeviceIdType.MESH
WIDE = 3
HALF = 4
REGION, SOURCE, ITERATE = 0, 1, 2
WIDTHS = (3, 2, 2)
STEPS = ((-1, -1), (1, -1), (-1, 1), (1, 1), (0, -1), (0, 1), (-1, 0), (1, 0))


def kernel(
    n_gx, n_gy,
    owners_in, table_in, source_ref, region_ref, out_ref,
    owners_ref, table_ref, labels, source, iterate, cond, weight, diag2, group, holders, squeezed, whole_corr, spread, wide,
    send_sem, recv_sem, g_send, g_recv, h_send, h_recv, in_sem,
):
    nx, ny, nz = out_ref.shape
    cx, cy, cz = nx // 2, ny // 2, nz // 2
    first, last = WIDE, WIDE + nx
    gx, gy = lax.axis_index("gx"), lax.axis_index("gy")
    fields = (labels, source, iterate)

    def exists(dx, dy):
        x, y = gx + dx, gy + dy
        return (x >= 0) & (x < n_gx) & (y >= 0) & (y < n_gy)

    near_slabs = [
        (dx, off) for dx in (-1, 1, 0) for off in reversed(range(n_gy)) if (dx, off) != (0, 0)
    ]

    barrier = pltpu.get_barrier_semaphore()
    count = jnp.int32(0)
    for dx, off in near_slabs:
        near = exists(dx, 0)

        @pl.when(near)
        def _():
            pl.semaphore_signal(
                barrier, inc=1, device_id=(gx + dx, lax.rem(gy + off, n_gy)), device_id_type=MESH
            )

        count = count + near.astype(jnp.int32)

    load_source = pltpu.make_async_copy(
        source_ref, source.at[pl.ds(first, nx), pl.ds(0, ny)], in_sem.at[0]
    )
    load_region = pltpu.make_async_copy(
        region_ref, labels.at[pl.ds(first, nx), pl.ds(0, ny)], in_sem.at[1]
    )
    load_table = pltpu.make_async_copy(table_in, table_ref, in_sem.at[2])
    load_owners = pltpu.make_async_copy(owners_in, owners_ref, in_sem.at[3])
    load_region.start()
    load_table.start()
    load_source.start()
    load_owners.start()

    def landing(kind, dx, dy):
        w = WIDTHS[kind]
        start, size = {0: (first, nx), -1: (last, w), 1: (first - w, w)}[dx]
        row, high = {0: (0, ny), -1: (ny, HALF), 1: (ny + HALF, HALF)}[dy]
        return fields[kind].at[pl.ds(start, size), pl.ds(row, high)]

    def remote(kind, which):
        dx, dy = STEPS[which]
        w = WIDTHS[kind]
        base = first if kind == ITERATE else 0
        start, size = {0: (0, nx), -1: (0, w), 1: (nx - w, w)}[dx]
        row, high = {0: (0, ny), -1: (0, HALF), 1: (ny - HALF, HALF)}[dy]
        origin = (region_ref, source_ref, iterate)[kind]
        return pltpu.make_async_remote_copy(
            src_ref=origin.at[pl.ds(base + start, size), pl.ds(row, high)],
            dst_ref=landing(kind, dx, dy),
            send_sem=send_sem.at[kind, which],
            recv_sem=recv_sem.at[kind, which],
            device_id=(gx + dx, gy + dy),
            device_id_type=MESH,
        )

    def send(kind):
        for which, (dx, dy) in enumerate(STEPS):
            @pl.when(exists(dx, dy))
            def _():
                remote(kind, which).start()

    def receive(kind, inner):
        for which, (dx, dy) in enumerate(STEPS):
            if (dx == 0) == inner:
                @pl.when(exists(-dx, -dy))
                def _():
                    remote(kind, which).wait_recv()

    def finish(kind):
        for which, (dx, dy) in enumerate(STEPS):
            @pl.when(exists(dx, dy))
            def _():
                remote(kind, which).wait_send()

    def gather(kind, dx, off):
        at = pl.ds(pl.multiple_of(gy * cy, 8), cy)
        return pltpu.make_async_remote_copy(
            src_ref=group.at[kind, 1, :, at],
            dst_ref=group.at[kind, 1 - dx, :, at],
            send_sem=g_send.at[kind, dx + 1, off],
            recv_sem=g_recv.at[kind, dx + 1, off],
            device_id=(gx + dx, lax.rem(gy + off, n_gy)),
            device_id_type=MESH,
        )

    def gather_in(kind, dx, off):
        sender = lax.rem(gy + n_gy - off, n_gy)
        theirs = group.at[kind, 1 - dx, :, pl.ds(pl.multiple_of(sender * cy, 8), cy)]
        return pltpu.make_async_remote_copy(
            src_ref=theirs,
            dst_ref=theirs,
            send_sem=g_send.at[kind, dx + 1, off],
            recv_sem=g_recv.at[kind, dx + 1, off],
            device_id=(gx - dx, sender),
            device_id_type=MESH,
        )

    def tell(dx):
        return pltpu.make_async_remote_copy(
            src_ref=holders.at[1],
            dst_ref=holders.at[1 - dx],
            send_sem=h_send.at[(dx + 1) // 2],
            recv_sem=h_recv.at[(dx + 1) // 2],
            device_id=(gx + dx, gy),
            device_id_type=MESH,
        )

    def gather_start(kind):
        for dx, off in near_slabs:
            @pl.when(exists(dx, 0))
            def _():
                gather(kind, dx, off).start()

    def gather_wait(kind):
        for dx, off in near_slabs:
            @pl.when(exists(-dx, 0))
            def _():
                gather_in(kind, dx, off).wait_recv()

    for dx, dy in STEPS:
        @pl.when(jnp.logical_not(exists(-dx, -dy)))
        def _():
            ref = landing(REGION, dx, dy)
            ref[...] = jnp.full(ref.shape, table_ref.shape[1], jnp.int32)
            for kind in (SOURCE, ITERATE):
                ref = landing(kind, dx, dy)
                ref[...] = jnp.zeros(ref.shape, jnp.float32)
    for dx in (-1, 1):
        @pl.when(jnp.logical_not(exists(-dx, 0)))
        def _():
            for kind in range(2):
                ref = group.at[kind, 1 - dx]
                ref[...] = jnp.zeros(ref.shape, jnp.float32)
            ref = holders.at[1 - dx]
            ref[...] = jnp.zeros(ref.shape, jnp.float32)

    with jax.named_scope("wait_neighbours"):
        pl.semaphore_wait(barrier, count)
    send(REGION)
    send(SOURCE)

    load_table.wait()
    with jax.named_scope("wait_own_region"):
        load_region.wait()
    regions = table_ref.shape[1]
    pair = jnp.concatenate([table_ref[...], jnp.zeros((1, 128 - regions), jnp.float32)], axis=1)
    table = jnp.broadcast_to(pair, (8, 128))

    def look_up(planes, tiles):
        for i in planes:
            for r in tiles:
                for c in range(0, nz, 128):
                    spot = labels[i, pl.ds(r, 8), pl.ds(c, 128)]
                    cond[i, pl.ds(r, 8), pl.ds(c, 128)] = jnp.take_along_axis(table, spot, axis=1)

    look_up(range(first, last), range(0, ny, 8))

    lane = lax.broadcasted_iota(jnp.int32, (1, nz), 1)
    z_low = jnp.where(lane == 0, 0.0, 0.5)
    z_high = jnp.where(lane == nz - 1, 0.0, 0.5)
    rows = ny + 8

    def blend(a, b, c, keep=rows):
        u = b + 0.5 * (a + c)
        u = u + 0.5 * (pltpu.roll(u, 1, 0) + pltpu.roll(u, rows - 1, 0))
        u = u[:keep]
        return u + z_low * pltpu.roll(u, 1, 1) + z_high * pltpu.roll(u, nz - 1, 1)

    lane128 = lax.broadcasted_iota(jnp.int32, (8, 128), 1)
    even = lax.rem(2 * lane128, jnp.int32(128))
    half_of = lane128 // 2

    def coarsen(pairs, kind):
        for i, pair_sum in enumerate(pairs):
            total = pair_sum + pltpu.roll(pair_sum, nz - 1, 1)
            for r in range(0, ny, 8):
                low = jnp.take_along_axis(total[r:r + 8, :128], even, axis=1)
                high = jnp.take_along_axis(total[r:r + 8, 128:], even, axis=1)
                squeezed[i, pl.ds(r, 8), :] = jnp.where(lane128 < 64, low, high)
            block = squeezed[i, pl.ds(0, cy, stride=2), :] + squeezed[i, pl.ds(1, cy, stride=2), :]
            group[kind, 1, i, pl.ds(pl.multiple_of(gy * cy, 8), cy), :] = 0.125 * block

    coarsen(
        [cond[first + 2 * i, pl.ds(0, ny), :] + cond[first + 2 * i + 1, pl.ds(0, ny), :]
         for i in range(cx)],
        0,
    )
    load_owners.wait()
    for c in range(n_gy):
        holders[1, c] = jnp.full((8, cz), owners_ref[0, c].astype(jnp.float32))

    row = lax.broadcasted_iota(jnp.int32, (rows, 1), 0)
    y = gy * ny + jnp.where(row < ny + HALF, row, row - rows)
    in_y = jnp.where((y >= 0) & (y < n_gy * ny), RELAX_WEIGHT, 0.0)

    def weigh(planes):
        for i in planes:
            mine = cond[i]
            mixed = blend(cond[i - 1], mine, cond[i + 1])
            x = gx * nx + (i - first)
            in_x = jnp.where((x >= 0) & (x < n_gx * nx), 1.0, 0.0)
            weight[i] = (in_y * in_x) / (MASS_TERM + 6.0 * mine + mixed)
            diag2[i] = MASS_TERM + 8.0 * mine + mixed

    with jax.named_scope("wait_region_rows"):
        receive(REGION, True)
    look_up(range(first, last), (ny,))
    weigh(range(first + 1, last - 1))
    with jax.named_scope("wait_region_planes"):
        receive(REGION, False)
    edges = [*range(first - WIDE, first), *range(last, last + WIDE)]
    look_up(edges, range(0, rows, 8))
    weigh([first - 2, first - 1, first, last - 1, last, last + 1])
    with jax.named_scope("start_coarse_cond"):
        gather_start(0)
    for dx in (-1, 1):
        @pl.when(exists(dx, 0))
        def _():
            tell(dx).start()

    def defect(i, values, flux, keep=rows):
        at = pl.ds(0, keep)
        lhs = cond[i, at] * blend(values[i - 1], values[i], values[i + 1], keep)
        rhs = blend(flux[i - 1], flux[i], flux[i + 1], keep)
        return source[i, at] - diag2[i, at] * values[i][:keep] + lhs + rhs

    load_source.wait()
    with jax.named_scope("wait_source_rows"):
        receive(SOURCE, True)
    with jax.named_scope("wait_source_planes"):
        receive(SOURCE, False)
    values, flux = {}, {}
    for i in range(first - 2, last + 2):
        values[i] = weight[i] * source[i]
        flux[i] = cond[i] * values[i]
    smooth = {}
    for i in range(first - 1, last + 1):
        smooth[i] = values[i] + weight[i] * defect(i, values, flux)
    flux = {i: cond[i] * smooth[i] for i in smooth}
    pairs = []
    for i in range(cx):
        j = first + 2 * i
        pairs.append(defect(j, smooth, flux, ny) + defect(j + 1, smooth, flux, ny))
    coarsen(pairs, 1)
    with jax.named_scope("start_coarse_res"):
        gather_start(1)
    for i in range(first, last):
        iterate[i, pl.ds(0, ny), :] = smooth[i][:ny]
    send(ITERATE)

    all_y = n_gy * cy
    crow = lax.broadcasted_iota(jnp.int32, (all_y, cz), 0)
    clane = lax.broadcasted_iota(jnp.int32, (1, cz), 1)
    cz_low = jnp.where(clane == 0, 0.0, 0.5)
    cz_high = jnp.where(clane == cz - 1, 0.0, 0.5)

    def coarse_blend(planes, y_low, y_high):
        mixed = []
        for i, u in enumerate(planes):
            near = [planes[j] for j in (i - 1, i + 1) if 0 <= j < cx]
            u = u + 0.5 * functools.reduce(jnp.add, near) if near else u
            u = u + y_low * pltpu.roll(u, 1, 0) + y_high * pltpu.roll(u, all_y - 1, 0)
            mixed.append(u + cz_low * pltpu.roll(u, 1, 1) + cz_high * pltpu.roll(u, cz - 1, 1))
        return mixed

    def total(planes, c):
        whole = functools.reduce(jnp.add, [v[c * cy:(c + 1) * cy] for v in planes])
        return jnp.sum(whole, keepdims=True)

    with jax.named_scope("wait_holders"):
        for dx in (-1, 1):
            @pl.when(exists(-dx, 0))
            def _():
                tell(dx).wait_recv()
    with jax.named_scope("wait_coarse_cond"):
        gather_wait(0)
    slabs = []
    for g in range(3):
        held = [holders[g, c, pl.ds(0, 1), :] for c in range(n_gy)]
        same = lambda a, b: jnp.where(held[a] == held[b], 1.0, 0.0)
        y_low = jnp.where(crow == 0, 0.0, 0.5)
        y_high = jnp.where(crow == all_y - 1, 0.0, 0.5)
        for c in range(1, n_gy):
            tied = 0.5 * same(c - 1, c)
            y_low = jnp.where(crow == c * cy, tied, y_low)
            y_high = jnp.where(crow == c * cy - 1, tied, y_high)
        k = [group[0, g, i] for i in range(cx)]
        mixed = coarse_blend(k, y_low, y_high)
        diag = [MASS_TERM + 1.5 * a + 0.25 * b for a, b in zip(k, mixed)]
        step = [RELAX_WEIGHT / d for d in diag]
        ones = coarse_blend([jnp.ones((all_y, cz), jnp.float32)] * cx, y_low, y_high)
        slabs.append(dict(
            y_low=y_low, y_high=y_high, k=k, step=step,
            keep=[1.0 - s * (d + 0.5 * a) for s, d, a in zip(step, diag, k)],
            mine=[0.25 * s * a for s, a in zip(step, k)],
            theirs=[0.25 * s for s in step],
            drain=[MASS_TERM + 0.25 * a * (8.0 - b) for a, b in zip(k, ones)],
            same=[[same(a, b)[:, :1] for b in range(n_gy)] for a in range(n_gy)],
            diag_sum=[total(diag, c) for c in range(n_gy)],
        ))

    with jax.named_scope("wait_coarse_res"):
        gather_wait(1)
    e = []
    for g, s in enumerate(slabs):
        s["res"] = [group[1, g, i] for i in range(cx)]
        s["start"] = [a * b for a, b in zip(s["step"], s["res"])]
        e.append(s["start"])
    for _ in range(COARSE_SWEEPS - 1):
        for g, s in enumerate(slabs):
            straight = coarse_blend(e[g], s["y_low"], s["y_high"])
            carried = coarse_blend([a * v for a, v in zip(s["k"], e[g])], s["y_low"], s["y_high"])
            e[g] = [
                s["start"][i] + s["keep"][i] * e[g][i]
                + (s["mine"][i] * straight[i] + s["theirs"][i] * carried[i])
                for i in range(cx)
            ]
    keep_planes = ((0, cx - 1), *[(1, i) for i in range(cx)], (2, 0))
    ratios = []
    for g, s in enumerate(slabs):
        left = [r - d * v for r, d, v in zip(s["res"], s["drain"], e[g])]
        left = [total(left, c) for c in range(n_gy)]
        shares = []
        for c in range(n_gy):
            num = functools.reduce(jnp.add, [s["same"][c][b] * left[b] for b in range(n_gy)])
            den = functools.reduce(jnp.add, [s["same"][c][b] * s["diag_sum"][b] for b in range(n_gy)])
            shares.append(num / jnp.maximum(den, 1.0))
        ratios.append(shares)
    for slot, (g, i) in enumerate(keep_planes):
        whole_corr[slot, pl.ds(0, 8), :] = jnp.zeros((8, cz), jnp.float32)
        whole_corr[slot, pl.ds(8 + all_y, 8), :] = jnp.zeros((8, cz), jnp.float32)
        for c in range(n_gy):
            whole_corr[slot, pl.ds(8 + c * cy, cy), :] = e[g][i][c * cy:(c + 1) * cy] + ratios[g][c]

    sub = lax.broadcasted_iota(jnp.int32, (8, cz), 0)
    for i in range(cx + 2):
        mine = whole_corr[i, pl.ds(pl.multiple_of(8 + gy * cy, 8), cy), :]
        below = whole_corr[i, pl.ds(pl.multiple_of(gy * cy, 8), 8), :]
        above = whole_corr[i, pl.ds(pl.multiple_of(8 + gy * cy + cy, 8), 8), :]
        spread[i, pl.ds(0, cy, stride=2), :] = mine
        spread[i, pl.ds(1, cy, stride=2), :] = mine
        for r in range(0, rows, 8):
            if r < ny:
                tile = spread[i, pl.ds(r, 8), :]
            else:
                tile = jnp.where(
                    sub < HALF,
                    jnp.broadcast_to(above[:1], (8, cz)),
                    jnp.broadcast_to(below[7:], (8, cz)),
                )
            for part in range(2):
                wide[i, pl.ds(r, 8), pl.ds(128 * part, 128)] = jnp.take_along_axis(
                    tile, half_of + 64 * part, axis=1
                )
    with jax.named_scope("wait_iterate_rows"):
        receive(ITERATE, True)
    with jax.named_scope("wait_iterate_planes"):
        receive(ITERATE, False)
    values = {
        i: iterate[i] + wide[(i - first + 2) // 2] for i in range(first - 2, last + 2)
    }
    for sweep in range(POST_SWEEPS):
        reach = POST_SWEEPS - 1 - sweep
        keep = rows if reach else ny
        flux = {i: cond[i] * values[i] for i in values}
        values = {
            i: values[i][:keep] + weight[i, pl.ds(0, keep)] * defect(i, values, flux, keep)
            for i in range(first - reach, last + reach)
        }
    for i in range(nx):
        out_ref[i] = values[first + i][:ny]

    with jax.named_scope("wait_sends"):
        for kind in range(3):
            finish(kind)
        for dx in (-1, 1):
            @pl.when(exists(dx, 0))
            def _():
                tell(dx).wait_send()
        for kind in range(2):
            for dx, off in near_slabs:
                @pl.when(exists(dx, 0))
                def _():
                    gather(kind, dx, off).wait_send()


def on_device(source, region, permeability, owners, *, n_gx, n_gy):
    nx, ny, nz = source.shape
    planes = nx + 2 * WIDE
    cx, all_y, cz = nx // 2, n_gy * ny // 2, nz // 2
    f32 = jnp.float32
    return pl.pallas_call(
        functools.partial(kernel, n_gx, n_gy),
        out_shape=jax.ShapeDtypeStruct(source.shape, f32),
        in_specs=[pl.BlockSpec(memory_space=pltpu.HBM)] * 4,
        out_specs=pl.BlockSpec(memory_space=pltpu.VMEM),
        scratch_shapes=[
            pltpu.SMEM((1, n_gy), jnp.int32),
            pltpu.VMEM((1, permeability.shape[0]), f32),
            pltpu.VMEM((planes, ny + 8, nz), jnp.int32),
            pltpu.VMEM((planes, ny + 8, nz), f32),
            pltpu.VMEM((planes, ny + 8, nz), f32),
            pltpu.VMEM((planes, ny + 8, nz), f32),
            pltpu.VMEM((planes, ny + 8, nz), f32),
            pltpu.VMEM((planes, ny + 8, nz), f32),
            pltpu.VMEM((2, 3, cx, all_y, cz), f32),
            pltpu.VMEM((3, n_gy, 8, cz), f32),
            pltpu.VMEM((cx, ny, cz), f32),
            pltpu.VMEM((cx + 2, all_y + 16, cz), f32),
            pltpu.VMEM((cx + 2, ny, cz), f32),
            pltpu.VMEM((cx + 2, ny + 8, nz), f32),
            pltpu.SemaphoreType.DMA((3, 8)),
            pltpu.SemaphoreType.DMA((3, 8)),
            pltpu.SemaphoreType.DMA((2, 3, n_gy)),
            pltpu.SemaphoreType.DMA((2, 3, n_gy)),
            pltpu.SemaphoreType.DMA((2,)),
            pltpu.SemaphoreType.DMA((2,)),
            pltpu.SemaphoreType.DMA((4,)),
        ],
        compiler_params=pltpu.CompilerParams(
            collective_id=0, has_side_effects=True, vmem_limit_bytes=56328192
        ),
    )(*[
        pltpu.with_memory_space_constraint(a, pltpu.HBM)
        for a in (owners, permeability[None, :], source, region)
    ])


def solution(mesh):
    placed = (P("gx", "gy", None), P("gx", "gy", None), P(), P("gx", None))
    body = functools.partial(on_device, n_gx=mesh.shape["gx"], n_gy=mesh.shape["gy"])
    return jax.shard_map(
        body, mesh=mesh, in_specs=placed, out_specs=P("gx", "gy", None), check_vma=False
    )
```

```python
import functools

import jax
import jax.numpy as jnp
from jax import lax
from jax.experimental import pallas as pl
from jax.experimental.pallas import tpu as pltpu
from jax.sharding import PartitionSpec as P

POST_SWEEPS = 2
COARSE_SWEEPS = 6
RELAX_WEIGHT = 0.6
MASS_TERM = 0.1

MESH = pl.DeviceIdType.MESH
WIDE = 3
HALF = 4
REGION, SOURCE, ITERATE = 0, 1, 2
WIDTHS = (3, 2, 2)
STEPS = ((-1, -1), (1, -1), (-1, 1), (1, 1), (0, -1), (0, 1), (-1, 0), (1, 0))


def kernel(
    n_gx, n_gy,
    owners_in, table_in, source_ref, region_ref, out_ref,
    owners_ref, table_ref, labels, store, group, holders, squeezed, whole_corr, spread, wide,
    send_sem, recv_sem, in_sem,
):
    nx, ny, nz = out_ref.shape
    cx, cy, cz = nx // 2, ny // 2, nz // 2
    first, last = WIDE, WIDE + nx
    gx, gy = lax.axis_index("gx"), lax.axis_index("gy")
    planes = nx + 2 * WIDE
    source, iterate, cond, weight, diag2 = (
        store.at[pl.ds(k * planes, planes)] for k in range(5)
    )
    fields = (labels, source, iterate)
    all_y = n_gy * cy

    def exists(dx, dy):
        x, y = gx + dx, gy + dy
        return (x >= 0) & (x < n_gx) & (y >= 0) & (y < n_gy)

    near_slabs = [
        (dx, off) for dx in (-1, 1, 0) for off in reversed(range(n_gy)) if (dx, off) != (0, 0)
    ]

    barrier = pltpu.get_barrier_semaphore()
    count = jnp.int32(0)
    for dx, off in near_slabs:
        near = exists(dx, 0)

        @pl.when(near)
        def _():
            pl.semaphore_signal(
                barrier, inc=1, device_id=(gx + dx, lax.rem(gy + off, n_gy)), device_id_type=MESH
            )

        count = count + near.astype(jnp.int32)

    load_source = pltpu.make_async_copy(
        source_ref, source.at[pl.ds(first, nx), pl.ds(0, ny)], in_sem.at[0]
    )
    load_region = pltpu.make_async_copy(
        region_ref, labels.at[pl.ds(first, nx), pl.ds(0, ny)], in_sem.at[1]
    )
    load_table = pltpu.make_async_copy(table_in, table_ref, in_sem.at[2])
    load_owners = pltpu.make_async_copy(owners_in, owners_ref, in_sem.at[3])
    load_region.start()
    load_table.start()
    load_source.start()
    load_owners.start()

    def landing(kind, dx, dy):
        w = WIDTHS[kind]
        start, size = {0: (first, nx), -1: (last, w), 1: (first - w, w)}[dx]
        row, high = {0: (0, ny), -1: (ny, HALF), 1: (ny + HALF, HALF)}[dy]
        return fields[kind].at[pl.ds(start, size), pl.ds(row, high)]

    def remote(kind, which):
        dx, dy = STEPS[which]
        w = WIDTHS[kind]
        base = first if kind == ITERATE else 0
        start, size = {0: (0, nx), -1: (0, w), 1: (nx - w, w)}[dx]
        row, high = {0: (0, ny), -1: (0, HALF), 1: (ny - HALF, HALF)}[dy]
        origin = (region_ref, source_ref, iterate)[kind]
        return pltpu.make_async_remote_copy(
            src_ref=origin.at[pl.ds(base + start, size), pl.ds(row, high)],
            dst_ref=landing(kind, dx, dy),
            send_sem=send_sem.at[abs(dx)],
            recv_sem=recv_sem.at[2 * kind + abs(dx)],
            device_id=(gx + dx, gy + dy),
            device_id_type=MESH,
        )

    def send(kind):
        for which, (dx, dy) in enumerate(STEPS):
            @pl.when(exists(dx, dy))
            def _():
                remote(kind, which).start()

    def by_neighbours(act):
        for a in (1, 2):
            for b in (1, 2) if n_gy > 2 else (1,):
                xs = exists(-1, 0).astype(jnp.int32) + exists(1, 0).astype(jnp.int32)
                ys = exists(0, -1).astype(jnp.int32) + exists(0, 1).astype(jnp.int32)

                @pl.when((xs == a) & (ys == b))
                def _():
                    act(a, b)

    def wait(ref, sem):
        pltpu.make_async_copy(ref, ref, sem).wait()

    def of_rows(n):
        high = next(r for r in (40, 32, 24, 16, 8, HALF) if n % r == 0 and r <= store.shape[1])
        return store.at[pl.ds(0, n // high), pl.ds(0, high)]

    def receive(kind, inner):
        def act(a, b):
            n = nx * b * HALF if inner else a * WIDTHS[kind] * (ny + b * HALF)
            wait(of_rows(n), recv_sem.at[2 * kind + 1 - inner])

        by_neighbours(act)

    def finish(a, b):
        wait(of_rows(3 * nx * b * HALF), send_sem.at[0])
        wait(of_rows(sum(WIDTHS) * a * (ny + b * HALF)), send_sem.at[1])
        wait(group.at[:, :, pl.ds(0, (a * n_gy + n_gy - 1) * cy)], send_sem.at[2])
        wait(holders.at[pl.ds(0, a)], send_sem.at[3])

    def gather(kind, dx, off):
        at = pl.ds(pl.multiple_of(all_y + gy * cy, 8), cy)
        to = pl.ds(pl.multiple_of((1 - dx) * all_y + gy * cy, 8), cy)
        return pltpu.make_async_remote_copy(
            src_ref=group.at[kind, :, at],
            dst_ref=group.at[kind, :, to],
            send_sem=send_sem.at[2],
            recv_sem=recv_sem.at[6 + kind],
            device_id=(gx + dx, lax.rem(gy + off, n_gy)),
            device_id_type=MESH,
        )

    def tell(dx):
        return pltpu.make_async_remote_copy(
            src_ref=holders.at[1],
            dst_ref=holders.at[1 - dx],
            send_sem=send_sem.at[3],
            recv_sem=recv_sem.at[8],
            device_id=(gx + dx, gy),
            device_id_type=MESH,
        )

    def gather_start(kind):
        for dx, off in near_slabs:
            @pl.when(exists(dx, 0))
            def _():
                gather(kind, dx, off).start()

    def gather_wait(kind):
        by_neighbours(lambda a, b: wait(
            group.at[kind, :, pl.ds(0, (a * n_gy + n_gy - 1) * cy)], recv_sem.at[6 + kind]
        ))

    for dx, dy in STEPS:
        @pl.when(jnp.logical_not(exists(-dx, -dy)))
        def _():
            ref = landing(REGION, dx, dy)
            ref[...] = jnp.full(ref.shape, table_ref.shape[1], jnp.int32)
            for kind in (SOURCE, ITERATE):
                ref = landing(kind, dx, dy)
                ref[...] = jnp.zeros(ref.shape, jnp.float32)
    for dx in (-1, 1):
        @pl.when(jnp.logical_not(exists(-dx, 0)))
        def _():
            for kind in range(2):
                ref = group.at[kind, :, pl.ds((1 - dx) * all_y, all_y)]
                ref[...] = jnp.zeros(ref.shape, jnp.float32)
            ref = holders.at[1 - dx]
            ref[...] = jnp.zeros(ref.shape, jnp.float32)

    with jax.named_scope("wait_neighbours"):
        pl.semaphore_wait(barrier, count)
    send(REGION)
    send(SOURCE)

    load_owners.wait()
    eight = lax.broadcasted_iota(jnp.int32, (8, cz), 0)
    held = jnp.zeros((8, cz), jnp.float32)
    for c in range(n_gy):
        held = jnp.where(eight == c, owners_ref[0, c].astype(jnp.float32), held)
    holders[1] = held
    for dx in (-1, 1):
        @pl.when(exists(dx, 0))
        def _():
            tell(dx).start()

    load_table.wait()
    with jax.named_scope("wait_own_region"):
        load_region.wait()
    regions = table_ref.shape[1]
    pair = jnp.concatenate([table_ref[...], jnp.zeros((1, 128 - regions), jnp.float32)], axis=1)
    table = jnp.broadcast_to(pair, (8, 128))

    def look_up(planes, tiles):
        for i in planes:
            for r in tiles:
                for c in range(0, nz, 128):
                    spot = labels[i, pl.ds(r, 8), pl.ds(c, 128)]
                    cond[i, pl.ds(r, 8), pl.ds(c, 128)] = jnp.take_along_axis(table, spot, axis=1)

    look_up(range(first, last), range(0, ny, 8))

    lane = lax.broadcasted_iota(jnp.int32, (1, nz), 1)
    z_low = jnp.where(lane == 0, 0.0, 0.5)
    z_high = jnp.where(lane == nz - 1, 0.0, 0.5)
    rows = ny + 8

    def blend(a, b, c, keep=rows):
        u = b + 0.5 * (a + c)
        u = u + 0.5 * (pltpu.roll(u, 1, 0) + pltpu.roll(u, rows - 1, 0))
        u = u[:keep]
        return u + z_low * pltpu.roll(u, 1, 1) + z_high * pltpu.roll(u, nz - 1, 1)

    lane128 = lax.broadcasted_iota(jnp.int32, (8, 128), 1)
    even = lax.rem(2 * lane128, jnp.int32(128))
    half_of = lane128 // 2

    def coarsen(pairs, kind):
        for i, pair_sum in enumerate(pairs):
            total = pair_sum + pltpu.roll(pair_sum, nz - 1, 1)
            for r in range(0, ny, 8):
                low = jnp.take_along_axis(total[r:r + 8, :128], even, axis=1)
                high = jnp.take_along_axis(total[r:r + 8, 128:], even, axis=1)
                squeezed[i, pl.ds(r, 8), :] = jnp.where(lane128 < 64, low, high)
            block = squeezed[i, pl.ds(0, cy, stride=2), :] + squeezed[i, pl.ds(1, cy, stride=2), :]
            group[kind, i, pl.ds(pl.multiple_of(all_y + gy * cy, 8), cy), :] = 0.125 * block

    coarsen(
        [cond[first + 2 * i, pl.ds(0, ny), :] + cond[first + 2 * i + 1, pl.ds(0, ny), :]
         for i in range(cx)],
        0,
    )

    row = lax.broadcasted_iota(jnp.int32, (rows, 1), 0)
    y = gy * ny + jnp.where(row < ny + HALF, row, row - rows)
    in_y = jnp.where((y >= 0) & (y < n_gy * ny), RELAX_WEIGHT, 0.0)

    def weigh(planes):
        for i in planes:
            mine = cond[i]
            mixed = blend(cond[i - 1], mine, cond[i + 1])
            x = gx * nx + (i - first)
            in_x = jnp.where((x >= 0) & (x < n_gx * nx), 1.0, 0.0)
            weight[i] = (in_y * in_x) / (MASS_TERM + 6.0 * mine + mixed)
            diag2[i] = MASS_TERM + 8.0 * mine + mixed

    with jax.named_scope("wait_region_rows"):
        receive(REGION, True)
    look_up(range(first, last), (ny,))
    weigh(range(first + 1, last - 1))
    with jax.named_scope("wait_region_planes"):
        receive(REGION, False)
    edges = [*range(first - WIDE, first), *range(last, last + WIDE)]
    look_up(edges, range(0, rows, 8))
    weigh([first - 2, first - 1, first, last - 1, last, last + 1])
    with jax.named_scope("start_coarse_cond"):
        gather_start(0)
    def defect(i, values, flux, keep=rows):
        at = pl.ds(0, keep)
        lhs = cond[i, at] * blend(values[i - 1], values[i], values[i + 1], keep)
        rhs = blend(flux[i - 1], flux[i], flux[i + 1], keep)
        return source[i, at] - diag2[i, at] * values[i][:keep] + lhs + rhs

    values, flux, smooth = {}, {}, {}

    def first_sweep(at):
        for i in at:
            values[i] = weight[i] * source[i]
            flux[i] = cond[i] * values[i]

    def second_sweep(at):
        for i in at:
            smooth[i] = values[i] + weight[i] * defect(i, values, flux)

    load_source.wait()
    with jax.named_scope("wait_source_rows"):
        receive(SOURCE, True)
    first_sweep(range(first, last))
    second_sweep(range(first + 1, last - 1))
    with jax.named_scope("wait_source_planes"):
        receive(SOURCE, False)
    first_sweep((first - 2, first - 1, last, last + 1))
    second_sweep((first - 1, first, last - 1, last))
    flux = {i: cond[i] * smooth[i] for i in smooth}
    pairs = []
    for i in range(cx):
        j = first + 2 * i
        pairs.append(defect(j, smooth, flux, ny) + defect(j + 1, smooth, flux, ny))
    coarsen(pairs, 1)
    with jax.named_scope("start_coarse_res"):
        gather_start(1)
    for i in range(first, last):
        iterate[i, pl.ds(0, ny), :] = smooth[i][:ny]
    send(ITERATE)

    crow = lax.broadcasted_iota(jnp.int32, (all_y, cz), 0)
    clane = lax.broadcasted_iota(jnp.int32, (1, cz), 1)
    cz_low = jnp.where(clane == 0, 0.0, 0.5)
    cz_high = jnp.where(clane == cz - 1, 0.0, 0.5)

    def coarse_blend(planes, y_low, y_high):
        mixed = []
        for i, u in enumerate(planes):
            near = [planes[j] for j in (i - 1, i + 1) if 0 <= j < cx]
            u = u + 0.5 * functools.reduce(jnp.add, near) if near else u
            u = u + y_low * pltpu.roll(u, 1, 0) + y_high * pltpu.roll(u, all_y - 1, 0)
            mixed.append(u + cz_low * pltpu.roll(u, 1, 1) + cz_high * pltpu.roll(u, cz - 1, 1))
        return mixed

    def total(planes, c):
        whole = functools.reduce(jnp.add, [v[c * cy:(c + 1) * cy] for v in planes])
        return jnp.sum(whole, keepdims=True)

    with jax.named_scope("wait_holders"):
        by_neighbours(lambda a, b: wait(holders.at[pl.ds(0, a)], recv_sem.at[8]))
    with jax.named_scope("wait_coarse_cond"):
        gather_wait(0)
    slabs = []
    for g in range(3):
        held = [holders[g, pl.ds(c, 1), :] for c in range(n_gy)]
        same = lambda a, b: jnp.where(held[a] == held[b], 1.0, 0.0)
        y_low = jnp.where(crow == 0, 0.0, 0.5)
        y_high = jnp.where(crow == all_y - 1, 0.0, 0.5)
        for c in range(1, n_gy):
            tied = 0.5 * same(c - 1, c)
            y_low = jnp.where(crow == c * cy, tied, y_low)
            y_high = jnp.where(crow == c * cy - 1, tied, y_high)
        k = [group[0, i, pl.ds(g * all_y, all_y), :] for i in range(cx)]
        mixed = coarse_blend(k, y_low, y_high)
        diag = [MASS_TERM + 1.5 * a + 0.25 * b for a, b in zip(k, mixed)]
        step = [RELAX_WEIGHT / d for d in diag]
        ones = coarse_blend([jnp.ones((all_y, cz), jnp.float32)] * cx, y_low, y_high)
        slabs.append(dict(
            y_low=y_low, y_high=y_high, k=k, step=step,
            keep=[1.0 - s * (d + 0.5 * a) for s, d, a in zip(step, diag, k)],
            mine=[0.25 * s * a for s, a in zip(step, k)],
            theirs=[0.25 * s for s in step],
            drain=[MASS_TERM + 0.25 * a * (8.0 - b) for a, b in zip(k, ones)],
            same=[[same(a, b)[:, :1] for b in range(n_gy)] for a in range(n_gy)],
            diag_sum=[total(diag, c) for c in range(n_gy)],
        ))

    with jax.named_scope("wait_coarse_res"):
        gather_wait(1)
    e = []
    for g, s in enumerate(slabs):
        s["res"] = [group[1, i, pl.ds(g * all_y, all_y), :] for i in range(cx)]
        s["start"] = [a * b for a, b in zip(s["step"], s["res"])]
        e.append(s["start"])
    for _ in range(COARSE_SWEEPS - 1):
        for g, s in enumerate(slabs):
            straight = coarse_blend(e[g], s["y_low"], s["y_high"])
            carried = coarse_blend([a * v for a, v in zip(s["k"], e[g])], s["y_low"], s["y_high"])
            e[g] = [
                s["start"][i] + s["keep"][i] * e[g][i]
                + (s["mine"][i] * straight[i] + s["theirs"][i] * carried[i])
                for i in range(cx)
            ]
    keep_planes = ((0, cx - 1), *[(1, i) for i in range(cx)], (2, 0))
    ratios = []
    for g, s in enumerate(slabs):
        left = [r - d * v for r, d, v in zip(s["res"], s["drain"], e[g])]
        left = [total(left, c) for c in range(n_gy)]
        shares = []
        for c in range(n_gy):
            num = functools.reduce(jnp.add, [s["same"][c][b] * left[b] for b in range(n_gy)])
            den = functools.reduce(jnp.add, [s["same"][c][b] * s["diag_sum"][b] for b in range(n_gy)])
            shares.append(num / jnp.maximum(den, 1.0))
        ratios.append(shares)
    for slot, (g, i) in enumerate(keep_planes):
        whole_corr[slot, pl.ds(0, 8), :] = jnp.zeros((8, cz), jnp.float32)
        whole_corr[slot, pl.ds(8 + all_y, 8), :] = jnp.zeros((8, cz), jnp.float32)
        for c in range(n_gy):
            whole_corr[slot, pl.ds(8 + c * cy, cy), :] = e[g][i][c * cy:(c + 1) * cy] + ratios[g][c]

    sub = lax.broadcasted_iota(jnp.int32, (8, cz), 0)
    for i in range(cx + 2):
        mine = whole_corr[i, pl.ds(pl.multiple_of(8 + gy * cy, 8), cy), :]
        below = whole_corr[i, pl.ds(pl.multiple_of(gy * cy, 8), 8), :]
        above = whole_corr[i, pl.ds(pl.multiple_of(8 + gy * cy + cy, 8), 8), :]
        spread[i, pl.ds(0, cy, stride=2), :] = mine
        spread[i, pl.ds(1, cy, stride=2), :] = mine
        for r in range(0, rows, 8):
            if r < ny:
                tile = spread[i, pl.ds(r, 8), :]
            else:
                tile = jnp.where(
                    sub < HALF,
                    jnp.broadcast_to(above[:1], (8, cz)),
                    jnp.broadcast_to(below[7:], (8, cz)),
                )
            for part in range(2):
                wide[i, pl.ds(r, 8), pl.ds(128 * part, 128)] = jnp.take_along_axis(
                    tile, half_of + 64 * part, axis=1
                )
    with jax.named_scope("wait_iterate_rows"):
        receive(ITERATE, True)
    with jax.named_scope("wait_iterate_planes"):
        receive(ITERATE, False)
    values = {
        i: iterate[i] + wide[(i - first + 2) // 2] for i in range(first - 2, last + 2)
    }
    for sweep in range(POST_SWEEPS):
        reach = POST_SWEEPS - 1 - sweep
        keep = rows if reach else ny
        flux = {i: cond[i] * values[i] for i in values}
        values = {
            i: values[i][:keep] + weight[i, pl.ds(0, keep)] * defect(i, values, flux, keep)
            for i in range(first - reach, last + reach)
        }
    for i in range(nx):
        out_ref[i] = values[first + i][:ny]

    with jax.named_scope("wait_sends"):
        by_neighbours(finish)


def on_device(source, region, permeability, owners, *, n_gx, n_gy):
    nx, ny, nz = source.shape
    planes = nx + 2 * WIDE
    cx, all_y, cz = nx // 2, n_gy * ny // 2, nz // 2
    f32 = jnp.float32
    return pl.pallas_call(
        functools.partial(kernel, n_gx, n_gy),
        out_shape=jax.ShapeDtypeStruct(source.shape, f32),
        in_specs=[pl.BlockSpec(memory_space=pltpu.HBM)] * 4,
        out_specs=pl.BlockSpec(memory_space=pltpu.VMEM),
        scratch_shapes=[
            pltpu.SMEM((1, n_gy), jnp.int32),
            pltpu.VMEM((1, permeability.shape[0]), f32),
            pltpu.VMEM((planes, ny + 8, nz), jnp.int32),
            pltpu.VMEM((7 * planes, ny + 8, nz), f32),
            pltpu.VMEM((2, cx, 3 * all_y, cz), f32),
            pltpu.VMEM((3, 8, cz), f32),
            pltpu.VMEM((cx, ny, cz), f32),
            pltpu.VMEM((cx + 2, all_y + 16, cz), f32),
            pltpu.VMEM((cx + 2, ny, cz), f32),
            pltpu.VMEM((cx + 2, ny + 8, nz), f32),
            pltpu.SemaphoreType.DMA((4,)),
            pltpu.SemaphoreType.DMA((9,)),
            pltpu.SemaphoreType.DMA((4,)),
        ],
        compiler_params=pltpu.CompilerParams(
            collective_id=0, has_side_effects=True, vmem_limit_bytes=56328192
        ),
    )(*[
        pltpu.with_memory_space_constraint(a, pltpu.HBM)
        for a in (owners, permeability[None, :], source, region)
    ])


def solution(mesh):
    placed = (P("gx", "gy", None), P("gx", "gy", None), P(), P("gx", None))
    body = functools.partial(on_device, n_gx=mesh.shape["gx"], n_gy=mesh.shape["gy"])
    return jax.shard_map(
        body, mesh=mesh, in_specs=placed, out_specs=P("gx", "gy", None), check_vma=False
    )
```

```python
import functools

import jax
import jax.numpy as jnp
from jax import lax
from jax.experimental import pallas as pl
from jax.experimental.pallas import tpu as pltpu
from jax.sharding import PartitionSpec as P

POST_SWEEPS = 2
COARSE_SWEEPS = 6
RELAX_WEIGHT = 0.6
MASS_TERM = 0.1

MESH = pl.DeviceIdType.MESH
WIDE = 3
HALF = 4
REGION, SOURCE, ITERATE = 0, 1, 2
EDGE = 2
BESIDE = (2, 1, 2)
CORNER = ((3, HALF), (2, EDGE), (2, HALF))
STRIP = (3, 2)
STEPS = ((-1, -1), (1, -1), (-1, 1), (1, 1), (0, -1), (0, 1), (-1, 0), (1, 0))


def kernel(
    n_gx, n_gy,
    owners_in, table_in, source_ref, region_ref, out_ref,
    owners_ref, table_ref, labels, store, shipped, group, holders, squeezed, whole_corr, spread, wide,
    send_sem, recv_sem, in_sem,
):
    nx, ny, nz = out_ref.shape
    cx, cy, cz = nx // 2, ny // 2, nz // 2
    first, last = WIDE, WIDE + nx
    gx, gy = lax.axis_index("gx"), lax.axis_index("gy")
    planes = nx + 2 * WIDE
    source, iterate, cond, weight, diag2 = (
        store.at[pl.ds(k * planes, planes)] for k in range(5)
    )
    fields = (labels, source, iterate)
    all_y = n_gy * cy

    def exists(dx, dy):
        x, y = gx + dx, gy + dy
        return (x >= 0) & (x < n_gx) & (y >= 0) & (y < n_gy)

    near_slabs = [
        (dx, off) for dx in (-1, 1, 0) for off in reversed(range(n_gy)) if (dx, off) != (0, 0)
    ]

    nowhere = table_ref.shape[1]
    for i in range(planes):
        if i in (0, planes - 1):
            labels[i] = jnp.full((ny + 8, nz), nowhere, jnp.int32)
        else:
            labels[i, pl.ds(ny, 8), :] = jnp.full((8, nz), nowhere, jnp.int32)

    barrier = pltpu.get_barrier_semaphore()
    count = jnp.int32(0)
    for dx, off in near_slabs:
        near = exists(dx, 0)

        @pl.when(near)
        def _():
            pl.semaphore_signal(
                barrier, inc=1, device_id=(gx + dx, lax.rem(gy + off, n_gy)), device_id_type=MESH
            )

        count = count + near.astype(jnp.int32)

    load_source = pltpu.make_async_copy(
        source_ref, source.at[pl.ds(first, nx), pl.ds(0, ny)], in_sem.at[0]
    )
    load_region = pltpu.make_async_copy(
        region_ref, labels.at[pl.ds(first, nx), pl.ds(0, ny)], in_sem.at[1]
    )
    load_table = pltpu.make_async_copy(table_in, table_ref, in_sem.at[2])
    load_owners = pltpu.make_async_copy(owners_in, owners_ref, in_sem.at[3])
    load_region.start()
    load_table.start()
    load_source.start()
    load_owners.start()

    def box(kind, dx, dy):
        if dx == 0:
            w, high = nx, HALF
        elif dy == 0:
            w, high = BESIDE[kind], ny
        else:
            w, high = CORNER[kind]
        plane = nx - w if dx > 0 else 0
        land = {0: first, -1: last, 1: first - w}[dx]
        row = ny - high if dy > 0 else 0
        to = {0: 0, -1: ny, 1: ny + 8 - high}[dy]
        return (plane, w, row, high), (land, w, to, high)

    def move(kind, dx, dy, here, there):
        plane, w, row, high = here
        base = first if kind == ITERATE else 0
        origin = (region_ref, source_ref, iterate)[kind]
        land, _, to, _ = there
        return pltpu.make_async_remote_copy(
            src_ref=origin.at[pl.ds(base + plane, w), pl.ds(row, high)],
            dst_ref=fields[kind].at[pl.ds(land, w), pl.ds(to, high)],
            send_sem=send_sem.at[abs(dx)],
            recv_sem=recv_sem.at[2 * kind + abs(dx)],
            device_id=(gx + dx, gy + dy),
            device_id_type=MESH,
        )

    def strips(kind, dx):
        far = STRIP[kind]
        plane, land = (nx - far, first - far) if dx > 0 else (far - 1, last + far - 1)
        for row in (0, ny - EDGE):
            yield move(kind, dx, 0, (plane, 1, row, EDGE), (land, 1, row, EDGE))

    def ship(dx):
        side = (1 - dx) // 2
        return pltpu.make_async_remote_copy(
            src_ref=shipped.at[2 + side],
            dst_ref=shipped.at[side],
            send_sem=send_sem.at[1],
            recv_sem=recv_sem.at[2 * SOURCE + 1],
            device_id=(gx + dx, gy),
            device_id_type=MESH,
        )

    def send(kind):
        for dx, dy in STEPS:
            @pl.when(exists(dx, dy))
            def _():
                move(kind, dx, dy, *box(kind, dx, dy)).start()
                if dy == 0 and kind != ITERATE:
                    for strip in strips(kind, dx):
                        strip.start()

    def by_neighbours(act):
        for a in (1, 2):
            for b in (1, 2) if n_gy > 2 else (1,):
                xs = exists(-1, 0).astype(jnp.int32) + exists(1, 0).astype(jnp.int32)
                ys = exists(0, -1).astype(jnp.int32) + exists(0, 1).astype(jnp.int32)

                @pl.when((xs == a) & (ys == b))
                def _():
                    act(a, b)

    def wait(ref, sem):
        pltpu.make_async_copy(ref, ref, sem).wait()

    def of_rows(n):
        high = next(r for r in (40, 32, 24, 16, 8, HALF) if n % r == 0 and r <= store.shape[1])
        return store.at[pl.ds(0, n // high), pl.ds(0, high)]

    def beside(kind, b):
        n = BESIDE[kind] * ny + b * CORNER[kind][0] * CORNER[kind][1]
        return n + {REGION: 2 * EDGE, SOURCE: 2 * EDGE + ny, ITERATE: 0}[kind]

    def receive(kind, inner):
        def act(a, b):
            n = nx * b * HALF if inner else a * beside(kind, b)
            wait(of_rows(n), recv_sem.at[2 * kind + 1 - inner])

        by_neighbours(act)

    def finish(a, b):
        wait(of_rows(3 * nx * b * HALF), send_sem.at[0])
        wait(of_rows(a * sum(beside(kind, b) for kind in range(3))), send_sem.at[1])
        wait(group.at[:, :, pl.ds(0, (a * n_gy + n_gy - 1) * cy)], send_sem.at[2])
        wait(holders.at[pl.ds(0, a)], send_sem.at[3])

    def gather(kind, dx, off):
        at = pl.ds(pl.multiple_of(all_y + gy * cy, 8), cy)
        to = pl.ds(pl.multiple_of((1 - dx) * all_y + gy * cy, 8), cy)
        return pltpu.make_async_remote_copy(
            src_ref=group.at[kind, :, at],
            dst_ref=group.at[kind, :, to],
            send_sem=send_sem.at[2],
            recv_sem=recv_sem.at[6 + kind],
            device_id=(gx + dx, lax.rem(gy + off, n_gy)),
            device_id_type=MESH,
        )

    def tell(dx):
        return pltpu.make_async_remote_copy(
            src_ref=holders.at[1],
            dst_ref=holders.at[1 - dx],
            send_sem=send_sem.at[3],
            recv_sem=recv_sem.at[8],
            device_id=(gx + dx, gy),
            device_id_type=MESH,
        )

    def gather_start(kind):
        for dx, off in near_slabs:
            @pl.when(exists(dx, 0))
            def _():
                gather(kind, dx, off).start()

    def gather_wait(kind):
        by_neighbours(lambda a, b: wait(
            group.at[kind, :, pl.ds(0, (a * n_gy + n_gy - 1) * cy)], recv_sem.at[6 + kind]
        ))

    for dy in (-1, 1):
        @pl.when(jnp.logical_not(exists(0, -dy)))
        def _():
            at = pl.ds(ny if dy < 0 else ny + HALF, HALF)
            for ref in (source, iterate):
                ref[:, at, :] = jnp.zeros((planes, HALF, nz), jnp.float32)
    for dx in (-1, 1):
        @pl.when(jnp.logical_not(exists(-dx, 0)))
        def _():
            at = pl.ds(last if dx < 0 else 0, WIDE)
            labels[at] = jnp.full((WIDE, ny + 8, nz), nowhere, jnp.int32)
            for ref in (source, iterate):
                ref[at] = jnp.zeros((WIDE, ny + 8, nz), jnp.float32)
            shipped[(1 - dx) // 2] = jnp.zeros((ny, nz), jnp.float32)
            for kind in range(2):
                ref = group.at[kind, :, pl.ds((1 - dx) * all_y, all_y)]
                ref[...] = jnp.zeros(ref.shape, jnp.float32)
            ref = holders.at[1 - dx]
            ref[...] = jnp.zeros(ref.shape, jnp.float32)

    with jax.named_scope("wait_neighbours"):
        pl.semaphore_wait(barrier, count)
    send(REGION)
    send(SOURCE)

    load_owners.wait()
    eight = lax.broadcasted_iota(jnp.int32, (8, cz), 0)
    held = jnp.zeros((8, cz), jnp.float32)
    for c in range(n_gy):
        held = jnp.where(eight == c, owners_ref[0, c].astype(jnp.float32), held)
    holders[1] = held
    for dx in (-1, 1):
        @pl.when(exists(dx, 0))
        def _():
            tell(dx).start()

    load_table.wait()
    with jax.named_scope("wait_own_region"):
        load_region.wait()
    regions = table_ref.shape[1]
    pair = jnp.concatenate([table_ref[...], jnp.zeros((1, 128 - regions), jnp.float32)], axis=1)
    table = jnp.broadcast_to(pair, (8, 128))

    def look_up(planes, tiles):
        for i in planes:
            for r in tiles:
                for c in range(0, nz, 128):
                    spot = labels[i, pl.ds(r, 8), pl.ds(c, 128)]
                    cond[i, pl.ds(r, 8), pl.ds(c, 128)] = jnp.take_along_axis(table, spot, axis=1)

    look_up(range(first, last), range(0, ny, 8))

    lane = lax.broadcasted_iota(jnp.int32, (1, nz), 1)
    z_low = jnp.where(lane == 0, 0.0, 0.5)
    z_high = jnp.where(lane == nz - 1, 0.0, 0.5)
    rows = ny + 8

    def blend(a, b, c, keep=rows):
        u = b + 0.5 * (a + c)
        u = u + 0.5 * (pltpu.roll(u, 1, 0) + pltpu.roll(u, rows - 1, 0))
        u = u[:keep]
        return u + z_low * pltpu.roll(u, 1, 1) + z_high * pltpu.roll(u, nz - 1, 1)

    lane128 = lax.broadcasted_iota(jnp.int32, (8, 128), 1)
    even = lax.rem(2 * lane128, jnp.int32(128))
    half_of = lane128 // 2

    def coarsen(pairs, kind):
        for i, pair_sum in enumerate(pairs):
            total = pair_sum + pltpu.roll(pair_sum, nz - 1, 1)
            for r in range(0, ny, 8):
                low = jnp.take_along_axis(total[r:r + 8, :128], even, axis=1)
                high = jnp.take_along_axis(total[r:r + 8, 128:], even, axis=1)
                squeezed[i, pl.ds(r, 8), :] = jnp.where(lane128 < 64, low, high)
            block = squeezed[i, pl.ds(0, cy, stride=2), :] + squeezed[i, pl.ds(1, cy, stride=2), :]
            group[kind, i, pl.ds(pl.multiple_of(all_y + gy * cy, 8), cy), :] = 0.125 * block

    load_source.wait()
    for dx, i in ((1, last - EDGE), (-1, first + EDGE - 1)):
        mine = cond[i, pl.ds(0, ny), :]
        mixed = blend(cond[i - 1], cond[i], cond[i + 1], ny)
        shipped[2 + (1 - dx) // 2] = (
            RELAX_WEIGHT * source[i, pl.ds(0, ny), :] / (MASS_TERM + 6.0 * mine + mixed)
        )

        @pl.when(exists(dx, 0))
        def _():
            ship(dx).start()

    coarsen(
        [cond[first + 2 * i, pl.ds(0, ny), :] + cond[first + 2 * i + 1, pl.ds(0, ny), :]
         for i in range(cx)],
        0,
    )

    row = lax.broadcasted_iota(jnp.int32, (rows, 1), 0)
    y = gy * ny + jnp.where(row < ny + HALF, row, row - rows)
    in_y = jnp.where((y >= 0) & (y < n_gy * ny), RELAX_WEIGHT, 0.0)

    def weigh(at):
        for i in at:
            mine = cond[i]
            mixed = blend(cond[i - 1], mine, cond[i + 1])
            x = gx * nx + (i - first)
            in_x = jnp.where((x >= 0) & (x < n_gx * nx), 1.0, 0.0)
            weight[i] = (in_y * in_x) / (MASS_TERM + 6.0 * mine + mixed)
            diag2[i] = MASS_TERM + 8.0 * mine + mixed

    with jax.named_scope("wait_region_rows"):
        receive(REGION, True)
    look_up(range(first, last), (ny,))
    weigh(range(first + 1, last - 1))
    with jax.named_scope("wait_region_planes"):
        receive(REGION, False)
    edges = [*range(first - WIDE, first), *range(last, last + WIDE)]
    look_up(edges, range(0, rows, 8))
    weigh([first - 2, first - 1, first, last - 1, last, last + 1])
    with jax.named_scope("start_coarse_cond"):
        gather_start(0)
    def defect(i, values, flux, keep=rows):
        at = pl.ds(0, keep)
        lhs = cond[i, at] * blend(values[i - 1], values[i], values[i + 1], keep)
        rhs = blend(flux[i - 1], flux[i], flux[i + 1], keep)
        return source[i, at] - diag2[i, at] * values[i][:keep] + lhs + rhs

    values, flux, smooth = {}, {}, {}

    def first_sweep(at):
        for i in at:
            values[i] = weight[i] * source[i]
            if i in (first - EDGE, last + EDGE - 1):
                side = int(i > first)
                far = jnp.concatenate([shipped[side], jnp.zeros((8, nz), jnp.float32)])
                values[i] = jnp.where((row > 0) & (row < ny - 1), far, values[i])
            flux[i] = cond[i] * values[i]

    def second_sweep(at):
        for i in at:
            smooth[i] = values[i] + weight[i] * defect(i, values, flux)

    with jax.named_scope("wait_source_rows"):
        receive(SOURCE, True)
    first_sweep(range(first, last))
    second_sweep(range(first + 1, last - 1))
    with jax.named_scope("wait_source_planes"):
        receive(SOURCE, False)
    first_sweep((first - 2, first - 1, last, last + 1))
    second_sweep((first - 1, first, last - 1, last))
    flux = {i: cond[i] * smooth[i] for i in smooth}
    pairs = []
    for i in range(cx):
        j = first + 2 * i
        pairs.append(defect(j, smooth, flux, ny) + defect(j + 1, smooth, flux, ny))
    coarsen(pairs, 1)
    with jax.named_scope("start_coarse_res"):
        gather_start(1)
    for i in range(first, last):
        iterate[i, pl.ds(0, ny), :] = smooth[i][:ny]
    send(ITERATE)

    crow = lax.broadcasted_iota(jnp.int32, (all_y, cz), 0)
    clane = lax.broadcasted_iota(jnp.int32, (1, cz), 1)
    cz_low = jnp.where(clane == 0, 0.0, 0.5)
    cz_high = jnp.where(clane == cz - 1, 0.0, 0.5)

    def coarse_blend(planes, y_low, y_high):
        mixed = []
        for i, u in enumerate(planes):
            near = [planes[j] for j in (i - 1, i + 1) if 0 <= j < cx]
            u = u + 0.5 * functools.reduce(jnp.add, near) if near else u
            u = u + y_low * pltpu.roll(u, 1, 0) + y_high * pltpu.roll(u, all_y - 1, 0)
            mixed.append(u + cz_low * pltpu.roll(u, 1, 1) + cz_high * pltpu.roll(u, cz - 1, 1))
        return mixed

    def total(planes, c):
        whole = functools.reduce(jnp.add, [v[c * cy:(c + 1) * cy] for v in planes])
        return jnp.sum(whole, keepdims=True)

    with jax.named_scope("wait_holders"):
        by_neighbours(lambda a, b: wait(holders.at[pl.ds(0, a)], recv_sem.at[8]))
    with jax.named_scope("wait_coarse_cond"):
        gather_wait(0)
    slabs = []
    for g in range(3):
        held = [holders[g, pl.ds(c, 1), :] for c in range(n_gy)]
        same = lambda a, b: jnp.where(held[a] == held[b], 1.0, 0.0)
        y_low = jnp.where(crow == 0, 0.0, 0.5)
        y_high = jnp.where(crow == all_y - 1, 0.0, 0.5)
        for c in range(1, n_gy):
            tied = 0.5 * same(c - 1, c)
            y_low = jnp.where(crow == c * cy, tied, y_low)
            y_high = jnp.where(crow == c * cy - 1, tied, y_high)
        k = [group[0, i, pl.ds(g * all_y, all_y), :] for i in range(cx)]
        mixed = coarse_blend(k, y_low, y_high)
        diag = [MASS_TERM + 1.5 * a + 0.25 * b for a, b in zip(k, mixed)]
        step = [RELAX_WEIGHT / d for d in diag]
        ones = coarse_blend([jnp.ones((all_y, cz), jnp.float32)] * cx, y_low, y_high)
        slabs.append(dict(
            y_low=y_low, y_high=y_high, k=k, step=step,
            keep=[1.0 - s * (d + 0.5 * a) for s, d, a in zip(step, diag, k)],
            mine=[0.25 * s * a for s, a in zip(step, k)],
            theirs=[0.25 * s for s in step],
            drain=[MASS_TERM + 0.25 * a * (8.0 - b) for a, b in zip(k, ones)],
            same=[[same(a, b)[:, :1] for b in range(n_gy)] for a in range(n_gy)],
            diag_sum=[total(diag, c) for c in range(n_gy)],
        ))

    with jax.named_scope("wait_coarse_res"):
        gather_wait(1)
    e = []
    for g, s in enumerate(slabs):
        s["res"] = [group[1, i, pl.ds(g * all_y, all_y), :] for i in range(cx)]
        s["start"] = [a * b for a, b in zip(s["step"], s["res"])]
        e.append(s["start"])
    for _ in range(COARSE_SWEEPS - 1):
        for g, s in enumerate(slabs):
            straight = coarse_blend(e[g], s["y_low"], s["y_high"])
            carried = coarse_blend([a * v for a, v in zip(s["k"], e[g])], s["y_low"], s["y_high"])
            e[g] = [
                s["start"][i] + s["keep"][i] * e[g][i]
                + (s["mine"][i] * straight[i] + s["theirs"][i] * carried[i])
                for i in range(cx)
            ]
    keep_planes = ((0, cx - 1), *[(1, i) for i in range(cx)], (2, 0))
    ratios = []
    for g, s in enumerate(slabs):
        left = [r - d * v for r, d, v in zip(s["res"], s["drain"], e[g])]
        left = [total(left, c) for c in range(n_gy)]
        shares = []
        for c in range(n_gy):
            num = functools.reduce(jnp.add, [s["same"][c][b] * left[b] for b in range(n_gy)])
            den = functools.reduce(jnp.add, [s["same"][c][b] * s["diag_sum"][b] for b in range(n_gy)])
            shares.append(num / jnp.maximum(den, 1.0))
        ratios.append(shares)
    for slot, (g, i) in enumerate(keep_planes):
        whole_corr[slot, pl.ds(0, 8), :] = jnp.zeros((8, cz), jnp.float32)
        whole_corr[slot, pl.ds(8 + all_y, 8), :] = jnp.zeros((8, cz), jnp.float32)
        for c in range(n_gy):
            whole_corr[slot, pl.ds(8 + c * cy, cy), :] = e[g][i][c * cy:(c + 1) * cy] + ratios[g][c]

    sub = lax.broadcasted_iota(jnp.int32, (8, cz), 0)
    for i in range(cx + 2):
        mine = whole_corr[i, pl.ds(pl.multiple_of(8 + gy * cy, 8), cy), :]
        below = whole_corr[i, pl.ds(pl.multiple_of(gy * cy, 8), 8), :]
        above = whole_corr[i, pl.ds(pl.multiple_of(8 + gy * cy + cy, 8), 8), :]
        spread[i, pl.ds(0, cy, stride=2), :] = mine
        spread[i, pl.ds(1, cy, stride=2), :] = mine
        for r in range(0, rows, 8):
            if r < ny:
                tile = spread[i, pl.ds(r, 8), :]
            else:
                tile = jnp.where(
                    sub < HALF,
                    jnp.broadcast_to(above[:1], (8, cz)),
                    jnp.broadcast_to(below[7:], (8, cz)),
                )
            for part in range(2):
                wide[i, pl.ds(r, 8), pl.ds(128 * part, 128)] = jnp.take_along_axis(
                    tile, half_of + 64 * part, axis=1
                )
    with jax.named_scope("wait_iterate_rows"):
        receive(ITERATE, True)
    with jax.named_scope("wait_iterate_planes"):
        receive(ITERATE, False)
    values = {
        i: iterate[i] + wide[(i - first + 2) // 2] for i in range(first - 2, last + 2)
    }
    for sweep in range(POST_SWEEPS):
        reach = POST_SWEEPS - 1 - sweep
        keep = rows if reach else ny
        flux = {i: cond[i] * values[i] for i in values}
        values = {
            i: values[i][:keep] + weight[i, pl.ds(0, keep)] * defect(i, values, flux, keep)
            for i in range(first - reach, last + reach)
        }
    for i in range(nx):
        out_ref[i] = values[first + i][:ny]

    with jax.named_scope("wait_sends"):
        by_neighbours(finish)


def on_device(source, region, permeability, owners, *, n_gx, n_gy):
    nx, ny, nz = source.shape
    planes = nx + 2 * WIDE
    cx, all_y, cz = nx // 2, n_gy * ny // 2, nz // 2
    f32 = jnp.float32
    return pl.pallas_call(
        functools.partial(kernel, n_gx, n_gy),
        out_shape=jax.ShapeDtypeStruct(source.shape, f32),
        in_specs=[pl.BlockSpec(memory_space=pltpu.HBM)] * 4,
        out_specs=pl.BlockSpec(memory_space=pltpu.VMEM),
        scratch_shapes=[
            pltpu.SMEM((1, n_gy), jnp.int32),
            pltpu.VMEM((1, permeability.shape[0]), f32),
            pltpu.VMEM((planes, ny + 8, nz), jnp.int32),
            pltpu.VMEM((7 * planes, ny + 8, nz), f32),
            pltpu.VMEM((4, ny, nz), f32),
            pltpu.VMEM((2, cx, 3 * all_y, cz), f32),
            pltpu.VMEM((3, 8, cz), f32),
            pltpu.VMEM((cx, ny, cz), f32),
            pltpu.VMEM((cx + 2, all_y + 16, cz), f32),
            pltpu.VMEM((cx + 2, ny, cz), f32),
            pltpu.VMEM((cx + 2, ny + 8, nz), f32),
            pltpu.SemaphoreType.DMA((4,)),
            pltpu.SemaphoreType.DMA((9,)),
            pltpu.SemaphoreType.DMA((4,)),
        ],
        compiler_params=pltpu.CompilerParams(
            collective_id=0, has_side_effects=True, vmem_limit_bytes=56328192
        ),
    )(*[
        pltpu.with_memory_space_constraint(a, pltpu.HBM)
        for a in (owners, permeability[None, :], source, region)
    ])


def solution(mesh):
    placed = (P("gx", "gy", None), P("gx", "gy", None), P(), P("gx", None))
    body = functools.partial(on_device, n_gx=mesh.shape["gx"], n_gy=mesh.shape["gy"])
    return jax.shard_map(
        body, mesh=mesh, in_specs=placed, out_specs=P("gx", "gy", None), check_vma=False
    )
```

```python
import functools

import jax
import jax.numpy as jnp
from jax import lax
from jax.experimental import pallas as pl
from jax.experimental.pallas import tpu as pltpu
from jax.sharding import PartitionSpec as P

POST_SWEEPS = 2
COARSE_SWEEPS = 6
RELAX_WEIGHT = 0.6
MASS_TERM = 0.1

MESH = pl.DeviceIdType.MESH
WIDE = 3
HALF = 4
REGION, SOURCE, ITERATE = 0, 1, 2
EDGE = 2
BESIDE = (2, 1, 2)
CORNER = ((3, HALF), (2, EDGE), (2, HALF))
STRIP = (3, 2)
STEPS = ((-1, -1), (1, -1), (-1, 1), (1, 1), (0, -1), (0, 1), (-1, 0), (1, 0))


def kernel(
    n_gx, n_gy,
    owners_in, table_in, source_ref, region_ref, out_ref,
    owners_ref, table_ref, labels, store, shipped, group, holders, squeezed, whole_corr, spread, wide,
    send_sem, recv_sem, in_sem, ready_sem,
):
    nx, ny, nz = out_ref.shape
    cx, cy, cz = nx // 2, ny // 2, nz // 2
    first, last = WIDE, WIDE + nx
    gx, gy = lax.axis_index("gx"), lax.axis_index("gy")
    planes = nx + 2 * WIDE
    source, iterate, cond, weight, diag2 = (
        store.at[pl.ds(k * planes, planes)] for k in range(5)
    )
    fields = (labels, source, iterate)
    all_y = n_gy * cy

    def exists(dx, dy):
        x, y = gx + dx, gy + dy
        return (x >= 0) & (x < n_gx) & (y >= 0) & (y < n_gy)

    near_slabs = [
        (dx, off) for dx in (-1, 1, 0) for off in reversed(range(n_gy)) if (dx, off) != (0, 0)
    ]

    nowhere = table_ref.shape[1]
    for i in range(planes):
        if i in (0, planes - 1):
            labels[i] = jnp.full((ny + 8, nz), nowhere, jnp.int32)
        else:
            labels[i, pl.ds(ny, 8), :] = jnp.full((8, nz), nowhere, jnp.int32)

    barrier = pltpu.get_barrier_semaphore()
    count = jnp.int32(0)
    for dx, off in near_slabs:
        if dx != 0 and off != 0:
            continue
        near = exists(dx, 0)

        @pl.when(near)
        def _():
            pl.semaphore_signal(
                barrier, inc=1, device_id=(gx + dx, lax.rem(gy + off, n_gy)), device_id_type=MESH
            )

        count = count + near.astype(jnp.int32)

    load_source = pltpu.make_async_copy(
        source_ref, source.at[pl.ds(first, nx), pl.ds(0, ny)], in_sem.at[0]
    )
    load_region = pltpu.make_async_copy(
        region_ref, labels.at[pl.ds(first, nx), pl.ds(0, ny)], in_sem.at[1]
    )
    load_table = pltpu.make_async_copy(table_in, table_ref, in_sem.at[2])
    load_owners = pltpu.make_async_copy(owners_in, owners_ref, in_sem.at[3])
    load_region.start()
    load_table.start()
    load_source.start()
    load_owners.start()

    def box(kind, dx, dy):
        if dx == 0:
            w, high = nx, HALF
        elif dy == 0:
            w, high = BESIDE[kind], ny
        else:
            w, high = CORNER[kind]
        plane = nx - w if dx > 0 else 0
        land = {0: first, -1: last, 1: first - w}[dx]
        row = ny - high if dy > 0 else 0
        to = {0: 0, -1: ny, 1: ny + 8 - high}[dy]
        return (plane, w, row, high), (land, w, to, high)

    def move(kind, dx, dy, here, there):
        plane, w, row, high = here
        base = first if kind == ITERATE else 0
        origin = (region_ref, source_ref, iterate)[kind]
        land, _, to, _ = there
        return pltpu.make_async_remote_copy(
            src_ref=origin.at[pl.ds(base + plane, w), pl.ds(row, high)],
            dst_ref=fields[kind].at[pl.ds(land, w), pl.ds(to, high)],
            send_sem=send_sem.at[abs(dx)],
            recv_sem=recv_sem.at[2 * kind + abs(dx)],
            device_id=(gx + dx, gy + dy),
            device_id_type=MESH,
        )

    def strips(kind, dx):
        far = STRIP[kind]
        plane, land = (nx - far, first - far) if dx > 0 else (far - 1, last + far - 1)
        for row in (0, ny - EDGE):
            yield move(kind, dx, 0, (plane, 1, row, EDGE), (land, 1, row, EDGE))

    def ship(dx):
        side = (1 - dx) // 2
        return pltpu.make_async_remote_copy(
            src_ref=shipped.at[2 + side],
            dst_ref=shipped.at[side],
            send_sem=send_sem.at[1],
            recv_sem=recv_sem.at[2 * SOURCE + 1],
            device_id=(gx + dx, gy),
            device_id_type=MESH,
        )

    def far(dx):
        return lax.rem(gx + (dx + 1) // 2, 4) == 0

    def send(kind, corners=(False, True), late=None):
        for dx, dy in STEPS:
            if (dx * dy != 0) not in corners:
                continue
            now = exists(dx, dy)
            if late is not None and dx != 0:
                now = now & (far(dx) == late)
            elif late:
                continue

            @pl.when(now)
            def _():
                move(kind, dx, dy, *box(kind, dx, dy)).start()
                if dy == 0 and kind != ITERATE:
                    for strip in strips(kind, dx):
                        strip.start()

    def by_neighbours(act):
        for a in (1, 2):
            for b in (1, 2) if n_gy > 2 else (1,):
                xs = exists(-1, 0).astype(jnp.int32) + exists(1, 0).astype(jnp.int32)
                ys = exists(0, -1).astype(jnp.int32) + exists(0, 1).astype(jnp.int32)

                @pl.when((xs == a) & (ys == b))
                def _():
                    act(a, b)

    def wait(ref, sem):
        pltpu.make_async_copy(ref, ref, sem).wait()

    def of_rows(n):
        high = next(r for r in (40, 32, 24, 16, 8, HALF) if n % r == 0 and r <= store.shape[1])
        return store.at[pl.ds(0, n // high), pl.ds(0, high)]

    def beside(kind, b):
        n = BESIDE[kind] * ny + b * CORNER[kind][0] * CORNER[kind][1]
        return n + {REGION: 2 * EDGE, SOURCE: 2 * EDGE + ny, ITERATE: 0}[kind]

    def receive(kind, inner):
        def act(a, b):
            n = nx * b * HALF if inner else a * beside(kind, b)
            wait(of_rows(n), recv_sem.at[2 * kind + 1 - inner])

        by_neighbours(act)

    def finish(a, b):
        wait(of_rows(3 * nx * b * HALF), send_sem.at[0])
        wait(of_rows(a * sum(beside(kind, b) for kind in range(3))), send_sem.at[1])
        wait(group.at[:, :, pl.ds(0, (a * n_gy + n_gy - 1) * cy)], send_sem.at[2])
        wait(holders.at[pl.ds(0, a)], send_sem.at[3])

    def gather(kind, dx, off):
        at = pl.ds(pl.multiple_of(all_y + gy * cy, 8), cy)
        to = pl.ds(pl.multiple_of((1 - dx) * all_y + gy * cy, 8), cy)
        return pltpu.make_async_remote_copy(
            src_ref=group.at[kind, :, at],
            dst_ref=group.at[kind, :, to],
            send_sem=send_sem.at[2],
            recv_sem=recv_sem.at[6 + kind],
            device_id=(gx + dx, lax.rem(gy + off, n_gy)),
            device_id_type=MESH,
        )

    def tell(dx):
        return pltpu.make_async_remote_copy(
            src_ref=holders.at[1],
            dst_ref=holders.at[1 - dx],
            send_sem=send_sem.at[3],
            recv_sem=recv_sem.at[8],
            device_id=(gx + dx, gy),
            device_id_type=MESH,
        )

    def gather_start(kind):
        for dx, off in near_slabs:
            @pl.when(exists(dx, 0))
            def _():
                gather(kind, dx, off).start()

    def gather_wait(kind):
        by_neighbours(lambda a, b: wait(
            group.at[kind, :, pl.ds(0, (a * n_gy + n_gy - 1) * cy)], recv_sem.at[6 + kind]
        ))

    for dy in (-1, 1):
        @pl.when(jnp.logical_not(exists(0, -dy)))
        def _():
            at = pl.ds(ny if dy < 0 else ny + HALF, HALF)
            for ref in (source, iterate):
                ref[:, at, :] = jnp.zeros((planes, HALF, nz), jnp.float32)
    for dx in (-1, 1):
        @pl.when(jnp.logical_not(exists(-dx, 0)))
        def _():
            at = pl.ds(last if dx < 0 else 0, WIDE)
            labels[at] = jnp.full((WIDE, ny + 8, nz), nowhere, jnp.int32)
            for ref in (source, iterate):
                ref[at] = jnp.zeros((WIDE, ny + 8, nz), jnp.float32)
            shipped[(1 - dx) // 2] = jnp.zeros((ny, nz), jnp.float32)
            for kind in range(2):
                ref = group.at[kind, :, pl.ds((1 - dx) * all_y, all_y)]
                ref[...] = jnp.zeros(ref.shape, jnp.float32)
            ref = holders.at[1 - dx]
            ref[...] = jnp.zeros(ref.shape, jnp.float32)

    with jax.named_scope("wait_neighbours"):
        pl.semaphore_wait(barrier, count)
    send(REGION, (False,))
    for off in range(1, n_gy):
        pl.semaphore_signal(
            ready_sem, inc=1, device_id=(gx, lax.rem(gy + off, n_gy)), device_id_type=MESH
        )
    send(SOURCE, (False,), False)

    load_owners.wait()
    eight = lax.broadcasted_iota(jnp.int32, (8, cz), 0)
    held = jnp.zeros((8, cz), jnp.float32)
    for c in range(n_gy):
        held = jnp.where(eight == c, owners_ref[0, c].astype(jnp.float32), held)
    holders[1] = held
    for dx in (-1, 1):
        @pl.when(exists(dx, 0))
        def _():
            tell(dx).start()

    load_table.wait()
    with jax.named_scope("wait_own_region"):
        load_region.wait()
    regions = table_ref.shape[1]
    pair = jnp.concatenate([table_ref[...], jnp.zeros((1, 128 - regions), jnp.float32)], axis=1)
    table = jnp.broadcast_to(pair, (8, 128))

    def look_up(planes, tiles):
        for i in planes:
            for r in tiles:
                for c in range(0, nz, 128):
                    spot = labels[i, pl.ds(r, 8), pl.ds(c, 128)]
                    cond[i, pl.ds(r, 8), pl.ds(c, 128)] = jnp.take_along_axis(table, spot, axis=1)

    look_up(range(first, last), range(0, ny, 8))

    rows = ny + 8

    def blend(a, b, c, keep=rows):
        u = b + 0.5 * (a + c)
        u = u + 0.5 * (pltpu.roll(u, 1, 0) + pltpu.roll(u, rows - 1, 0))
        u = u[:keep]
        parts = [u[:, c:c + 128] for c in range(0, nz, 128)]
        up = [pltpu.roll(p, 1, 1) for p in parts]
        down = [pltpu.roll(p, 127, 1) for p in parts]
        mixed = []
        for j, p in enumerate(parts):
            low = jnp.where(lane128[:1] == 0, up[j - 1] if j else 0.0, up[j])
            high = jnp.where(lane128[:1] == 127, down[j + 1] if j + 1 < len(parts) else 0.0, down[j])
            mixed.append(p + 0.5 * (low + high))
        return jnp.concatenate(mixed, axis=1)

    lane128 = lax.broadcasted_iota(jnp.int32, (8, 128), 1)
    even = lax.rem(2 * lane128, jnp.int32(128))
    half_of = lane128 // 2

    def coarsen(pairs, kind):
        for i, pair_sum in enumerate(pairs):
            total = pair_sum + pltpu.roll(pair_sum, nz - 1, 1)
            for r in range(0, ny, 8):
                low = jnp.take_along_axis(total[r:r + 8, :128], even, axis=1)
                high = jnp.take_along_axis(total[r:r + 8, 128:], even, axis=1)
                squeezed[i, pl.ds(r, 8), :] = jnp.where(lane128 < 64, low, high)
            block = squeezed[i, pl.ds(0, cy, stride=2), :] + squeezed[i, pl.ds(1, cy, stride=2), :]
            group[kind, i, pl.ds(pl.multiple_of(all_y + gy * cy, 8), cy), :] = 0.125 * block

    load_source.wait()
    for dx, i in ((1, last - EDGE), (-1, first + EDGE - 1)):
        mine = cond[i, pl.ds(0, ny), :]
        mixed = blend(cond[i - 1], cond[i], cond[i + 1], ny)
        shipped[2 + (1 - dx) // 2] = (
            RELAX_WEIGHT * source[i, pl.ds(0, ny), :] / (MASS_TERM + 6.0 * mine + mixed)
        )

        @pl.when(exists(dx, 0))
        def _():
            ship(dx).start()

    with jax.named_scope("wait_corners"):
        pl.semaphore_wait(ready_sem, n_gy - 1)
    send(REGION, (True,))
    send(SOURCE, (True,))
    send(SOURCE, (False,), True)

    coarsen(
        [cond[first + 2 * i, pl.ds(0, ny), :] + cond[first + 2 * i + 1, pl.ds(0, ny), :]
         for i in range(cx)],
        0,
    )

    row = lax.broadcasted_iota(jnp.int32, (rows, 1), 0)
    y = gy * ny + jnp.where(row < ny + HALF, row, row - rows)
    in_y = jnp.where((y >= 0) & (y < n_gy * ny), RELAX_WEIGHT, 0.0)

    def weigh(at):
        for i in at:
            mine = cond[i]
            mixed = blend(cond[i - 1], mine, cond[i + 1])
            x = gx * nx + (i - first)
            in_x = jnp.where((x >= 0) & (x < n_gx * nx), 1.0, 0.0)
            weight[i] = (in_y * in_x) / (MASS_TERM + 6.0 * mine + mixed)
            diag2[i] = MASS_TERM + 8.0 * mine + mixed

    with jax.named_scope("wait_region_rows"):
        receive(REGION, True)
    look_up(range(first, last), (ny,))
    weigh(range(first + 1, last - 1))
    with jax.named_scope("wait_region_planes"):
        receive(REGION, False)
    edges = [*range(first - WIDE, first), *range(last, last + WIDE)]
    look_up(edges, range(0, rows, 8))
    weigh([first - 2, first - 1, first, last - 1, last, last + 1])
    with jax.named_scope("start_coarse_cond"):
        gather_start(0)
    def defect(i, values, flux, keep=rows):
        at = pl.ds(0, keep)
        lhs = cond[i, at] * blend(values[i - 1], values[i], values[i + 1], keep)
        rhs = blend(flux[i - 1], flux[i], flux[i + 1], keep)
        return source[i, at] - diag2[i, at] * values[i][:keep] + lhs + rhs

    values, flux, smooth = {}, {}, {}

    def first_sweep(at):
        for i in at:
            values[i] = weight[i] * source[i]
            if i in (first - EDGE, last + EDGE - 1):
                side = int(i > first)
                far = jnp.concatenate([shipped[side], jnp.zeros((8, nz), jnp.float32)])
                values[i] = jnp.where((row > 0) & (row < ny - 1), far, values[i])
            flux[i] = cond[i] * values[i]

    def second_sweep(at):
        for i in at:
            smooth[i] = values[i] + weight[i] * defect(i, values, flux)

    with jax.named_scope("wait_source_rows"):
        receive(SOURCE, True)
    first_sweep(range(first, last))
    second_sweep(range(first + 1, last - 1))
    with jax.named_scope("wait_source_planes"):
        receive(SOURCE, False)
    first_sweep((first - 2, first - 1, last, last + 1))
    second_sweep((first - 1, first, last - 1, last))
    flux = {i: cond[i] * smooth[i] for i in smooth}
    pairs = []
    for i in range(cx):
        j = first + 2 * i
        pairs.append(defect(j, smooth, flux, ny) + defect(j + 1, smooth, flux, ny))
    coarsen(pairs, 1)
    with jax.named_scope("start_coarse_res"):
        gather_start(1)
    for i in range(first, last):
        iterate[i, pl.ds(0, ny), :] = smooth[i][:ny]
    send(ITERATE)

    crow = lax.broadcasted_iota(jnp.int32, (all_y, cz), 0)
    clane = lax.broadcasted_iota(jnp.int32, (1, cz), 1)
    cz_low = jnp.where(clane == 0, 0.0, 0.5)
    cz_high = jnp.where(clane == cz - 1, 0.0, 0.5)

    def coarse_blend(planes, y_low, y_high):
        mixed = []
        for i, u in enumerate(planes):
            near = [planes[j] for j in (i - 1, i + 1) if 0 <= j < cx]
            u = u + 0.5 * functools.reduce(jnp.add, near) if near else u
            u = u + y_low * pltpu.roll(u, 1, 0) + y_high * pltpu.roll(u, all_y - 1, 0)
            mixed.append(u + cz_low * pltpu.roll(u, 1, 1) + cz_high * pltpu.roll(u, cz - 1, 1))
        return mixed

    def total(planes, c):
        whole = functools.reduce(jnp.add, [v[c * cy:(c + 1) * cy] for v in planes])
        return jnp.sum(whole, keepdims=True)

    with jax.named_scope("wait_holders"):
        by_neighbours(lambda a, b: wait(holders.at[pl.ds(0, a)], recv_sem.at[8]))
    with jax.named_scope("wait_coarse_cond"):
        gather_wait(0)
    slabs = []
    for g in range(3):
        held = [holders[g, pl.ds(c, 1), :] for c in range(n_gy)]
        same = lambda a, b: jnp.where(held[a] == held[b], 1.0, 0.0)
        y_low = jnp.where(crow == 0, 0.0, 0.5)
        y_high = jnp.where(crow == all_y - 1, 0.0, 0.5)
        for c in range(1, n_gy):
            tied = 0.5 * same(c - 1, c)
            y_low = jnp.where(crow == c * cy, tied, y_low)
            y_high = jnp.where(crow == c * cy - 1, tied, y_high)
        k = [group[0, i, pl.ds(g * all_y, all_y), :] for i in range(cx)]
        mixed = coarse_blend(k, y_low, y_high)
        diag = [MASS_TERM + 1.5 * a + 0.25 * b for a, b in zip(k, mixed)]
        step = [RELAX_WEIGHT / d for d in diag]
        ones = coarse_blend([jnp.ones((all_y, cz), jnp.float32)] * cx, y_low, y_high)
        slabs.append(dict(
            y_low=y_low, y_high=y_high, k=k, step=step,
            keep=[1.0 - s * (d + 0.5 * a) for s, d, a in zip(step, diag, k)],
            mine=[0.25 * s * a for s, a in zip(step, k)],
            theirs=[0.25 * s for s in step],
            drain=[MASS_TERM + 0.25 * a * (8.0 - b) for a, b in zip(k, ones)],
            same=[[same(a, b)[:, :1] for b in range(n_gy)] for a in range(n_gy)],
            diag_sum=[total(diag, c) for c in range(n_gy)],
        ))

    with jax.named_scope("wait_coarse_res"):
        gather_wait(1)
    e = []
    for g, s in enumerate(slabs):
        s["res"] = [group[1, i, pl.ds(g * all_y, all_y), :] for i in range(cx)]
        s["start"] = [a * b for a, b in zip(s["step"], s["res"])]
        e.append(s["start"])
    for _ in range(COARSE_SWEEPS - 1):
        for g, s in enumerate(slabs):
            straight = coarse_blend(e[g], s["y_low"], s["y_high"])
            carried = coarse_blend([a * v for a, v in zip(s["k"], e[g])], s["y_low"], s["y_high"])
            e[g] = [
                s["start"][i] + s["keep"][i] * e[g][i]
                + (s["mine"][i] * straight[i] + s["theirs"][i] * carried[i])
                for i in range(cx)
            ]
    keep_planes = ((0, cx - 1), *[(1, i) for i in range(cx)], (2, 0))
    ratios = []
    for g, s in enumerate(slabs):
        left = [r - d * v for r, d, v in zip(s["res"], s["drain"], e[g])]
        left = [total(left, c) for c in range(n_gy)]
        shares = []
        for c in range(n_gy):
            num = functools.reduce(jnp.add, [s["same"][c][b] * left[b] for b in range(n_gy)])
            den = functools.reduce(jnp.add, [s["same"][c][b] * s["diag_sum"][b] for b in range(n_gy)])
            shares.append(num / jnp.maximum(den, 1.0))
        ratios.append(shares)
    for slot, (g, i) in enumerate(keep_planes):
        whole_corr[slot, pl.ds(0, 8), :] = jnp.zeros((8, cz), jnp.float32)
        whole_corr[slot, pl.ds(8, all_y), :] = e[g][i]
        whole_corr[slot, pl.ds(8 + all_y, 8), :] = jnp.zeros((8, cz), jnp.float32)

    sub = lax.broadcasted_iota(jnp.int32, (8, nz), 0)

    def of_column(g, column):
        found = jnp.zeros((1, 1), jnp.float32)
        for c in range(n_gy):
            found = jnp.where(column == c, ratios[g][c], found)
        return jnp.broadcast_to(found, (8, nz))

    shifts = [
        (of_column(g, gy), jnp.where(sub < HALF, of_column(g, gy + 1), of_column(g, gy - 1)))
        for g in range(3)
    ]
    for i, (g, _) in enumerate(keep_planes):
        mine = whole_corr[i, pl.ds(pl.multiple_of(8 + gy * cy, 8), cy), :]
        below = whole_corr[i, pl.ds(pl.multiple_of(gy * cy, 8), 8), :]
        above = whole_corr[i, pl.ds(pl.multiple_of(8 + gy * cy + cy, 8), 8), :]
        spread[i, pl.ds(0, cy, stride=2), :] = mine
        spread[i, pl.ds(1, cy, stride=2), :] = mine
        for r in range(0, rows, 8):
            if r < ny:
                tile = spread[i, pl.ds(r, 8), :]
            else:
                tile = jnp.where(
                    sub[:, :cz] < HALF,
                    jnp.broadcast_to(above[:1], (8, cz)),
                    jnp.broadcast_to(below[7:], (8, cz)),
                )
            halves = [
                jnp.take_along_axis(tile, half_of + 64 * part, axis=1) for part in range(2)
            ]
            wide[i, pl.ds(r, 8), :] = jnp.concatenate(halves, axis=1) + shifts[g][int(r >= ny)]
    with jax.named_scope("wait_iterate_rows"):
        receive(ITERATE, True)
    with jax.named_scope("wait_iterate_planes"):
        receive(ITERATE, False)
    values = {
        i: iterate[i] + wide[(i - first + 2) // 2] for i in range(first - 2, last + 2)
    }
    for sweep in range(POST_SWEEPS):
        reach = POST_SWEEPS - 1 - sweep
        keep = rows if reach else ny
        flux = {i: cond[i] * values[i] for i in values}
        values = {
            i: values[i][:keep] + weight[i, pl.ds(0, keep)] * defect(i, values, flux, keep)
            for i in range(first - reach, last + reach)
        }
    for i in range(nx):
        out_ref[i] = values[first + i][:ny]

    with jax.named_scope("wait_sends"):
        by_neighbours(finish)


def on_device(source, region, permeability, owners, *, n_gx, n_gy):
    nx, ny, nz = source.shape
    planes = nx + 2 * WIDE
    cx, all_y, cz = nx // 2, n_gy * ny // 2, nz // 2
    f32 = jnp.float32
    return pl.pallas_call(
        functools.partial(kernel, n_gx, n_gy),
        out_shape=jax.ShapeDtypeStruct(source.shape, f32),
        in_specs=[pl.BlockSpec(memory_space=pltpu.HBM)] * 4,
        out_specs=pl.BlockSpec(memory_space=pltpu.VMEM),
        scratch_shapes=[
            pltpu.SMEM((1, n_gy), jnp.int32),
            pltpu.VMEM((1, permeability.shape[0]), f32),
            pltpu.VMEM((planes, ny + 8, nz), jnp.int32),
            pltpu.VMEM((7 * planes, ny + 8, nz), f32),
            pltpu.VMEM((4, ny, nz), f32),
            pltpu.VMEM((2, cx, 3 * all_y, cz), f32),
            pltpu.VMEM((3, 8, cz), f32),
            pltpu.VMEM((cx, ny, cz), f32),
            pltpu.VMEM((cx + 2, all_y + 16, cz), f32),
            pltpu.VMEM((cx + 2, ny, cz), f32),
            pltpu.VMEM((cx + 2, ny + 8, nz), f32),
            pltpu.SemaphoreType.DMA((4,)),
            pltpu.SemaphoreType.DMA((9,)),
            pltpu.SemaphoreType.DMA((4,)),
            pltpu.SemaphoreType.REGULAR,
        ],
        compiler_params=pltpu.CompilerParams(
            collective_id=0, has_side_effects=True, vmem_limit_bytes=56328192
        ),
    )(*[
        pltpu.with_memory_space_constraint(a, pltpu.HBM)
        for a in (owners, permeability[None, :], source, region)
    ])


def solution(mesh):
    placed = (P("gx", "gy", None), P("gx", "gy", None), P(), P("gx", None))
    body = functools.partial(on_device, n_gx=mesh.shape["gx"], n_gy=mesh.shape["gy"])
    return jax.shard_map(
        body, mesh=mesh, in_specs=placed, out_specs=P("gx", "gy", None), check_vma=False
    )
```

```python
import functools

import jax
import jax.numpy as jnp
from jax import lax
from jax.experimental import pallas as pl
from jax.experimental.pallas import tpu as pltpu
from jax.sharding import PartitionSpec as P

POST_SWEEPS = 2
COARSE_SWEEPS = 6
RELAX_WEIGHT = 0.6
MASS_TERM = 0.1

MESH = pl.DeviceIdType.MESH
WIDE = 3
HALF = 4
REGION, SOURCE, ITERATE = 0, 1, 2
EDGE = 2
BESIDE = (2, 1, 2)
CORNER = ((3, HALF), (2, EDGE), (2, HALF))
STRIP = (3, 2)
STEPS = ((-1, -1), (1, -1), (-1, 1), (1, 1), (0, -1), (0, 1), (-1, 0), (1, 0))


def kernel(
    n_gx, n_gy,
    owners_in, table_in, source_ref, region_ref, out_ref,
    owners_ref, table_ref, labels, store, shipped, group, holders, squeezed, whole_corr, spread, wide,
    send_sem, recv_sem, in_sem, ready_sem, pace_sem,
):
    nx, ny, nz = out_ref.shape
    cx, cy, cz = nx // 2, ny // 2, nz // 2
    first, last = WIDE, WIDE + nx
    gx, gy = lax.axis_index("gx"), lax.axis_index("gy")
    planes = nx + 2 * WIDE
    source, iterate, cond, weight, diag2 = (
        store.at[pl.ds(k * planes, planes)] for k in range(5)
    )
    fields = (labels, source, iterate)
    all_y = n_gy * cy

    def exists(dx, dy):
        x, y = gx + dx, gy + dy
        return (x >= 0) & (x < n_gx) & (y >= 0) & (y < n_gy)

    near_slabs = [
        (dx, off) for dx in (-1, 1, 0) for off in reversed(range(n_gy)) if (dx, off) != (0, 0)
    ]

    nowhere = table_ref.shape[1]
    for i in range(planes):
        if i in (0, planes - 1):
            labels[i] = jnp.full((ny + 8, nz), nowhere, jnp.int32)
        else:
            labels[i, pl.ds(ny, 8), :] = jnp.full((8, nz), nowhere, jnp.int32)

    barrier = pltpu.get_barrier_semaphore()
    count = jnp.int32(0)
    for dx, off in near_slabs:
        if dx != 0 and off != 0:
            continue
        near = exists(dx, 0)

        @pl.when(near)
        def _():
            pl.semaphore_signal(
                barrier, inc=1, device_id=(gx + dx, lax.rem(gy + off, n_gy)), device_id_type=MESH
            )

        count = count + near.astype(jnp.int32)

    load_source = pltpu.make_async_copy(
        source_ref, source.at[pl.ds(first, nx), pl.ds(0, ny)], in_sem.at[0]
    )
    load_region = pltpu.make_async_copy(
        region_ref, labels.at[pl.ds(first, nx), pl.ds(0, ny)], in_sem.at[1]
    )
    load_table = pltpu.make_async_copy(table_in, table_ref, in_sem.at[2])
    load_owners = pltpu.make_async_copy(owners_in, owners_ref, in_sem.at[3])
    load_region.start()
    load_table.start()
    load_source.start()
    load_owners.start()

    def box(kind, dx, dy):
        if dx == 0:
            w, high = nx, HALF
        elif dy == 0:
            w, high = BESIDE[kind], ny
        else:
            w, high = CORNER[kind]
        plane = nx - w if dx > 0 else 0
        land = {0: first, -1: last, 1: first - w}[dx]
        row = ny - high if dy > 0 else 0
        to = {0: 0, -1: ny, 1: ny + 8 - high}[dy]
        return (plane, w, row, high), (land, w, to, high)

    def move(kind, dx, dy, here, there):
        plane, w, row, high = here
        base = first if kind == ITERATE else 0
        origin = (region_ref, source_ref, iterate)[kind]
        land, _, to, _ = there
        return pltpu.make_async_remote_copy(
            src_ref=origin.at[pl.ds(base + plane, w), pl.ds(row, high)],
            dst_ref=fields[kind].at[pl.ds(land, w), pl.ds(to, high)],
            send_sem=send_sem.at[abs(dx)],
            recv_sem=recv_sem.at[2 * kind + abs(dx)],
            device_id=(gx + dx, gy + dy),
            device_id_type=MESH,
        )

    def strips(kind, dx):
        far = STRIP[kind]
        plane, land = (nx - far, first - far) if dx > 0 else (far - 1, last + far - 1)
        for row in (0, ny - EDGE):
            yield move(kind, dx, 0, (plane, 1, row, EDGE), (land, 1, row, EDGE))

    def ship(dx):
        side = (1 - dx) // 2
        return pltpu.make_async_remote_copy(
            src_ref=shipped.at[2 + side],
            dst_ref=shipped.at[side],
            send_sem=send_sem.at[1],
            recv_sem=recv_sem.at[2 * SOURCE + 1],
            device_id=(gx + dx, gy),
            device_id_type=MESH,
        )

    def far(dx):
        return lax.rem(gx + (dx + 1) // 2, 4) == 0

    def to_group(sem):
        for off in range(1, n_gy):
            pl.semaphore_signal(
                sem, inc=1, device_id=(gx, lax.rem(gy + off, n_gy)), device_id_type=MESH
            )

    def send(kind, corners=(False, True), late=None):
        for dx, dy in STEPS:
            if (dx * dy != 0) not in corners:
                continue
            now = exists(dx, dy)
            if late is not None and dx != 0:
                now = now & (far(dx) == late)
            elif late:
                continue

            @pl.when(now)
            def _():
                move(kind, dx, dy, *box(kind, dx, dy)).start()
                if dy == 0 and kind != ITERATE:
                    for strip in strips(kind, dx):
                        strip.start()

    def by_neighbours(act):
        for a in (1, 2):
            for b in (1, 2) if n_gy > 2 else (1,):
                xs = exists(-1, 0).astype(jnp.int32) + exists(1, 0).astype(jnp.int32)
                ys = exists(0, -1).astype(jnp.int32) + exists(0, 1).astype(jnp.int32)

                @pl.when((xs == a) & (ys == b))
                def _():
                    act(a, b)

    def wait(ref, sem):
        pltpu.make_async_copy(ref, ref, sem).wait()

    def of_rows(n):
        high = next(r for r in (40, 32, 24, 16, 8, HALF) if n % r == 0 and r <= store.shape[1])
        return store.at[pl.ds(0, n // high), pl.ds(0, high)]

    def beside(kind, b):
        n = BESIDE[kind] * ny + b * CORNER[kind][0] * CORNER[kind][1]
        return n + {REGION: 2 * EDGE, SOURCE: 2 * EDGE + ny, ITERATE: 0}[kind]

    def receive(kind, inner):
        def act(a, b):
            n = nx * b * HALF if inner else a * beside(kind, b)
            wait(of_rows(n), recv_sem.at[2 * kind + 1 - inner])

        by_neighbours(act)

    def finish(a, b):
        wait(of_rows(3 * nx * b * HALF), send_sem.at[0])
        wait(of_rows(a * sum(beside(kind, b) for kind in range(3))), send_sem.at[1])
        wait(group.at[:, :, pl.ds(0, (a * n_gy + n_gy - 1) * cy)], send_sem.at[2])
        wait(holders.at[pl.ds(0, a)], send_sem.at[3])

    def gather(kind, dx, off):
        at = pl.ds(pl.multiple_of(all_y + gy * cy, 8), cy)
        to = pl.ds(pl.multiple_of((1 - dx) * all_y + gy * cy, 8), cy)
        return pltpu.make_async_remote_copy(
            src_ref=group.at[kind, :, at],
            dst_ref=group.at[kind, :, to],
            send_sem=send_sem.at[2],
            recv_sem=recv_sem.at[6 + kind],
            device_id=(gx + dx, lax.rem(gy + off, n_gy)),
            device_id_type=MESH,
        )

    def tell(dx):
        return pltpu.make_async_remote_copy(
            src_ref=holders.at[1],
            dst_ref=holders.at[1 - dx],
            send_sem=send_sem.at[3],
            recv_sem=recv_sem.at[8],
            device_id=(gx + dx, gy),
            device_id_type=MESH,
        )

    def gather_start(kind):
        for dx, off in near_slabs:
            @pl.when(exists(dx, 0))
            def _():
                gather(kind, dx, off).start()

    def gather_wait(kind):
        by_neighbours(lambda a, b: wait(
            group.at[kind, :, pl.ds(0, (a * n_gy + n_gy - 1) * cy)], recv_sem.at[6 + kind]
        ))

    for dy in (-1, 1):
        @pl.when(jnp.logical_not(exists(0, -dy)))
        def _():
            at = pl.ds(ny if dy < 0 else ny + HALF, HALF)
            for ref in (source, iterate):
                ref[:, at, :] = jnp.zeros((planes, HALF, nz), jnp.float32)
    for dx in (-1, 1):
        @pl.when(jnp.logical_not(exists(-dx, 0)))
        def _():
            at = pl.ds(last if dx < 0 else 0, WIDE)
            labels[at] = jnp.full((WIDE, ny + 8, nz), nowhere, jnp.int32)
            for ref in (source, iterate):
                ref[at] = jnp.zeros((WIDE, ny + 8, nz), jnp.float32)
            shipped[(1 - dx) // 2] = jnp.zeros((ny, nz), jnp.float32)
            for kind in range(2):
                ref = group.at[kind, :, pl.ds((1 - dx) * all_y, all_y)]
                ref[...] = jnp.zeros(ref.shape, jnp.float32)
            ref = holders.at[1 - dx]
            ref[...] = jnp.zeros(ref.shape, jnp.float32)

    with jax.named_scope("wait_neighbours"):
        pl.semaphore_wait(barrier, count)
    send(REGION, (False,))
    to_group(ready_sem)
    send(SOURCE, (False,), False)

    load_owners.wait()
    eight = lax.broadcasted_iota(jnp.int32, (8, cz), 0)
    held = jnp.zeros((8, cz), jnp.float32)
    for c in range(n_gy):
        held = jnp.where(eight == c, owners_ref[0, c].astype(jnp.float32), held)
    holders[1] = held
    for dx in (-1, 1):
        @pl.when(exists(dx, 0))
        def _():
            tell(dx).start()

    load_table.wait()
    with jax.named_scope("wait_own_region"):
        load_region.wait()
    regions = table_ref.shape[1]
    pair = jnp.concatenate([table_ref[...], jnp.zeros((1, 128 - regions), jnp.float32)], axis=1)
    table = jnp.broadcast_to(pair, (8, 128))

    def look_up(planes, tiles):
        for i in planes:
            for r in tiles:
                for c in range(0, nz, 128):
                    spot = labels[i, pl.ds(r, 8), pl.ds(c, 128)]
                    cond[i, pl.ds(r, 8), pl.ds(c, 128)] = jnp.take_along_axis(table, spot, axis=1)

    look_up(range(first, last), range(0, ny, 8))

    rows = ny + 8

    def blend(a, b, c, keep=rows):
        u = b + 0.5 * (a + c)
        u = u + 0.5 * (pltpu.roll(u, 1, 0) + pltpu.roll(u, rows - 1, 0))
        u = u[:keep]
        parts = [u[:, c:c + 128] for c in range(0, nz, 128)]
        up = [pltpu.roll(p, 1, 1) for p in parts]
        down = [pltpu.roll(p, 127, 1) for p in parts]
        mixed = []
        for j, p in enumerate(parts):
            low = jnp.where(lane128[:1] == 0, up[j - 1] if j else 0.0, up[j])
            high = jnp.where(lane128[:1] == 127, down[j + 1] if j + 1 < len(parts) else 0.0, down[j])
            mixed.append(p + 0.5 * (low + high))
        return jnp.concatenate(mixed, axis=1)

    lane128 = lax.broadcasted_iota(jnp.int32, (8, 128), 1)
    even = lax.rem(2 * lane128, jnp.int32(128))
    half_of = lane128 // 2

    def coarsen(pairs, kind):
        for i, pair_sum in enumerate(pairs):
            total = pair_sum + pltpu.roll(pair_sum, nz - 1, 1)
            for r in range(0, ny, 8):
                low = jnp.take_along_axis(total[r:r + 8, :128], even, axis=1)
                high = jnp.take_along_axis(total[r:r + 8, 128:], even, axis=1)
                squeezed[i, pl.ds(r, 8), :] = jnp.where(lane128 < 64, low, high)
            block = squeezed[i, pl.ds(0, cy, stride=2), :] + squeezed[i, pl.ds(1, cy, stride=2), :]
            group[kind, i, pl.ds(pl.multiple_of(all_y + gy * cy, 8), cy), :] = 0.125 * block

    load_source.wait()
    for dx, i in ((1, last - EDGE), (-1, first + EDGE - 1)):
        mine = cond[i, pl.ds(0, ny), :]
        mixed = blend(cond[i - 1], cond[i], cond[i + 1], ny)
        shipped[2 + (1 - dx) // 2] = (
            RELAX_WEIGHT * source[i, pl.ds(0, ny), :] / (MASS_TERM + 6.0 * mine + mixed)
        )

        @pl.when(exists(dx, 0) & jnp.logical_not(far(dx)))
        def _():
            ship(dx).start()

    with jax.named_scope("wait_corners"):
        pl.semaphore_wait(ready_sem, n_gy - 1)
    send(REGION, (True,))
    send(SOURCE, (True,))
    coarsen(
        [cond[first + 2 * i, pl.ds(0, ny), :] + cond[first + 2 * i + 1, pl.ds(0, ny), :]
         for i in range(cx)],
        0,
    )

    row = lax.broadcasted_iota(jnp.int32, (rows, 1), 0)
    y = gy * ny + jnp.where(row < ny + HALF, row, row - rows)
    in_y = jnp.where((y >= 0) & (y < n_gy * ny), RELAX_WEIGHT, 0.0)

    def weigh(at):
        for i in at:
            mine = cond[i]
            mixed = blend(cond[i - 1], mine, cond[i + 1])
            x = gx * nx + (i - first)
            in_x = jnp.where((x >= 0) & (x < n_gx * nx), 1.0, 0.0)
            weight[i] = (in_y * in_x) / (MASS_TERM + 6.0 * mine + mixed)
            diag2[i] = MASS_TERM + 8.0 * mine + mixed

    with jax.named_scope("pace"):
        to_group(pace_sem)
        pl.semaphore_wait(pace_sem, n_gy - 1)
    send(SOURCE, (False,), True)
    for dx in (-1, 1):
        @pl.when(exists(dx, 0) & far(dx))
        def _():
            ship(dx).start()

    with jax.named_scope("wait_region_rows"):
        receive(REGION, True)
    look_up(range(first, last), (ny,))
    weigh(range(first + 1, last - 1))
    with jax.named_scope("wait_region_planes"):
        receive(REGION, False)
    edges = [*range(first - WIDE, first), *range(last, last + WIDE)]
    look_up(edges, range(0, rows, 8))
    weigh([first - 2, first - 1, first, last - 1, last, last + 1])
    with jax.named_scope("start_coarse_cond"):
        gather_start(0)
    def defect(i, values, flux, keep=rows):
        at = pl.ds(0, keep)
        lhs = cond[i, at] * blend(values[i - 1], values[i], values[i + 1], keep)
        rhs = blend(flux[i - 1], flux[i], flux[i + 1], keep)
        return source[i, at] - diag2[i, at] * values[i][:keep] + lhs + rhs

    values, flux, smooth = {}, {}, {}

    def first_sweep(at):
        for i in at:
            values[i] = weight[i] * source[i]
            if i in (first - EDGE, last + EDGE - 1):
                side = int(i > first)
                far = jnp.concatenate([shipped[side], jnp.zeros((8, nz), jnp.float32)])
                values[i] = jnp.where((row > 0) & (row < ny - 1), far, values[i])
            flux[i] = cond[i] * values[i]

    def second_sweep(at):
        for i in at:
            smooth[i] = values[i] + weight[i] * defect(i, values, flux)

    with jax.named_scope("wait_source_rows"):
        receive(SOURCE, True)
    first_sweep(range(first, last))
    second_sweep(range(first + 1, last - 1))
    with jax.named_scope("wait_source_planes"):
        receive(SOURCE, False)
    first_sweep((first - 2, first - 1, last, last + 1))
    second_sweep((first - 1, first, last - 1, last))
    flux = {i: cond[i] * smooth[i] for i in smooth}
    pairs = []
    for i in range(cx):
        j = first + 2 * i
        pairs.append(defect(j, smooth, flux, ny) + defect(j + 1, smooth, flux, ny))
    coarsen(pairs, 1)
    with jax.named_scope("start_coarse_res"):
        gather_start(1)
    for i in range(first, last):
        iterate[i, pl.ds(0, ny), :] = smooth[i][:ny]
    send(ITERATE)

    crow = lax.broadcasted_iota(jnp.int32, (all_y, cz), 0)
    clane = lax.broadcasted_iota(jnp.int32, (1, cz), 1)
    cz_low = jnp.where(clane == 0, 0.0, 0.5)
    cz_high = jnp.where(clane == cz - 1, 0.0, 0.5)

    def coarse_blend(planes, y_low, y_high):
        mixed = []
        for i, u in enumerate(planes):
            near = [planes[j] for j in (i - 1, i + 1) if 0 <= j < cx]
            u = u + 0.5 * functools.reduce(jnp.add, near) if near else u
            u = u + y_low * pltpu.roll(u, 1, 0) + y_high * pltpu.roll(u, all_y - 1, 0)
            mixed.append(u + cz_low * pltpu.roll(u, 1, 1) + cz_high * pltpu.roll(u, cz - 1, 1))
        return mixed

    def total(planes, c):
        whole = functools.reduce(jnp.add, [v[c * cy:(c + 1) * cy] for v in planes])
        return jnp.sum(whole, keepdims=True)

    with jax.named_scope("wait_holders"):
        by_neighbours(lambda a, b: wait(holders.at[pl.ds(0, a)], recv_sem.at[8]))
    with jax.named_scope("wait_coarse_cond"):
        gather_wait(0)
    slabs = []
    for g in range(3):
        held = [holders[g, pl.ds(c, 1), :] for c in range(n_gy)]
        same = lambda a, b: jnp.where(held[a] == held[b], 1.0, 0.0)
        y_low = jnp.where(crow == 0, 0.0, 0.5)
        y_high = jnp.where(crow == all_y - 1, 0.0, 0.5)
        for c in range(1, n_gy):
            tied = 0.5 * same(c - 1, c)
            y_low = jnp.where(crow == c * cy, tied, y_low)
            y_high = jnp.where(crow == c * cy - 1, tied, y_high)
        k = [group[0, i, pl.ds(g * all_y, all_y), :] for i in range(cx)]
        mixed = coarse_blend(k, y_low, y_high)
        diag = [MASS_TERM + 1.5 * a + 0.25 * b for a, b in zip(k, mixed)]
        step = [RELAX_WEIGHT / d for d in diag]
        ones = coarse_blend([jnp.ones((all_y, cz), jnp.float32)] * cx, y_low, y_high)
        slabs.append(dict(
            y_low=y_low, y_high=y_high, k=k, step=step,
            keep=[1.0 - s * (d + 0.5 * a) for s, d, a in zip(step, diag, k)],
            mine=[0.25 * s * a for s, a in zip(step, k)],
            theirs=[0.25 * s for s in step],
            drain=[MASS_TERM + 0.25 * a * (8.0 - b) for a, b in zip(k, ones)],
            same=[[same(a, b)[:, :1] for b in range(n_gy)] for a in range(n_gy)],
            diag_sum=[total(diag, c) for c in range(n_gy)],
        ))

    with jax.named_scope("wait_coarse_res"):
        gather_wait(1)
    e = []
    for g, s in enumerate(slabs):
        s["res"] = [group[1, i, pl.ds(g * all_y, all_y), :] for i in range(cx)]
        s["start"] = [a * b for a, b in zip(s["step"], s["res"])]
        e.append(s["start"])
    for _ in range(COARSE_SWEEPS - 1):
        for g, s in enumerate(slabs):
            straight = coarse_blend(e[g], s["y_low"], s["y_high"])
            carried = coarse_blend([a * v for a, v in zip(s["k"], e[g])], s["y_low"], s["y_high"])
            e[g] = [
                s["start"][i] + s["keep"][i] * e[g][i]
                + (s["mine"][i] * straight[i] + s["theirs"][i] * carried[i])
                for i in range(cx)
            ]
    keep_planes = ((0, cx - 1), *[(1, i) for i in range(cx)], (2, 0))
    ratios = []
    for g, s in enumerate(slabs):
        left = [r - d * v for r, d, v in zip(s["res"], s["drain"], e[g])]
        left = [total(left, c) for c in range(n_gy)]
        shares = []
        for c in range(n_gy):
            num = functools.reduce(jnp.add, [s["same"][c][b] * left[b] for b in range(n_gy)])
            den = functools.reduce(jnp.add, [s["same"][c][b] * s["diag_sum"][b] for b in range(n_gy)])
            shares.append(num / jnp.maximum(den, 1.0))
        ratios.append(shares)
    for slot, (g, i) in enumerate(keep_planes):
        whole_corr[slot, pl.ds(0, 8), :] = jnp.zeros((8, cz), jnp.float32)
        whole_corr[slot, pl.ds(8, all_y), :] = e[g][i]
        whole_corr[slot, pl.ds(8 + all_y, 8), :] = jnp.zeros((8, cz), jnp.float32)

    sub = lax.broadcasted_iota(jnp.int32, (8, nz), 0)

    def of_column(g, column):
        found = jnp.zeros((1, 1), jnp.float32)
        for c in range(n_gy):
            found = jnp.where(column == c, ratios[g][c], found)
        return jnp.broadcast_to(found, (8, nz))

    shifts = [
        (of_column(g, gy), jnp.where(sub < HALF, of_column(g, gy + 1), of_column(g, gy - 1)))
        for g in range(3)
    ]
    for i, (g, _) in enumerate(keep_planes):
        mine = whole_corr[i, pl.ds(pl.multiple_of(8 + gy * cy, 8), cy), :]
        below = whole_corr[i, pl.ds(pl.multiple_of(gy * cy, 8), 8), :]
        above = whole_corr[i, pl.ds(pl.multiple_of(8 + gy * cy + cy, 8), 8), :]
        spread[i, pl.ds(0, cy, stride=2), :] = mine
        spread[i, pl.ds(1, cy, stride=2), :] = mine
        for r in range(0, rows, 8):
            if r < ny:
                tile = spread[i, pl.ds(r, 8), :]
            else:
                tile = jnp.where(
                    sub[:, :cz] < HALF,
                    jnp.broadcast_to(above[:1], (8, cz)),
                    jnp.broadcast_to(below[7:], (8, cz)),
                )
            halves = [
                jnp.take_along_axis(tile, half_of + 64 * part, axis=1) for part in range(2)
            ]
            wide[i, pl.ds(r, 8), :] = jnp.concatenate(halves, axis=1) + shifts[g][int(r >= ny)]
    with jax.named_scope("wait_iterate_rows"):
        receive(ITERATE, True)
    with jax.named_scope("wait_iterate_planes"):
        receive(ITERATE, False)
    values = {
        i: iterate[i] + wide[(i - first + 2) // 2] for i in range(first - 2, last + 2)
    }
    for sweep in range(POST_SWEEPS):
        reach = POST_SWEEPS - 1 - sweep
        keep = rows if reach else ny
        flux = {i: cond[i] * values[i] for i in values}
        values = {
            i: values[i][:keep] + weight[i, pl.ds(0, keep)] * defect(i, values, flux, keep)
            for i in range(first - reach, last + reach)
        }
    for i in range(nx):
        out_ref[i] = values[first + i][:ny]

    with jax.named_scope("wait_sends"):
        by_neighbours(finish)


def on_device(source, region, permeability, owners, *, n_gx, n_gy):
    nx, ny, nz = source.shape
    planes = nx + 2 * WIDE
    cx, all_y, cz = nx // 2, n_gy * ny // 2, nz // 2
    f32 = jnp.float32
    return pl.pallas_call(
        functools.partial(kernel, n_gx, n_gy),
        out_shape=jax.ShapeDtypeStruct(source.shape, f32),
        in_specs=[pl.BlockSpec(memory_space=pltpu.HBM)] * 4,
        out_specs=pl.BlockSpec(memory_space=pltpu.VMEM),
        scratch_shapes=[
            pltpu.SMEM((1, n_gy), jnp.int32),
            pltpu.VMEM((1, permeability.shape[0]), f32),
            pltpu.VMEM((planes, ny + 8, nz), jnp.int32),
            pltpu.VMEM((7 * planes, ny + 8, nz), f32),
            pltpu.VMEM((4, ny, nz), f32),
            pltpu.VMEM((2, cx, 3 * all_y, cz), f32),
            pltpu.VMEM((3, 8, cz), f32),
            pltpu.VMEM((cx, ny, cz), f32),
            pltpu.VMEM((cx + 2, all_y + 16, cz), f32),
            pltpu.VMEM((cx + 2, ny, cz), f32),
            pltpu.VMEM((cx + 2, ny + 8, nz), f32),
            pltpu.SemaphoreType.DMA((4,)),
            pltpu.SemaphoreType.DMA((9,)),
            pltpu.SemaphoreType.DMA((4,)),
            pltpu.SemaphoreType.REGULAR,
            pltpu.SemaphoreType.REGULAR,
        ],
        compiler_params=pltpu.CompilerParams(
            collective_id=0, has_side_effects=True, vmem_limit_bytes=56328192
        ),
    )(*[
        pltpu.with_memory_space_constraint(a, pltpu.HBM)
        for a in (owners, permeability[None, :], source, region)
    ])


def solution(mesh):
    placed = (P("gx", "gy", None), P("gx", "gy", None), P(), P("gx", None))
    body = functools.partial(on_device, n_gx=mesh.shape["gx"], n_gy=mesh.shape["gy"])
    return jax.shard_map(
        body, mesh=mesh, in_specs=placed, out_specs=P("gx", "gy", None), check_vma=False
    )
```

```python
import functools

import jax
import jax.numpy as jnp
from jax import lax
from jax.experimental import pallas as pl
from jax.experimental.pallas import tpu as pltpu
from jax.sharding import PartitionSpec as P

POST_SWEEPS = 2
COARSE_SWEEPS = 6
RELAX_WEIGHT = 0.6
MASS_TERM = 0.1

MESH = pl.DeviceIdType.MESH
WIDE = 3
HALF = 4
REGION, SOURCE, ITERATE = 0, 1, 2
EDGE = 2
BESIDE = (2, 1, 2)
CORNER = ((3, HALF), (2, EDGE), (2, HALF))
STRIP = (3, 2)
STEPS = ((-1, -1), (1, -1), (-1, 1), (1, 1), (0, -1), (0, 1), (-1, 0), (1, 0))


def kernel(
    n_gx, n_gy,
    owners_in, table_in, source_ref, region_ref, out_ref,
    owners_ref, table_ref, labels, store, shipped, group, holders, squeezed, whole_corr, spread, wide,
    send_sem, recv_sem, in_sem, ready_sem, pace_sem,
):
    nx, ny, nz = out_ref.shape
    cx, cy, cz = nx // 2, ny // 2, nz // 2
    first, last = WIDE, WIDE + nx
    gx, gy = lax.axis_index("gx"), lax.axis_index("gy")
    planes = nx + 2 * WIDE
    source, iterate, cond, weight, diag2 = (
        store.at[pl.ds(k * planes, planes)] for k in range(5)
    )
    fields = (labels, source, iterate)
    all_y = n_gy * cy

    def exists(dx, dy):
        x, y = gx + dx, gy + dy
        return (x >= 0) & (x < n_gx) & (y >= 0) & (y < n_gy)

    near_slabs = [
        (dx, off) for dx in (-1, 1, 0) for off in reversed(range(n_gy)) if (dx, off) != (0, 0)
    ]

    nowhere = table_ref.shape[1]
    for i in range(planes):
        if i in (0, planes - 1):
            labels[i] = jnp.full((ny + 8, nz), nowhere, jnp.int32)
        else:
            labels[i, pl.ds(ny, 8), :] = jnp.full((8, nz), nowhere, jnp.int32)

    barrier = pltpu.get_barrier_semaphore()
    count = jnp.int32(0)
    for dx, off in near_slabs:
        if dx != 0 and off != 0:
            continue
        near = exists(dx, 0)

        @pl.when(near)
        def _():
            pl.semaphore_signal(
                barrier, inc=1, device_id=(gx + dx, lax.rem(gy + off, n_gy)), device_id_type=MESH
            )

        count = count + near.astype(jnp.int32)

    load_source = pltpu.make_async_copy(
        source_ref, source.at[pl.ds(first, nx), pl.ds(0, ny)], in_sem.at[0]
    )
    load_region = pltpu.make_async_copy(
        region_ref, labels.at[pl.ds(first, nx), pl.ds(0, ny)], in_sem.at[1]
    )
    load_table = pltpu.make_async_copy(table_in, table_ref, in_sem.at[2])
    load_owners = pltpu.make_async_copy(owners_in, owners_ref, in_sem.at[3])
    load_region.start()
    load_table.start()
    load_source.start()
    load_owners.start()

    def box(kind, dx, dy):
        if dx == 0:
            w, high = nx, HALF
        elif dy == 0:
            w, high = BESIDE[kind], ny
        else:
            w, high = CORNER[kind]
        plane = nx - w if dx > 0 else 0
        land = {0: first, -1: last, 1: first - w}[dx]
        row = ny - high if dy > 0 else 0
        to = {0: 0, -1: ny, 1: ny + 8 - high}[dy]
        return (plane, w, row, high), (land, w, to, high)

    def move(kind, dx, dy, here, there):
        plane, w, row, high = here
        land, _, to, _ = there
        return pltpu.make_async_remote_copy(
            src_ref=fields[kind].at[pl.ds(first + plane, w), pl.ds(row, high)],
            dst_ref=fields[kind].at[pl.ds(land, w), pl.ds(to, high)],
            send_sem=send_sem.at[abs(dx)],
            recv_sem=recv_sem.at[9 if kind == REGION and dx * dy else 2 * kind + abs(dx)],
            device_id=(gx + dx, gy + dy),
            device_id_type=MESH,
        )

    def strips(kind, dx):
        far = STRIP[kind]
        plane, land = (nx - far, first - far) if dx > 0 else (far - 1, last + far - 1)
        for row in (0, ny - EDGE):
            yield move(kind, dx, 0, (plane, 1, row, EDGE), (land, 1, row, EDGE))

    def ship(dx):
        side = (1 - dx) // 2
        return pltpu.make_async_remote_copy(
            src_ref=shipped.at[2 + side],
            dst_ref=shipped.at[side],
            send_sem=send_sem.at[1],
            recv_sem=recv_sem.at[2 * SOURCE + 1],
            device_id=(gx + dx, gy),
            device_id_type=MESH,
        )

    def far(dx):
        return lax.rem(gx + (dx + 1) // 2, 4) == 0

    def to_group(sem):
        for off in range(1, n_gy):
            pl.semaphore_signal(
                sem, inc=1, device_id=(gx, lax.rem(gy + off, n_gy)), device_id_type=MESH
            )

    def send(kind, corners=(False, True), late=None):
        for dx, dy in STEPS:
            if (dx * dy != 0) not in corners:
                continue
            now = exists(dx, dy)
            if late is not None and dx != 0:
                now = now & (far(dx) == late)
            elif late:
                continue

            @pl.when(now)
            def _():
                move(kind, dx, dy, *box(kind, dx, dy)).start()
                if dy == 0 and kind != ITERATE:
                    for strip in strips(kind, dx):
                        strip.start()

    def by_neighbours(act):
        for a in (1, 2):
            for b in (1, 2) if n_gy > 2 else (1,):
                xs = exists(-1, 0).astype(jnp.int32) + exists(1, 0).astype(jnp.int32)
                ys = exists(0, -1).astype(jnp.int32) + exists(0, 1).astype(jnp.int32)

                @pl.when((xs == a) & (ys == b))
                def _():
                    act(a, b)

    def wait(ref, sem):
        pltpu.make_async_copy(ref, ref, sem).wait()

    def of_rows(n):
        high = next(r for r in (40, 32, 24, 16, 8, HALF) if n % r == 0 and r <= store.shape[1])
        return store.at[pl.ds(0, n // high), pl.ds(0, high)]

    def beside(kind, b):
        n = BESIDE[kind] * ny + b * CORNER[kind][0] * CORNER[kind][1]
        return n + {REGION: 2 * EDGE, SOURCE: 2 * EDGE + ny, ITERATE: 0}[kind]

    def receive(kind, inner):
        def act(a, b):
            n = nx * b * HALF if inner else a * beside(kind, 0 if kind == REGION else b)
            wait(of_rows(n), recv_sem.at[2 * kind + 1 - inner])

        by_neighbours(act)

    def finish(a, b):
        wait(of_rows(3 * nx * b * HALF), send_sem.at[0])
        wait(of_rows(a * sum(beside(kind, b) for kind in range(3))), send_sem.at[1])
        wait(group.at[:, :, pl.ds(0, (a * n_gy + n_gy - 1) * cy)], send_sem.at[2])
        wait(holders.at[pl.ds(0, a)], send_sem.at[3])

    def gather(kind, dx, off):
        at = pl.ds(pl.multiple_of(all_y + gy * cy, 8), cy)
        to = pl.ds(pl.multiple_of((1 - dx) * all_y + gy * cy, 8), cy)
        return pltpu.make_async_remote_copy(
            src_ref=group.at[kind, :, at],
            dst_ref=group.at[kind, :, to],
            send_sem=send_sem.at[2],
            recv_sem=recv_sem.at[6 + kind],
            device_id=(gx + dx, lax.rem(gy + off, n_gy)),
            device_id_type=MESH,
        )

    def tell(dx):
        return pltpu.make_async_remote_copy(
            src_ref=holders.at[1],
            dst_ref=holders.at[1 - dx],
            send_sem=send_sem.at[3],
            recv_sem=recv_sem.at[8],
            device_id=(gx + dx, gy),
            device_id_type=MESH,
        )

    def gather_start(kind):
        for dx, off in near_slabs:
            @pl.when(exists(dx, 0))
            def _():
                gather(kind, dx, off).start()

    def gather_wait(kind):
        by_neighbours(lambda a, b: wait(
            group.at[kind, :, pl.ds(0, (a * n_gy + n_gy - 1) * cy)], recv_sem.at[6 + kind]
        ))

    for dy in (-1, 1):
        @pl.when(jnp.logical_not(exists(0, -dy)))
        def _():
            at = pl.ds(ny if dy < 0 else ny + HALF, HALF)
            for ref in (source, iterate):
                ref[:, at, :] = jnp.zeros((planes, HALF, nz), jnp.float32)
    for dx in (-1, 1):
        @pl.when(jnp.logical_not(exists(-dx, 0)))
        def _():
            at = pl.ds(last if dx < 0 else 0, WIDE)
            labels[at] = jnp.full((WIDE, ny + 8, nz), nowhere, jnp.int32)
            for ref in (source, iterate):
                ref[at] = jnp.zeros((WIDE, ny + 8, nz), jnp.float32)
            shipped[(1 - dx) // 2] = jnp.zeros((ny, nz), jnp.float32)
            for kind in range(2):
                ref = group.at[kind, :, pl.ds((1 - dx) * all_y, all_y)]
                ref[...] = jnp.zeros(ref.shape, jnp.float32)
            ref = holders.at[1 - dx]
            ref[...] = jnp.zeros(ref.shape, jnp.float32)

    with jax.named_scope("wait_neighbours"):
        pl.semaphore_wait(barrier, count)
    with jax.named_scope("wait_own_region"):
        load_region.wait()
    send(REGION, (False,))
    to_group(ready_sem)
    load_source.wait()
    send(SOURCE, (False,), False)

    load_owners.wait()
    eight = lax.broadcasted_iota(jnp.int32, (8, cz), 0)
    held = jnp.zeros((8, cz), jnp.float32)
    for c in range(n_gy):
        held = jnp.where(eight == c, owners_ref[0, c].astype(jnp.float32), held)
    holders[1] = held
    for dx in (-1, 1):
        @pl.when(exists(dx, 0))
        def _():
            tell(dx).start()

    load_table.wait()
    regions = table_ref.shape[1]
    pair = jnp.concatenate([table_ref[...], jnp.zeros((1, 128 - regions), jnp.float32)], axis=1)
    table = jnp.broadcast_to(pair, (8, 128))

    def look_up(planes, tiles):
        for i in planes:
            for r in tiles:
                for c in range(0, nz, 128):
                    spot = labels[i, pl.ds(r, 8), pl.ds(c, 128)]
                    cond[i, pl.ds(r, 8), pl.ds(c, 128)] = jnp.take_along_axis(table, spot, axis=1)

    look_up(range(first, last), range(0, ny, 8))

    rows = ny + 8

    def blend(a, b, c, keep=rows):
        u = b + 0.5 * (a + c)
        u = u + 0.5 * (pltpu.roll(u, 1, 0) + pltpu.roll(u, rows - 1, 0))
        u = u[:keep]
        parts = [u[:, c:c + 128] for c in range(0, nz, 128)]
        up = [pltpu.roll(p, 1, 1) for p in parts]
        down = [pltpu.roll(p, 127, 1) for p in parts]
        mixed = []
        for j, p in enumerate(parts):
            low = jnp.where(lane128[:1] == 0, up[j - 1] if j else 0.0, up[j])
            high = jnp.where(lane128[:1] == 127, down[j + 1] if j + 1 < len(parts) else 0.0, down[j])
            mixed.append(p + 0.5 * (low + high))
        return jnp.concatenate(mixed, axis=1)

    lane128 = lax.broadcasted_iota(jnp.int32, (8, 128), 1)
    even = lax.rem(2 * lane128, jnp.int32(128))
    half_of = lane128 // 2

    def coarsen(pairs, kind):
        for i, pair_sum in enumerate(pairs):
            total = pair_sum + pltpu.roll(pair_sum, nz - 1, 1)
            for r in range(0, ny, 8):
                low = jnp.take_along_axis(total[r:r + 8, :128], even, axis=1)
                high = jnp.take_along_axis(total[r:r + 8, 128:], even, axis=1)
                squeezed[i, pl.ds(r, 8), :] = jnp.where(lane128 < 64, low, high)
            block = squeezed[i, pl.ds(0, cy, stride=2), :] + squeezed[i, pl.ds(1, cy, stride=2), :]
            group[kind, i, pl.ds(pl.multiple_of(all_y + gy * cy, 8), cy), :] = 0.125 * block

    for dx, i in ((1, last - EDGE), (-1, first + EDGE - 1)):
        mine = cond[i, pl.ds(0, ny), :]
        mixed = blend(cond[i - 1], cond[i], cond[i + 1], ny)
        shipped[2 + (1 - dx) // 2] = (
            RELAX_WEIGHT * source[i, pl.ds(0, ny), :] / (MASS_TERM + 6.0 * mine + mixed)
        )

        @pl.when(exists(dx, 0) & jnp.logical_not(far(dx)))
        def _():
            ship(dx).start()

    with jax.named_scope("wait_corners"):
        pl.semaphore_wait(ready_sem, n_gy - 1)
    send(REGION, (True,))
    send(SOURCE, (True,))
    coarsen(
        [cond[first + 2 * i, pl.ds(0, ny), :] + cond[first + 2 * i + 1, pl.ds(0, ny), :]
         for i in range(cx)],
        0,
    )

    row = lax.broadcasted_iota(jnp.int32, (rows, 1), 0)
    y = gy * ny + jnp.where(row < ny + HALF, row, row - rows)
    in_y = jnp.where((y >= 0) & (y < n_gy * ny), RELAX_WEIGHT, 0.0)

    def weigh(at):
        for i in at:
            mine = cond[i]
            mixed = blend(cond[i - 1], mine, cond[i + 1])
            x = gx * nx + (i - first)
            in_x = jnp.where((x >= 0) & (x < n_gx * nx), 1.0, 0.0)
            weight[i] = (in_y * in_x) / (MASS_TERM + 6.0 * mine + mixed)
            diag2[i] = MASS_TERM + 8.0 * mine + mixed

    with jax.named_scope("pace"):
        to_group(pace_sem)
        pl.semaphore_wait(pace_sem, n_gy - 1)
    send(SOURCE, (False,), True)
    for dx in (-1, 1):
        @pl.when(exists(dx, 0) & far(dx))
        def _():
            ship(dx).start()

    with jax.named_scope("wait_region_rows"):
        receive(REGION, True)
    look_up(range(first, last), (ny,))
    weigh(range(first + 1, last - 1))
    with jax.named_scope("wait_region_planes"):
        receive(REGION, False)
    edges = [*range(first - WIDE, first), *range(last, last + WIDE)]
    look_up(edges, range(0, ny, 8))
    with jax.named_scope("wait_region_corners"):
        by_neighbours(lambda a, b: wait(
            of_rows(a * b * CORNER[REGION][0] * CORNER[REGION][1]), recv_sem.at[9]
        ))
    look_up(edges, (ny,))
    weigh([first - 2, first - 1, first, last - 1, last, last + 1])
    with jax.named_scope("start_coarse_cond"):
        gather_start(0)
    def defect(i, values, flux, keep=rows):
        at = pl.ds(0, keep)
        lhs = cond[i, at] * blend(values[i - 1], values[i], values[i + 1], keep)
        rhs = blend(flux[i - 1], flux[i], flux[i + 1], keep)
        return source[i, at] - diag2[i, at] * values[i][:keep] + lhs + rhs

    values, flux, smooth = {}, {}, {}

    def first_sweep(at):
        for i in at:
            values[i] = weight[i] * source[i]
            if i in (first - EDGE, last + EDGE - 1):
                side = int(i > first)
                far = jnp.concatenate([shipped[side], jnp.zeros((8, nz), jnp.float32)])
                values[i] = jnp.where((row > 0) & (row < ny - 1), far, values[i])
            flux[i] = cond[i] * values[i]

    def second_sweep(at):
        for i in at:
            smooth[i] = values[i] + weight[i] * defect(i, values, flux)

    with jax.named_scope("wait_source_rows"):
        receive(SOURCE, True)
    first_sweep(range(first, last))
    second_sweep(range(first + 1, last - 1))
    with jax.named_scope("wait_source_planes"):
        receive(SOURCE, False)
    first_sweep((first - 2, first - 1, last, last + 1))
    second_sweep((first - 1, first, last - 1, last))
    flux = {i: cond[i] * smooth[i] for i in smooth}
    pairs = []
    for i in range(cx):
        j = first + 2 * i
        pairs.append(defect(j, smooth, flux, ny) + defect(j + 1, smooth, flux, ny))
    coarsen(pairs, 1)
    with jax.named_scope("start_coarse_res"):
        gather_start(1)
    for i in range(first, last):
        iterate[i, pl.ds(0, ny), :] = smooth[i][:ny]
    send(ITERATE)

    crow = lax.broadcasted_iota(jnp.int32, (all_y, cz), 0)
    clane = lax.broadcasted_iota(jnp.int32, (1, cz), 1)
    cz_low = jnp.where(clane == 0, 0.0, 0.5)
    cz_high = jnp.where(clane == cz - 1, 0.0, 0.5)

    def coarse_blend(planes, y_low, y_high):
        mixed = []
        for i, u in enumerate(planes):
            near = [planes[j] for j in (i - 1, i + 1) if 0 <= j < cx]
            u = u + 0.5 * functools.reduce(jnp.add, near) if near else u
            u = u + y_low * pltpu.roll(u, 1, 0) + y_high * pltpu.roll(u, all_y - 1, 0)
            mixed.append(u + cz_low * pltpu.roll(u, 1, 1) + cz_high * pltpu.roll(u, cz - 1, 1))
        return mixed

    def total(planes, c):
        whole = functools.reduce(jnp.add, [v[c * cy:(c + 1) * cy] for v in planes])
        return jnp.sum(whole, keepdims=True)

    with jax.named_scope("wait_holders"):
        by_neighbours(lambda a, b: wait(holders.at[pl.ds(0, a)], recv_sem.at[8]))
    with jax.named_scope("wait_coarse_cond"):
        gather_wait(0)
    slabs = []
    for g in range(3):
        held = [holders[g, pl.ds(c, 1), :] for c in range(n_gy)]
        same = lambda a, b: jnp.where(held[a] == held[b], 1.0, 0.0)
        y_low = jnp.where(crow == 0, 0.0, 0.5)
        y_high = jnp.where(crow == all_y - 1, 0.0, 0.5)
        for c in range(1, n_gy):
            tied = 0.5 * same(c - 1, c)
            y_low = jnp.where(crow == c * cy, tied, y_low)
            y_high = jnp.where(crow == c * cy - 1, tied, y_high)
        k = [group[0, i, pl.ds(g * all_y, all_y), :] for i in range(cx)]
        mixed = coarse_blend(k, y_low, y_high)
        diag = [MASS_TERM + 1.5 * a + 0.25 * b for a, b in zip(k, mixed)]
        step = [RELAX_WEIGHT / d for d in diag]
        ones = coarse_blend([jnp.ones((all_y, cz), jnp.float32)] * cx, y_low, y_high)
        slabs.append(dict(
            y_low=y_low, y_high=y_high, k=k, step=step,
            keep=[1.0 - s * (d + 0.5 * a) for s, d, a in zip(step, diag, k)],
            mine=[0.25 * s * a for s, a in zip(step, k)],
            theirs=[0.25 * s for s in step],
            drain=[MASS_TERM + 0.25 * a * (8.0 - b) for a, b in zip(k, ones)],
            same=[[same(a, b)[:, :1] for b in range(n_gy)] for a in range(n_gy)],
            diag_sum=[total(diag, c) for c in range(n_gy)],
        ))

    with jax.named_scope("wait_coarse_res"):
        gather_wait(1)
    e = []
    for g, s in enumerate(slabs):
        s["res"] = [group[1, i, pl.ds(g * all_y, all_y), :] for i in range(cx)]
        s["start"] = [a * b for a, b in zip(s["step"], s["res"])]
        e.append(s["start"])
    for _ in range(COARSE_SWEEPS - 1):
        for g, s in enumerate(slabs):
            straight = coarse_blend(e[g], s["y_low"], s["y_high"])
            carried = coarse_blend([a * v for a, v in zip(s["k"], e[g])], s["y_low"], s["y_high"])
            e[g] = [
                s["start"][i] + s["keep"][i] * e[g][i]
                + (s["mine"][i] * straight[i] + s["theirs"][i] * carried[i])
                for i in range(cx)
            ]
    keep_planes = ((0, cx - 1), *[(1, i) for i in range(cx)], (2, 0))
    ratios = []
    for g, s in enumerate(slabs):
        left = [r - d * v for r, d, v in zip(s["res"], s["drain"], e[g])]
        left = [total(left, c) for c in range(n_gy)]
        shares = []
        for c in range(n_gy):
            num = functools.reduce(jnp.add, [s["same"][c][b] * left[b] for b in range(n_gy)])
            den = functools.reduce(jnp.add, [s["same"][c][b] * s["diag_sum"][b] for b in range(n_gy)])
            shares.append(num / jnp.maximum(den, 1.0))
        ratios.append(shares)
    for slot, (g, i) in enumerate(keep_planes):
        whole_corr[slot, pl.ds(0, 8), :] = jnp.zeros((8, cz), jnp.float32)
        whole_corr[slot, pl.ds(8, all_y), :] = e[g][i]
        whole_corr[slot, pl.ds(8 + all_y, 8), :] = jnp.zeros((8, cz), jnp.float32)

    sub = lax.broadcasted_iota(jnp.int32, (8, nz), 0)

    def of_column(g, column):
        found = jnp.zeros((1, 1), jnp.float32)
        for c in range(n_gy):
            found = jnp.where(column == c, ratios[g][c], found)
        return jnp.broadcast_to(found, (8, nz))

    shifts = [
        (of_column(g, gy), jnp.where(sub < HALF, of_column(g, gy + 1), of_column(g, gy - 1)))
        for g in range(3)
    ]
    for i, (g, _) in enumerate(keep_planes):
        mine = whole_corr[i, pl.ds(pl.multiple_of(8 + gy * cy, 8), cy), :]
        below = whole_corr[i, pl.ds(pl.multiple_of(gy * cy, 8), 8), :]
        above = whole_corr[i, pl.ds(pl.multiple_of(8 + gy * cy + cy, 8), 8), :]
        spread[i, pl.ds(0, cy, stride=2), :] = mine
        spread[i, pl.ds(1, cy, stride=2), :] = mine
        for r in range(0, rows, 8):
            if r < ny:
                tile = spread[i, pl.ds(r, 8), :]
            else:
                tile = jnp.where(
                    sub[:, :cz] < HALF,
                    jnp.broadcast_to(above[:1], (8, cz)),
                    jnp.broadcast_to(below[7:], (8, cz)),
                )
            halves = [
                jnp.take_along_axis(tile, half_of + 64 * part, axis=1) for part in range(2)
            ]
            wide[i, pl.ds(r, 8), :] = jnp.concatenate(halves, axis=1) + shifts[g][int(r >= ny)]
    with jax.named_scope("wait_iterate_rows"):
        receive(ITERATE, True)
    with jax.named_scope("wait_iterate_planes"):
        receive(ITERATE, False)
    values = {
        i: iterate[i] + wide[(i - first + 2) // 2] for i in range(first - 2, last + 2)
    }
    for sweep in range(POST_SWEEPS):
        reach = POST_SWEEPS - 1 - sweep
        keep = rows if reach else ny
        flux = {i: cond[i] * values[i] for i in values}
        values = {
            i: values[i][:keep] + weight[i, pl.ds(0, keep)] * defect(i, values, flux, keep)
            for i in range(first - reach, last + reach)
        }
    for i in range(nx):
        out_ref[i] = values[first + i][:ny]

    with jax.named_scope("wait_sends"):
        by_neighbours(finish)


def on_device(source, region, permeability, owners, *, n_gx, n_gy):
    nx, ny, nz = source.shape
    planes = nx + 2 * WIDE
    cx, all_y, cz = nx // 2, n_gy * ny // 2, nz // 2
    f32 = jnp.float32
    return pl.pallas_call(
        functools.partial(kernel, n_gx, n_gy),
        out_shape=jax.ShapeDtypeStruct(source.shape, f32),
        in_specs=[pl.BlockSpec(memory_space=pltpu.HBM)] * 4,
        out_specs=pl.BlockSpec(memory_space=pltpu.VMEM),
        scratch_shapes=[
            pltpu.SMEM((1, n_gy), jnp.int32),
            pltpu.VMEM((1, permeability.shape[0]), f32),
            pltpu.VMEM((planes, ny + 8, nz), jnp.int32),
            pltpu.VMEM((7 * planes, ny + 8, nz), f32),
            pltpu.VMEM((4, ny, nz), f32),
            pltpu.VMEM((2, cx, 3 * all_y, cz), f32),
            pltpu.VMEM((3, 8, cz), f32),
            pltpu.VMEM((cx, ny, cz), f32),
            pltpu.VMEM((cx + 2, all_y + 16, cz), f32),
            pltpu.VMEM((cx + 2, ny, cz), f32),
            pltpu.VMEM((cx + 2, ny + 8, nz), f32),
            pltpu.SemaphoreType.DMA((4,)),
            pltpu.SemaphoreType.DMA((10,)),
            pltpu.SemaphoreType.DMA((4,)),
            pltpu.SemaphoreType.REGULAR,
            pltpu.SemaphoreType.REGULAR,
        ],
        compiler_params=pltpu.CompilerParams(
            collective_id=0, has_side_effects=True, vmem_limit_bytes=56328192
        ),
    )(*[
        pltpu.with_memory_space_constraint(a, pltpu.HBM)
        for a in (owners, permeability[None, :], source, region)
    ])


def solution(mesh):
    placed = (P("gx", "gy", None), P("gx", "gy", None), P(), P("gx", None))
    body = functools.partial(on_device, n_gx=mesh.shape["gx"], n_gy=mesh.shape["gy"])
    return jax.shard_map(
        body, mesh=mesh, in_specs=placed, out_specs=P("gx", "gy", None), check_vma=False
    )
```

```python
import functools

import jax
import jax.numpy as jnp
from jax import lax
from jax.experimental import pallas as pl
from jax.experimental.pallas import tpu as pltpu
from jax.sharding import PartitionSpec as P

POST_SWEEPS = 2
COARSE_SWEEPS = 6
RELAX_WEIGHT = 0.6
MASS_TERM = 0.1

MESH = pl.DeviceIdType.MESH
WIDE = 3
HALF = 4
REGION, SOURCE, ITERATE = 0, 1, 2
EDGE = 2
BESIDE = (2, 1, 2)
CORNER = ((3, HALF), (2, EDGE), (2, HALF))
STRIP = (3, 2)
STEPS = ((-1, -1), (1, -1), (-1, 1), (1, 1), (0, -1), (0, 1), (-1, 0), (1, 0))


def kernel(
    n_gx, n_gy,
    owners_in, table_in, source_ref, region_ref, out_ref,
    owners_ref, table_ref, labels, store, shipped, group, holders, squeezed, whole_corr, wide,
    send_sem, recv_sem, in_sem, ready_sem, pace_sem,
):
    nx, ny, nz = out_ref.shape
    cx, cy, cz = nx // 2, ny // 2, nz // 2
    first, last = WIDE, WIDE + nx
    gx, gy = lax.axis_index("gx"), lax.axis_index("gy")
    planes = nx + 2 * WIDE
    source, iterate, cond, weight, diag2 = (
        store.at[pl.ds(k * planes, planes)] for k in range(5)
    )
    fields = (labels, source, iterate)
    all_y = n_gy * cy

    def exists(dx, dy):
        x, y = gx + dx, gy + dy
        return (x >= 0) & (x < n_gx) & (y >= 0) & (y < n_gy)

    near_slabs = [
        (dx, off) for dx in (-1, 1, 0) for off in reversed(range(n_gy)) if (dx, off) != (0, 0)
    ]

    nowhere = table_ref.shape[1]
    for i in range(planes):
        if i in (0, planes - 1):
            labels[i] = jnp.full((ny + 8, nz), nowhere, jnp.int32)
        else:
            labels[i, pl.ds(ny, 8), :] = jnp.full((8, nz), nowhere, jnp.int32)

    barrier = pltpu.get_barrier_semaphore()
    count = jnp.int32(0)
    for dx, off in near_slabs:
        if dx != 0 and off != 0:
            continue
        near = exists(dx, 0)

        @pl.when(near)
        def _():
            pl.semaphore_signal(
                barrier, inc=1, device_id=(gx + dx, lax.rem(gy + off, n_gy)), device_id_type=MESH
            )

        count = count + near.astype(jnp.int32)

    load_source = pltpu.make_async_copy(
        source_ref, source.at[pl.ds(first, nx), pl.ds(0, ny)], in_sem.at[0]
    )
    load_region = pltpu.make_async_copy(
        region_ref, labels.at[pl.ds(first, nx), pl.ds(0, ny)], in_sem.at[1]
    )
    load_table = pltpu.make_async_copy(table_in, table_ref, in_sem.at[2])
    load_owners = pltpu.make_async_copy(owners_in, owners_ref, in_sem.at[3])
    load_region.start()
    load_table.start()
    load_source.start()
    load_owners.start()

    def box(kind, dx, dy):
        if dx == 0:
            w, high = nx, HALF
        elif dy == 0:
            w, high = BESIDE[kind], ny
        else:
            w, high = CORNER[kind]
        plane = nx - w if dx > 0 else 0
        land = {0: first, -1: last, 1: first - w}[dx]
        row = ny - high if dy > 0 else 0
        to = {0: 0, -1: ny, 1: ny + 8 - high}[dy]
        return (plane, w, row, high), (land, w, to, high)

    def move(kind, dx, dy, here, there):
        plane, w, row, high = here
        land, _, to, _ = there
        return pltpu.make_async_remote_copy(
            src_ref=fields[kind].at[pl.ds(first + plane, w), pl.ds(row, high)],
            dst_ref=fields[kind].at[pl.ds(land, w), pl.ds(to, high)],
            send_sem=send_sem.at[0],
            recv_sem=recv_sem.at[
                5 if kind == REGION and dx * dy else 2 * kind + abs(dx) * (kind != ITERATE)
            ],
            device_id=(gx + dx, gy + dy),
            device_id_type=MESH,
        )

    def strips(kind, dx):
        far = STRIP[kind]
        plane, land = (nx - far, first - far) if dx > 0 else (far - 1, last + far - 1)
        for row in (0, ny - EDGE):
            yield move(kind, dx, 0, (plane, 1, row, EDGE), (land, 1, row, EDGE))

    def ship(dx):
        side = (1 - dx) // 2
        return pltpu.make_async_remote_copy(
            src_ref=shipped.at[2 + side],
            dst_ref=shipped.at[side],
            send_sem=send_sem.at[0],
            recv_sem=recv_sem.at[2 * SOURCE + 1],
            device_id=(gx + dx, gy),
            device_id_type=MESH,
        )

    def far(dx):
        return lax.rem(gx + (dx + 1) // 2, 4) == 0

    def to_group(sem):
        for off in range(1, n_gy):
            pl.semaphore_signal(
                sem, inc=1, device_id=(gx, lax.rem(gy + off, n_gy)), device_id_type=MESH
            )

    def send(kind, corners=(False, True), late=None):
        for dx, dy in STEPS:
            if (dx * dy != 0) not in corners:
                continue
            now = exists(dx, dy)
            if late is not None and dx != 0:
                now = now & (far(dx) == late)
            elif late:
                continue

            @pl.when(now)
            def _():
                move(kind, dx, dy, *box(kind, dx, dy)).start()
                if dy == 0 and kind != ITERATE:
                    for strip in strips(kind, dx):
                        strip.start()

    def by_neighbours(act):
        for a in (1, 2):
            for b in (1, 2) if n_gy > 2 else (1,):
                xs = exists(-1, 0).astype(jnp.int32) + exists(1, 0).astype(jnp.int32)
                ys = exists(0, -1).astype(jnp.int32) + exists(0, 1).astype(jnp.int32)

                @pl.when((xs == a) & (ys == b))
                def _():
                    act(a, b)

    def wait(ref, sem):
        pltpu.make_async_copy(ref, ref, sem).wait()

    def of_rows(n):
        high = next(r for r in (40, 32, 24, 16, 8, HALF) if n % r == 0 and r <= store.shape[1])
        return store.at[pl.ds(0, n // high), pl.ds(0, high)]

    def beside(kind, b):
        n = BESIDE[kind] * ny + b * CORNER[kind][0] * CORNER[kind][1]
        return n + {REGION: 2 * EDGE, SOURCE: 2 * EDGE + ny, ITERATE: 0}[kind]

    def receive(kind, inner):
        def act(a, b):
            n = nx * b * HALF if inner else a * beside(kind, 0 if kind == REGION else b)
            if kind == ITERATE:
                n += nx * b * HALF
            wait(of_rows(n), recv_sem.at[2 * kind + (not inner and kind != ITERATE)])

        by_neighbours(act)

    def group_rows(a):
        return (a * n_gy + n_gy - 1) * cx * cy * cz // nz

    def finish(a, b):
        beside_x = a * sum(beside(kind, b) for kind in range(3))
        wait(of_rows(3 * nx * b * HALF + beside_x), send_sem.at[0])
        wait(of_rows(2 * group_rows(a) + 8 * a * cz // nz), send_sem.at[1])

    def gather(kind, dx, off):
        at = pl.ds(pl.multiple_of(all_y + gy * cy, 8), cy)
        to = pl.ds(pl.multiple_of((1 - dx) * all_y + gy * cy, 8), cy)
        return pltpu.make_async_remote_copy(
            src_ref=group.at[kind, :, at],
            dst_ref=group.at[kind, :, to],
            send_sem=send_sem.at[1],
            recv_sem=recv_sem.at[6 + kind],
            device_id=(gx + dx, lax.rem(gy + off, n_gy)),
            device_id_type=MESH,
        )

    def tell(dx):
        return pltpu.make_async_remote_copy(
            src_ref=holders.at[1],
            dst_ref=holders.at[1 - dx],
            send_sem=send_sem.at[1],
            recv_sem=recv_sem.at[6],
            device_id=(gx + dx, gy),
            device_id_type=MESH,
        )

    def gather_start(kind):
        for dx, off in near_slabs:
            @pl.when(exists(dx, 0))
            def _():
                gather(kind, dx, off).start()

    def gather_wait(kind):
        told = 0 if kind else 8 * cz // nz
        by_neighbours(lambda a, b: wait(
            of_rows(group_rows(a) + a * told), recv_sem.at[6 + kind]
        ))

    for dy in (-1, 1):
        @pl.when(jnp.logical_not(exists(0, -dy)))
        def _():
            at = pl.ds(ny if dy < 0 else ny + HALF, HALF)
            for ref in (source, iterate):
                ref[:, at, :] = jnp.zeros((planes, HALF, nz), jnp.float32)
    for dx in (-1, 1):
        @pl.when(jnp.logical_not(exists(-dx, 0)))
        def _():
            at = pl.ds(last if dx < 0 else 0, WIDE)
            labels[at] = jnp.full((WIDE, ny + 8, nz), nowhere, jnp.int32)
            for ref in (source, iterate):
                ref[at] = jnp.zeros((WIDE, ny + 8, nz), jnp.float32)
            shipped[(1 - dx) // 2] = jnp.zeros((ny, nz), jnp.float32)
            for kind in range(2):
                ref = group.at[kind, :, pl.ds((1 - dx) * all_y, all_y)]
                ref[...] = jnp.zeros(ref.shape, jnp.float32)
            ref = holders.at[1 - dx]
            ref[...] = jnp.zeros(ref.shape, jnp.float32)

    with jax.named_scope("wait_neighbours"):
        pl.semaphore_wait(barrier, count)
    with jax.named_scope("wait_own_region"):
        load_region.wait()
    send(REGION, (False,))
    to_group(ready_sem)
    load_source.wait()
    send(SOURCE, (False,), False)

    load_owners.wait()
    eight = lax.broadcasted_iota(jnp.int32, (8, cz), 0)
    held = jnp.zeros((8, cz), jnp.float32)
    for c in range(n_gy):
        held = jnp.where(eight == c, owners_ref[0, c].astype(jnp.float32), held)
    holders[1] = held
    for dx in (-1, 1):
        @pl.when(exists(dx, 0))
        def _():
            tell(dx).start()

    load_table.wait()
    regions = table_ref.shape[1]
    pair = jnp.concatenate([table_ref[...], jnp.zeros((1, 128 - regions), jnp.float32)], axis=1)
    table = jnp.broadcast_to(pair, (8, 128))

    def look_up(planes, tiles):
        for i in planes:
            for r in tiles:
                for c in range(0, nz, 128):
                    spot = labels[i, pl.ds(r, 8), pl.ds(c, 128)]
                    cond[i, pl.ds(r, 8), pl.ds(c, 128)] = jnp.take_along_axis(table, spot, axis=1)

    look_up(range(first, last), range(0, ny, 8))

    rows = ny + 8

    def blend(a, b, c, keep=rows):
        u = b + 0.5 * (a + c)
        u = u + 0.5 * (pltpu.roll(u, 1, 0) + pltpu.roll(u, rows - 1, 0))
        u = u[:keep]
        parts = [u[:, c:c + 128] for c in range(0, nz, 128)]
        up = [pltpu.roll(p, 1, 1) for p in parts]
        down = [pltpu.roll(p, 127, 1) for p in parts]
        mixed = []
        for j, p in enumerate(parts):
            low = jnp.where(lane128[:1] == 0, up[j - 1] if j else 0.0, up[j])
            high = jnp.where(lane128[:1] == 127, down[j + 1] if j + 1 < len(parts) else 0.0, down[j])
            mixed.append(p + 0.5 * (low + high))
        return jnp.concatenate(mixed, axis=1)

    lane128 = lax.broadcasted_iota(jnp.int32, (8, 128), 1)
    even = lax.rem(2 * lane128, jnp.int32(128))
    half_of = lane128 // 2

    def coarsen(pairs, kind):
        for i, pair_sum in enumerate(pairs):
            for r in range(0, ny, 8):
                halves = (pair_sum[r:r + 8, :128], pair_sum[r:r + 8, 128:])
                evens = [jnp.take_along_axis(h, even, axis=1) for h in halves]
                odds = [jnp.take_along_axis(h, even + 1, axis=1) for h in halves]
                squeezed[i, pl.ds(r, 8), :] = (
                    jnp.where(lane128 < 64, *evens) + jnp.where(lane128 < 64, *odds)
                )
            block = squeezed[i, pl.ds(0, cy, stride=2), :] + squeezed[i, pl.ds(1, cy, stride=2), :]
            group[kind, i, pl.ds(pl.multiple_of(all_y + gy * cy, 8), cy), :] = 0.125 * block

    for dx, i in ((1, last - EDGE), (-1, first + EDGE - 1)):
        mine = cond[i, pl.ds(0, ny), :]
        mixed = blend(cond[i - 1], cond[i], cond[i + 1], ny)
        shipped[2 + (1 - dx) // 2] = (
            RELAX_WEIGHT * source[i, pl.ds(0, ny), :] / (MASS_TERM + 6.0 * mine + mixed)
        )

        @pl.when(exists(dx, 0) & jnp.logical_not(far(dx)))
        def _():
            ship(dx).start()

    with jax.named_scope("wait_corners"):
        pl.semaphore_wait(ready_sem, n_gy - 1)
    send(REGION, (True,))
    send(SOURCE, (True,))
    coarsen(
        [cond[first + 2 * i, pl.ds(0, ny), :] + cond[first + 2 * i + 1, pl.ds(0, ny), :]
         for i in range(cx)],
        0,
    )

    row = lax.broadcasted_iota(jnp.int32, (rows, 1), 0)
    y = gy * ny + jnp.where(row < ny + HALF, row, row - rows)
    in_y = jnp.where((y >= 0) & (y < n_gy * ny), RELAX_WEIGHT, 0.0)

    def weigh(at):
        for i in at:
            mine = cond[i]
            mixed = blend(cond[i - 1], mine, cond[i + 1])
            x = gx * nx + (i - first)
            in_x = jnp.where((x >= 0) & (x < n_gx * nx), 1.0, 0.0)
            weight[i] = (in_y * in_x) / (MASS_TERM + 6.0 * mine + mixed)
            diag2[i] = MASS_TERM + 8.0 * mine + mixed

    with jax.named_scope("pace"):
        to_group(pace_sem)
        pl.semaphore_wait(pace_sem, n_gy - 1)
    send(SOURCE, (False,), True)
    for dx in (-1, 1):
        @pl.when(exists(dx, 0) & far(dx))
        def _():
            ship(dx).start()

    with jax.named_scope("wait_region_rows"):
        receive(REGION, True)
    look_up(range(first, last), (ny,))
    weigh(range(first + 1, last - 1))
    with jax.named_scope("wait_region_planes"):
        receive(REGION, False)
    edges = [*range(first - WIDE, first), *range(last, last + WIDE)]
    look_up(edges, range(0, ny, 8))
    with jax.named_scope("wait_region_corners"):
        by_neighbours(lambda a, b: wait(
            of_rows(a * b * CORNER[REGION][0] * CORNER[REGION][1]), recv_sem.at[5]
        ))
    look_up(edges, (ny,))
    weigh([first - 2, first - 1, first, last - 1, last, last + 1])
    with jax.named_scope("start_coarse_cond"):
        gather_start(0)
    def defect(i, values, flux, keep=rows):
        at = pl.ds(0, keep)
        lhs = cond[i, at] * blend(values[i - 1], values[i], values[i + 1], keep)
        rhs = blend(flux[i - 1], flux[i], flux[i + 1], keep)
        return source[i, at] - diag2[i, at] * values[i][:keep] + lhs + rhs

    values, flux, smooth = {}, {}, {}

    def first_sweep(at):
        for i in at:
            values[i] = weight[i] * source[i]
            if i in (first - EDGE, last + EDGE - 1):
                side = int(i > first)
                far = jnp.concatenate([shipped[side], jnp.zeros((8, nz), jnp.float32)])
                values[i] = jnp.where((row > 0) & (row < ny - 1), far, values[i])
            flux[i] = cond[i] * values[i]

    def second_sweep(at):
        for i in at:
            smooth[i] = values[i] + weight[i] * defect(i, values, flux)

    with jax.named_scope("wait_source_rows"):
        receive(SOURCE, True)
    first_sweep(range(first, last))
    second_sweep(range(first + 1, last - 1))
    with jax.named_scope("wait_source_planes"):
        receive(SOURCE, False)
    first_sweep((first - 2, first - 1, last, last + 1))
    second_sweep((first - 1, first, last - 1, last))
    flux = {i: cond[i] * smooth[i] for i in smooth}
    pairs = []
    for i in range(cx):
        j = first + 2 * i
        pairs.append(defect(j, smooth, flux, ny) + defect(j + 1, smooth, flux, ny))
    coarsen(pairs, 1)
    with jax.named_scope("start_coarse_res"):
        gather_start(1)
    for i in range(first, last):
        iterate[i, pl.ds(0, ny), :] = smooth[i][:ny]
    send(ITERATE)

    crow = lax.broadcasted_iota(jnp.int32, (all_y, cz), 0)
    clane = lax.broadcasted_iota(jnp.int32, (1, cz), 1)
    cz_low = jnp.where(clane == 0, 0.0, 0.5)
    cz_high = jnp.where(clane == cz - 1, 0.0, 0.5)

    def coarse_blend(planes, y_low, y_high):
        mixed = []
        for i, u in enumerate(planes):
            near = [planes[j] for j in (i - 1, i + 1) if 0 <= j < cx]
            u = u + 0.5 * functools.reduce(jnp.add, near) if near else u
            u = u + y_low * pltpu.roll(u, 1, 0) + y_high * pltpu.roll(u, all_y - 1, 0)
            mixed.append(u + cz_low * pltpu.roll(u, 1, 1) + cz_high * pltpu.roll(u, cz - 1, 1))
        return mixed

    def total(planes, c):
        whole = functools.reduce(jnp.add, [v[c * cy:(c + 1) * cy] for v in planes])
        return jnp.sum(whole, keepdims=True)

    with jax.named_scope("wait_coarse_cond"):
        gather_wait(0)
    slabs = []
    for g in range(3):
        held = [holders[g, pl.ds(c, 1), :] for c in range(n_gy)]
        same = lambda a, b: jnp.where(held[a] == held[b], 1.0, 0.0)
        y_low = jnp.where(crow == 0, 0.0, 0.5)
        y_high = jnp.where(crow == all_y - 1, 0.0, 0.5)
        for c in range(1, n_gy):
            tied = 0.5 * same(c - 1, c)
            y_low = jnp.where(crow == c * cy, tied, y_low)
            y_high = jnp.where(crow == c * cy - 1, tied, y_high)
        k = [group[0, i, pl.ds(g * all_y, all_y), :] for i in range(cx)]
        mixed = coarse_blend(k, y_low, y_high)
        diag = [MASS_TERM + 1.5 * a + 0.25 * b for a, b in zip(k, mixed)]
        step = [RELAX_WEIGHT / d for d in diag]
        ones = coarse_blend([jnp.ones((all_y, cz), jnp.float32)] * cx, y_low, y_high)
        slabs.append(dict(
            y_low=y_low, y_high=y_high, k=k, step=step,
            keep=[1.0 - s * (d + 0.5 * a) for s, d, a in zip(step, diag, k)],
            mine=[0.25 * s * a for s, a in zip(step, k)],
            theirs=[0.25 * s for s in step],
            drain=[MASS_TERM + 0.25 * a * (8.0 - b) for a, b in zip(k, ones)],
            same=[[same(a, b)[:, :1] for b in range(n_gy)] for a in range(n_gy)],
        ))
        s = slabs[-1]
        diag_sum = [total(diag, c) for c in range(n_gy)]
        for line in s["same"]:
            den = functools.reduce(jnp.add, [a * d for a, d in zip(line, diag_sum)])
            line[:] = [a / jnp.maximum(den, 1.0) for a in line]

    with jax.named_scope("wait_coarse_res"):
        gather_wait(1)
    e = []
    for g, s in enumerate(slabs):
        s["res"] = [group[1, i, pl.ds(g * all_y, all_y), :] for i in range(cx)]
        s["start"] = [a * b for a, b in zip(s["step"], s["res"])]
        e.append(s["start"])
    for _ in range(COARSE_SWEEPS - 1):
        for g, s in enumerate(slabs):
            straight = coarse_blend(e[g], s["y_low"], s["y_high"])
            carried = coarse_blend([a * v for a, v in zip(s["k"], e[g])], s["y_low"], s["y_high"])
            e[g] = [
                s["start"][i] + s["keep"][i] * e[g][i]
                + (s["mine"][i] * straight[i] + s["theirs"][i] * carried[i])
                for i in range(cx)
            ]
    keep_planes = ((0, cx - 1), *[(1, i) for i in range(cx)], (2, 0))
    ratios = []
    for g, s in enumerate(slabs):
        left = [r - d * v for r, d, v in zip(s["res"], s["drain"], e[g])]
        left = [total(left, c) for c in range(n_gy)]
        shares = []
        for c in range(n_gy):
            num = functools.reduce(jnp.add, [s["same"][c][b] * left[b] for b in range(n_gy)])
            shares.append(num)
        ratios.append(shares)
    for slot, (g, i) in enumerate(keep_planes):
        whole_corr[slot, pl.ds(0, 8), :] = jnp.zeros((8, cz), jnp.float32)
        whole_corr[slot, pl.ds(8, all_y), :] = e[g][i]
        whole_corr[slot, pl.ds(8 + all_y, 8), :] = jnp.zeros((8, cz), jnp.float32)

    sub = lax.broadcasted_iota(jnp.int32, (8, nz), 0)

    def of_column(g, column):
        found = jnp.zeros((1, 1), jnp.float32)
        for c in range(n_gy):
            found = jnp.where(column == c, ratios[g][c], found)
        return jnp.broadcast_to(found, (8, nz))

    shifts = [
        (of_column(g, gy), jnp.where(sub < HALF, of_column(g, gy + 1), of_column(g, gy - 1)))
        for g in range(3)
    ]
    for i, (g, _) in enumerate(keep_planes):
        mine = whole_corr[i, pl.ds(pl.multiple_of(8 + gy * cy, 8), cy), :]
        below = whole_corr[i, pl.ds(pl.multiple_of(gy * cy, 8), 8), :]
        above = whole_corr[i, pl.ds(pl.multiple_of(8 + gy * cy + cy, 8), 8), :]
        outer = jnp.where(
            sub[:, :cz] < HALF,
            jnp.broadcast_to(above[:1], (8, cz)),
            jnp.broadcast_to(below[7:], (8, cz)),
        )
        for part in range(2):
            at = half_of + 64 * part
            for r in range(0, cy, 8):
                tile = jnp.take_along_axis(mine[r:r + 8], at, axis=1) + shifts[g][0][:, :128]
                wide[i, part, pl.ds(2 * r, 8, stride=2), :] = tile
                wide[i, part, pl.ds(2 * r + 1, 8, stride=2), :] = tile
            wide[i, part, pl.ds(ny, 8), :] = (
                jnp.take_along_axis(outer, at, axis=1) + shifts[g][1][:, :128]
            )
    with jax.named_scope("wait_iterate_planes"):
        receive(ITERATE, False)
    values = {
        i: iterate[i] + jnp.concatenate([wide[(i - first + 2) // 2, part] for part in range(2)], axis=1)
        for i in range(first - 2, last + 2)
    }
    for sweep in range(POST_SWEEPS):
        reach = POST_SWEEPS - 1 - sweep
        keep = rows if reach else ny
        flux = {i: cond[i] * values[i] for i in values}
        values = {
            i: values[i][:keep] + weight[i, pl.ds(0, keep)] * defect(i, values, flux, keep)
            for i in range(first - reach, last + reach)
        }
    for i in range(nx):
        out_ref[i] = values[first + i][:ny]

    with jax.named_scope("wait_sends"):
        by_neighbours(finish)


def on_device(source, region, permeability, owners, *, n_gx, n_gy):
    nx, ny, nz = source.shape
    planes = nx + 2 * WIDE
    cx, all_y, cz = nx // 2, n_gy * ny // 2, nz // 2
    f32 = jnp.float32
    return pl.pallas_call(
        functools.partial(kernel, n_gx, n_gy),
        out_shape=jax.ShapeDtypeStruct(source.shape, f32),
        in_specs=[pl.BlockSpec(memory_space=pltpu.HBM)] * 4,
        out_specs=pl.BlockSpec(memory_space=pltpu.VMEM),
        scratch_shapes=[
            pltpu.SMEM((1, n_gy), jnp.int32),
            pltpu.VMEM((1, permeability.shape[0]), f32),
            pltpu.VMEM((planes, ny + 8, nz), jnp.int32),
            pltpu.VMEM((8 * planes, ny + 8, nz), f32),
            pltpu.VMEM((4, ny, nz), f32),
            pltpu.VMEM((2, cx, 3 * all_y, cz), f32),
            pltpu.VMEM((3, 8, cz), f32),
            pltpu.VMEM((cx, ny, cz), f32),
            pltpu.VMEM((cx + 2, all_y + 16, cz), f32),
            pltpu.VMEM((cx + 2, 2, ny + 8, cz), f32),
            pltpu.SemaphoreType.DMA((2,)),
            pltpu.SemaphoreType.DMA((8,)),
            pltpu.SemaphoreType.DMA((4,)),
            pltpu.SemaphoreType.REGULAR,
            pltpu.SemaphoreType.REGULAR,
        ],
        compiler_params=pltpu.CompilerParams(
            collective_id=0, has_side_effects=True, vmem_limit_bytes=56328192
        ),
    )(*[
        pltpu.with_memory_space_constraint(a, pltpu.HBM)
        for a in (owners, permeability[None, :], source, region)
    ])


def solution(mesh):
    placed = (P("gx", "gy", None), P("gx", "gy", None), P(), P("gx", None))
    body = functools.partial(on_device, n_gx=mesh.shape["gx"], n_gy=mesh.shape["gy"])
    return jax.shard_map(
        body, mesh=mesh, in_specs=placed, out_specs=P("gx", "gy", None), check_vma=False
    )
```

```python
import functools

import jax
import jax.numpy as jnp
from jax import lax
from jax.experimental import pallas as pl
from jax.experimental.pallas import tpu as pltpu
from jax.sharding import PartitionSpec as P

POST_SWEEPS = 2
COARSE_SWEEPS = 6
RELAX_WEIGHT = 0.6
MASS_TERM = 0.1

MESH = pl.DeviceIdType.MESH
WIDE = 3
HALF = 4
REGION, SOURCE, ITERATE = 0, 1, 2
EDGE = 2
BESIDE = (2, 1, 2)
CORNER = ((3, HALF), (2, EDGE), (2, HALF))
STRIP = (3, 2)
STEPS = ((-1, -1), (1, -1), (-1, 1), (1, 1), (0, -1), (0, 1), (-1, 0), (1, 0))


def kernel(
    n_gx, n_gy,
    owners_in, table_in, source_ref, region_ref, out_ref,
    owners_ref, table_ref, labels, store, shipped, group, holders, squeezed, whole_corr, wide,
    send_sem, recv_sem, in_sem, ready_sem, pace_sem,
):
    nx, ny, nz = out_ref.shape
    cx, cy, cz = nx // 2, ny // 2, nz // 2
    first, last = WIDE, WIDE + nx
    gx, gy = lax.axis_index("gx"), lax.axis_index("gy")
    planes = nx + 2 * WIDE
    source, iterate, cond, weight, diag2 = (
        store.at[pl.ds(k * planes, planes)] for k in range(5)
    )
    fields = (labels, source, iterate)
    all_y = n_gy * cy

    def exists(dx, dy):
        x, y = gx + dx, gy + dy
        return (x >= 0) & (x < n_gx) & (y >= 0) & (y < n_gy)

    near_slabs = [
        (dx, off) for off in reversed(range(n_gy)) for dx in (-1, 1, 0) if (dx, off) != (0, 0)
    ]

    nowhere = table_ref.shape[1]
    for i in range(planes):
        if i in (0, planes - 1):
            labels[i] = jnp.full((ny + 8, nz), nowhere, jnp.int32)
        else:
            labels[i, pl.ds(ny, 8), :] = jnp.full((8, nz), nowhere, jnp.int32)

    barrier = pltpu.get_barrier_semaphore()
    count = jnp.int32(0)
    for dx, off in near_slabs:
        if dx != 0 and off != 0:
            continue
        near = exists(dx, 0)

        @pl.when(near)
        def _():
            pl.semaphore_signal(
                barrier, inc=1, device_id=(gx + dx, lax.rem(gy + off, n_gy)), device_id_type=MESH
            )

        count = count + near.astype(jnp.int32)

    load_source = pltpu.make_async_copy(
        source_ref, source.at[pl.ds(first, nx), pl.ds(0, ny)], in_sem.at[0]
    )
    load_region = pltpu.make_async_copy(
        region_ref, labels.at[pl.ds(first, nx), pl.ds(0, ny)], in_sem.at[1]
    )
    load_table = pltpu.make_async_copy(table_in, table_ref, in_sem.at[2])
    load_owners = pltpu.make_async_copy(owners_in, owners_ref, in_sem.at[3])
    load_region.start()
    load_table.start()
    load_source.start()
    load_owners.start()

    def box(kind, dx, dy):
        if dx == 0:
            w, high = nx, HALF
        elif dy == 0:
            w, high = BESIDE[kind], ny
        else:
            w, high = CORNER[kind]
        plane = nx - w if dx > 0 else 0
        land = {0: first, -1: last, 1: first - w}[dx]
        row = ny - high if dy > 0 else 0
        to = {0: 0, -1: ny, 1: ny + 8 - high}[dy]
        return (plane, w, row, high), (land, w, to, high)

    def move(kind, dx, dy, here, there):
        plane, w, row, high = here
        land, _, to, _ = there
        return pltpu.make_async_remote_copy(
            src_ref=fields[kind].at[pl.ds(first + plane, w), pl.ds(row, high)],
            dst_ref=fields[kind].at[pl.ds(land, w), pl.ds(to, high)],
            send_sem=send_sem.at[0],
            recv_sem=recv_sem.at[
                5 if kind == REGION and dx * dy else 2 * kind + abs(dx) * (kind != ITERATE)
            ],
            device_id=(gx + dx, gy + dy),
            device_id_type=MESH,
        )

    def strips(kind, dx):
        far = STRIP[kind]
        plane, land = (nx - far, first - far) if dx > 0 else (far - 1, last + far - 1)
        for row in (0, ny - EDGE):
            yield move(kind, dx, 0, (plane, 1, row, EDGE), (land, 1, row, EDGE))

    def ship(dx):
        side = (1 - dx) // 2
        return pltpu.make_async_remote_copy(
            src_ref=shipped.at[2 + side],
            dst_ref=shipped.at[side],
            send_sem=send_sem.at[0],
            recv_sem=recv_sem.at[2 * SOURCE + 1],
            device_id=(gx + dx, gy),
            device_id_type=MESH,
        )

    def far(dx):
        return lax.rem(gx + (dx + 1) // 2, 4) == 0

    def to_group(sem):
        for off in range(1, n_gy):
            pl.semaphore_signal(
                sem, inc=1, device_id=(gx, lax.rem(gy + off, n_gy)), device_id_type=MESH
            )

    def send(kind, corners=(False, True), late=None):
        for dx, dy in STEPS:
            if (dx * dy != 0) not in corners:
                continue
            now = exists(dx, dy)
            if late is not None and dx != 0:
                now = now & (far(dx) == late)
            elif late:
                continue

            @pl.when(now)
            def _():
                move(kind, dx, dy, *box(kind, dx, dy)).start()
                if dy == 0 and kind != ITERATE:
                    for strip in strips(kind, dx):
                        strip.start()

    def by_neighbours(act):
        for a in (1, 2):
            for b in (1, 2) if n_gy > 2 else (1,):
                xs = exists(-1, 0).astype(jnp.int32) + exists(1, 0).astype(jnp.int32)
                ys = exists(0, -1).astype(jnp.int32) + exists(0, 1).astype(jnp.int32)

                @pl.when((xs == a) & (ys == b))
                def _():
                    act(a, b)

    def wait(ref, sem):
        pltpu.make_async_copy(ref, ref, sem).wait()

    def of_rows(n):
        high = next(r for r in (40, 32, 24, 16, 8, HALF) if n % r == 0 and r <= store.shape[1])
        return store.at[pl.ds(0, n // high), pl.ds(0, high)]

    def beside(kind, b):
        n = BESIDE[kind] * ny + b * CORNER[kind][0] * CORNER[kind][1]
        return n + {REGION: 2 * EDGE, SOURCE: 2 * EDGE + ny, ITERATE: 0}[kind]

    def receive(kind, inner):
        def act(a, b):
            n = nx * b * HALF if inner else a * beside(kind, 0 if kind == REGION else b)
            if kind == ITERATE:
                n += nx * b * HALF
            wait(of_rows(n), recv_sem.at[2 * kind + (not inner and kind != ITERATE)])

        by_neighbours(act)

    def group_rows(a):
        return (a * n_gy + n_gy - 1) * cx * cy * cz // nz

    def finish(a, b):
        beside_x = a * sum(beside(kind, b) for kind in range(3))
        wait(of_rows(3 * nx * b * HALF + beside_x), send_sem.at[0])
        wait(of_rows(2 * group_rows(a) + 8 * a * cz // nz), send_sem.at[1])

    def gather(kind, dx, off):
        at = pl.ds(pl.multiple_of(all_y + gy * cy, 8), cy)
        to = pl.ds(pl.multiple_of((1 - dx) * all_y + gy * cy, 8), cy)
        return pltpu.make_async_remote_copy(
            src_ref=group.at[kind, :, at],
            dst_ref=group.at[kind, :, to],
            send_sem=send_sem.at[1],
            recv_sem=recv_sem.at[6 + kind],
            device_id=(gx + dx, lax.rem(gy + off, n_gy)),
            device_id_type=MESH,
        )

    def tell(dx):
        return pltpu.make_async_remote_copy(
            src_ref=holders.at[1],
            dst_ref=holders.at[1 - dx],
            send_sem=send_sem.at[1],
            recv_sem=recv_sem.at[6],
            device_id=(gx + dx, gy),
            device_id_type=MESH,
        )

    def gather_start(kind):
        for dx, off in near_slabs:
            if not dx:
                gather(kind, dx, off).start()
        for dx, off in near_slabs:
            if dx:
                @pl.when(exists(dx, 0) & far(dx))
                def _():
                    gather(kind, dx, off).start()
        for dx, off in near_slabs:
            if dx:
                @pl.when(exists(dx, 0) & jnp.logical_not(far(dx)))
                def _():
                    gather(kind, dx, off).start()

    def gather_wait(kind):
        told = 0 if kind else 8 * cz // nz
        by_neighbours(lambda a, b: wait(
            of_rows(group_rows(a) + a * told), recv_sem.at[6 + kind]
        ))

    for dy in (-1, 1):
        @pl.when(jnp.logical_not(exists(0, -dy)))
        def _():
            at = pl.ds(ny if dy < 0 else ny + HALF, HALF)
            for ref in (source, iterate):
                ref[:, at, :] = jnp.zeros((planes, HALF, nz), jnp.float32)
    for dx in (-1, 1):
        @pl.when(jnp.logical_not(exists(-dx, 0)))
        def _():
            at = pl.ds(last if dx < 0 else 0, WIDE)
            labels[at] = jnp.full((WIDE, ny + 8, nz), nowhere, jnp.int32)
            for ref in (source, iterate):
                ref[at] = jnp.zeros((WIDE, ny + 8, nz), jnp.float32)
            shipped[(1 - dx) // 2] = jnp.zeros((ny, nz), jnp.float32)
            for kind in range(2):
                ref = group.at[kind, :, pl.ds((1 - dx) * all_y, all_y)]
                ref[...] = jnp.zeros(ref.shape, jnp.float32)
            ref = holders.at[1 - dx]
            ref[...] = jnp.zeros(ref.shape, jnp.float32)

    with jax.named_scope("wait_neighbours"):
        pl.semaphore_wait(barrier, count)
    with jax.named_scope("wait_own_region"):
        load_region.wait()
    send(REGION, (False,))
    to_group(ready_sem)
    load_source.wait()
    send(SOURCE, (False,), False)

    load_owners.wait()
    eight = lax.broadcasted_iota(jnp.int32, (8, cz), 0)
    held = jnp.zeros((8, cz), jnp.float32)
    for c in range(n_gy):
        held = jnp.where(eight == c, owners_ref[0, c].astype(jnp.float32), held)
    holders[1] = held
    for dx in (-1, 1):
        @pl.when(exists(dx, 0))
        def _():
            tell(dx).start()

    load_table.wait()
    regions = table_ref.shape[1]
    pair = jnp.concatenate([table_ref[...], jnp.zeros((1, 128 - regions), jnp.float32)], axis=1)
    table = jnp.broadcast_to(pair, (8, 128))

    def look_up(planes, tiles):
        for i in planes:
            for r in tiles:
                for c in range(0, nz, 128):
                    spot = labels[i, pl.ds(r, 8), pl.ds(c, 128)]
                    cond[i, pl.ds(r, 8), pl.ds(c, 128)] = jnp.take_along_axis(table, spot, axis=1)

    look_up(range(first, last), range(0, ny, 8))

    rows = ny + 8

    def blend(a, b, c, keep=rows):
        u = b + 0.5 * (a + c)
        u = u + 0.5 * (pltpu.roll(u, 1, 0) + pltpu.roll(u, rows - 1, 0))
        u = u[:keep]
        parts = [u[:, c:c + 128] for c in range(0, nz, 128)]
        up = [pltpu.roll(p, 1, 1) for p in parts]
        down = [pltpu.roll(p, 127, 1) for p in parts]
        mixed = []
        for j, p in enumerate(parts):
            low = jnp.where(lane128[:1] == 0, up[j - 1] if j else 0.0, up[j])
            high = jnp.where(lane128[:1] == 127, down[j + 1] if j + 1 < len(parts) else 0.0, down[j])
            mixed.append(p + 0.5 * (low + high))
        return jnp.concatenate(mixed, axis=1)

    lane128 = lax.broadcasted_iota(jnp.int32, (8, 128), 1)
    even = lax.rem(2 * lane128, jnp.int32(128))
    half_of = lane128 // 2

    def coarsen(pairs, kind):
        for i, pair_sum in enumerate(pairs):
            for r in range(0, ny, 8):
                halves = (pair_sum[r:r + 8, :128], pair_sum[r:r + 8, 128:])
                evens = [jnp.take_along_axis(h, even, axis=1) for h in halves]
                odds = [jnp.take_along_axis(h, even + 1, axis=1) for h in halves]
                squeezed[i, pl.ds(r, 8), :] = (
                    jnp.where(lane128 < 64, *evens) + jnp.where(lane128 < 64, *odds)
                )
            block = squeezed[i, pl.ds(0, cy, stride=2), :] + squeezed[i, pl.ds(1, cy, stride=2), :]
            group[kind, i, pl.ds(pl.multiple_of(all_y + gy * cy, 8), cy), :] = 0.125 * block

    for dx, i in ((1, last - EDGE), (-1, first + EDGE - 1)):
        mine = cond[i, pl.ds(0, ny), :]
        mixed = blend(cond[i - 1], cond[i], cond[i + 1], ny)
        shipped[2 + (1 - dx) // 2] = (
            RELAX_WEIGHT * source[i, pl.ds(0, ny), :] / (MASS_TERM + 6.0 * mine + mixed)
        )

        @pl.when(exists(dx, 0) & jnp.logical_not(far(dx)))
        def _():
            ship(dx).start()

    with jax.named_scope("wait_corners"):
        pl.semaphore_wait(ready_sem, n_gy - 1)
    send(REGION, (True,))
    send(SOURCE, (True,))
    coarsen(
        [cond[first + 2 * i, pl.ds(0, ny), :] + cond[first + 2 * i + 1, pl.ds(0, ny), :]
         for i in range(cx)],
        0,
    )

    row = lax.broadcasted_iota(jnp.int32, (rows, 1), 0)
    y = gy * ny + jnp.where(row < ny + HALF, row, row - rows)
    in_y = jnp.where((y >= 0) & (y < n_gy * ny), RELAX_WEIGHT, 0.0)

    def weigh(at):
        for i in at:
            mine = cond[i]
            mixed = blend(cond[i - 1], mine, cond[i + 1])
            x = gx * nx + (i - first)
            in_x = jnp.where((x >= 0) & (x < n_gx * nx), 1.0, 0.0)
            weight[i] = (in_y * in_x) / (MASS_TERM + 6.0 * mine + mixed)
            diag2[i] = MASS_TERM + 8.0 * mine + mixed

    with jax.named_scope("pace"):
        to_group(pace_sem)
        pl.semaphore_wait(pace_sem, n_gy - 1)
    send(SOURCE, (False,), True)
    for dx in (-1, 1):
        @pl.when(exists(dx, 0) & far(dx))
        def _():
            ship(dx).start()

    with jax.named_scope("wait_region_rows"):
        receive(REGION, True)
    look_up(range(first, last), (ny,))
    weigh(range(first + 1, last - 1))
    with jax.named_scope("wait_region_planes"):
        receive(REGION, False)
    edges = [*range(first - WIDE, first), *range(last, last + WIDE)]
    look_up(edges, range(0, ny, 8))
    with jax.named_scope("wait_region_corners"):
        by_neighbours(lambda a, b: wait(
            of_rows(a * b * CORNER[REGION][0] * CORNER[REGION][1]), recv_sem.at[5]
        ))
    look_up(edges, (ny,))
    weigh([first - 2, first - 1, first, last - 1, last, last + 1])
    with jax.named_scope("start_coarse_cond"):
        gather_start(0)
    def defect(i, values, flux, keep=rows):
        at = pl.ds(0, keep)
        lhs = cond[i, at] * blend(values[i - 1], values[i], values[i + 1], keep)
        rhs = blend(flux[i - 1], flux[i], flux[i + 1], keep)
        return source[i, at] - diag2[i, at] * values[i][:keep] + lhs + rhs

    values, flux, smooth = {}, {}, {}

    def first_sweep(at):
        for i in at:
            values[i] = weight[i] * source[i]
            if i in (first - EDGE, last + EDGE - 1):
                side = int(i > first)
                far = jnp.concatenate([shipped[side], jnp.zeros((8, nz), jnp.float32)])
                values[i] = jnp.where((row > 0) & (row < ny - 1), far, values[i])
            flux[i] = cond[i] * values[i]

    def second_sweep(at):
        for i in at:
            smooth[i] = values[i] + weight[i] * defect(i, values, flux)

    with jax.named_scope("wait_source_rows"):
        receive(SOURCE, True)
    first_sweep(range(first, last))
    second_sweep(range(first + 1, last - 1))
    with jax.named_scope("wait_source_planes"):
        receive(SOURCE, False)
    first_sweep((first - 2, first - 1, last, last + 1))
    second_sweep((first - 1, first, last - 1, last))
    flux = {i: cond[i] * smooth[i] for i in smooth}
    pairs = []
    for i in range(cx):
        j = first + 2 * i
        pairs.append(defect(j, smooth, flux, ny) + defect(j + 1, smooth, flux, ny))
    coarsen(pairs, 1)
    with jax.named_scope("start_coarse_res"):
        gather_start(1)
    for i in range(first, last):
        iterate[i, pl.ds(0, ny), :] = smooth[i][:ny]
    send(ITERATE)

    crow = lax.broadcasted_iota(jnp.int32, (all_y, cz), 0)
    clane = lax.broadcasted_iota(jnp.int32, (1, cz), 1)
    cz_low = jnp.where(clane == 0, 0.0, 0.5)
    cz_high = jnp.where(clane == cz - 1, 0.0, 0.5)

    def coarse_blend(planes, y_low, y_high):
        mixed = []
        for i, u in enumerate(planes):
            near = [planes[j] for j in (i - 1, i + 1) if 0 <= j < cx]
            u = u + 0.5 * functools.reduce(jnp.add, near) if near else u
            u = u + y_low * pltpu.roll(u, 1, 0) + y_high * pltpu.roll(u, all_y - 1, 0)
            mixed.append(u + cz_low * pltpu.roll(u, 1, 1) + cz_high * pltpu.roll(u, cz - 1, 1))
        return mixed

    def total(planes, c):
        whole = functools.reduce(jnp.add, [v[c * cy:(c + 1) * cy] for v in planes])
        return jnp.sum(whole, keepdims=True)

    with jax.named_scope("wait_coarse_cond"):
        gather_wait(0)
    slabs = []
    for g in range(3):
        held = [holders[g, pl.ds(c, 1), :] for c in range(n_gy)]
        same = lambda a, b: jnp.where(held[a] == held[b], 1.0, 0.0)
        y_low = jnp.where(crow == 0, 0.0, 0.5)
        y_high = jnp.where(crow == all_y - 1, 0.0, 0.5)
        for c in range(1, n_gy):
            tied = 0.5 * same(c - 1, c)
            y_low = jnp.where(crow == c * cy, tied, y_low)
            y_high = jnp.where(crow == c * cy - 1, tied, y_high)
        k = [group[0, i, pl.ds(g * all_y, all_y), :] for i in range(cx)]
        mixed = coarse_blend(k, y_low, y_high)
        diag = [MASS_TERM + 1.5 * a + 0.25 * b for a, b in zip(k, mixed)]
        step = [RELAX_WEIGHT / d for d in diag]
        ones = coarse_blend([jnp.ones((all_y, cz), jnp.float32)] * cx, y_low, y_high)
        slabs.append(dict(
            y_low=y_low, y_high=y_high, k=k, step=step,
            keep=[1.0 - s * (d + 0.5 * a) for s, d, a in zip(step, diag, k)],
            mine=[0.25 * s * a for s, a in zip(step, k)],
            theirs=[0.25 * s for s in step],
            drain=[MASS_TERM + 0.25 * a * (8.0 - b) for a, b in zip(k, ones)],
            same=[[same(a, b)[:, :1] for b in range(n_gy)] for a in range(n_gy)],
        ))
        s = slabs[-1]
        diag_sum = [total(diag, c) for c in range(n_gy)]
        for line in s["same"]:
            den = functools.reduce(jnp.add, [a * d for a, d in zip(line, diag_sum)])
            line[:] = [a / jnp.maximum(den, 1.0) for a in line]

    with jax.named_scope("wait_coarse_res"):
        gather_wait(1)
    e = []
    for g, s in enumerate(slabs):
        s["res"] = [group[1, i, pl.ds(g * all_y, all_y), :] for i in range(cx)]
        s["start"] = [a * b for a, b in zip(s["step"], s["res"])]
        e.append(s["start"])
    for _ in range(COARSE_SWEEPS - 1):
        for g, s in enumerate(slabs):
            straight = coarse_blend(e[g], s["y_low"], s["y_high"])
            carried = coarse_blend([a * v for a, v in zip(s["k"], e[g])], s["y_low"], s["y_high"])
            e[g] = [
                s["start"][i] + s["keep"][i] * e[g][i]
                + (s["mine"][i] * straight[i] + s["theirs"][i] * carried[i])
                for i in range(cx)
            ]
    keep_planes = ((0, cx - 1), *[(1, i) for i in range(cx)], (2, 0))
    ratios = []
    for g, s in enumerate(slabs):
        left = [r - d * v for r, d, v in zip(s["res"], s["drain"], e[g])]
        left = [total(left, c) for c in range(n_gy)]
        shares = []
        for c in range(n_gy):
            num = functools.reduce(jnp.add, [s["same"][c][b] * left[b] for b in range(n_gy)])
            shares.append(num)
        ratios.append(shares)
    for slot, (g, i) in enumerate(keep_planes):
        whole_corr[slot, pl.ds(0, 8), :] = jnp.zeros((8, cz), jnp.float32)
        whole_corr[slot, pl.ds(8, all_y), :] = e[g][i]
        whole_corr[slot, pl.ds(8 + all_y, 8), :] = jnp.zeros((8, cz), jnp.float32)

    sub = lax.broadcasted_iota(jnp.int32, (8, nz), 0)

    def of_column(g, column):
        found = jnp.zeros((1, 1), jnp.float32)
        for c in range(n_gy):
            found = jnp.where(column == c, ratios[g][c], found)
        return jnp.broadcast_to(found, (8, nz))

    shifts = [
        (of_column(g, gy), jnp.where(sub < HALF, of_column(g, gy + 1), of_column(g, gy - 1)))
        for g in range(3)
    ]
    for i, (g, _) in enumerate(keep_planes):
        mine = whole_corr[i, pl.ds(pl.multiple_of(8 + gy * cy, 8), cy), :]
        below = whole_corr[i, pl.ds(pl.multiple_of(gy * cy, 8), 8), :]
        above = whole_corr[i, pl.ds(pl.multiple_of(8 + gy * cy + cy, 8), 8), :]
        outer = jnp.where(
            sub[:, :cz] < HALF,
            jnp.broadcast_to(above[:1], (8, cz)),
            jnp.broadcast_to(below[7:], (8, cz)),
        )
        for part in range(2):
            at = half_of + 64 * part
            for r in range(0, cy, 8):
                tile = jnp.take_along_axis(mine[r:r + 8], at, axis=1) + shifts[g][0][:, :128]
                wide[i, part, pl.ds(2 * r, 8, stride=2), :] = tile
                wide[i, part, pl.ds(2 * r + 1, 8, stride=2), :] = tile
            wide[i, part, pl.ds(ny, 8), :] = (
                jnp.take_along_axis(outer, at, axis=1) + shifts[g][1][:, :128]
            )
    with jax.named_scope("wait_iterate_planes"):
        receive(ITERATE, False)
    values = {
        i: iterate[i] + jnp.concatenate([wide[(i - first + 2) // 2, part] for part in range(2)], axis=1)
        for i in range(first - 2, last + 2)
    }
    for sweep in range(POST_SWEEPS):
        reach = POST_SWEEPS - 1 - sweep
        keep = rows if reach else ny
        flux = {i: cond[i] * values[i] for i in values}
        values = {
            i: values[i][:keep] + weight[i, pl.ds(0, keep)] * defect(i, values, flux, keep)
            for i in range(first - reach, last + reach)
        }
    for i in range(nx):
        out_ref[i] = values[first + i][:ny]

    with jax.named_scope("wait_sends"):
        by_neighbours(finish)


def on_device(source, region, permeability, owners, *, n_gx, n_gy):
    nx, ny, nz = source.shape
    planes = nx + 2 * WIDE
    cx, all_y, cz = nx // 2, n_gy * ny // 2, nz // 2
    f32 = jnp.float32
    return pl.pallas_call(
        functools.partial(kernel, n_gx, n_gy),
        out_shape=jax.ShapeDtypeStruct(source.shape, f32),
        in_specs=[pl.BlockSpec(memory_space=pltpu.HBM)] * 4,
        out_specs=pl.BlockSpec(memory_space=pltpu.VMEM),
        scratch_shapes=[
            pltpu.SMEM((1, n_gy), jnp.int32),
            pltpu.VMEM((1, permeability.shape[0]), f32),
            pltpu.VMEM((planes, ny + 8, nz), jnp.int32),
            pltpu.VMEM((8 * planes, ny + 8, nz), f32),
            pltpu.VMEM((4, ny, nz), f32),
            pltpu.VMEM((2, cx, 3 * all_y, cz), f32),
            pltpu.VMEM((3, 8, cz), f32),
            pltpu.VMEM((cx, ny, cz), f32),
            pltpu.VMEM((cx + 2, all_y + 16, cz), f32),
            pltpu.VMEM((cx + 2, 2, ny + 8, cz), f32),
            pltpu.SemaphoreType.DMA((2,)),
            pltpu.SemaphoreType.DMA((8,)),
            pltpu.SemaphoreType.DMA((4,)),
            pltpu.SemaphoreType.REGULAR,
            pltpu.SemaphoreType.REGULAR,
        ],
        compiler_params=pltpu.CompilerParams(
            collective_id=0, has_side_effects=True, vmem_limit_bytes=56328192
        ),
    )(*[
        pltpu.with_memory_space_constraint(a, pltpu.HBM)
        for a in (owners, permeability[None, :], source, region)
    ])


def solution(mesh):
    placed = (P("gx", "gy", None), P("gx", "gy", None), P(), P("gx", None))
    body = functools.partial(on_device, n_gx=mesh.shape["gx"], n_gy=mesh.shape["gy"])
    return jax.shard_map(
        body, mesh=mesh, in_specs=placed, out_specs=P("gx", "gy", None), check_vma=False
    )
```

```python
import functools

import jax
import jax.numpy as jnp
from jax import lax
from jax.experimental import pallas as pl
from jax.experimental.pallas import tpu as pltpu
from jax.sharding import PartitionSpec as P

POST_SWEEPS = 2
COARSE_SWEEPS = 6
RELAX_WEIGHT = 0.6
MASS_TERM = 0.1

MESH = pl.DeviceIdType.MESH
WIDE = 3
HALF = 4
REGION, SOURCE, ITERATE = 0, 1, 2
EDGE = 2
BESIDE = (2, 1, 2)
CORNER = ((3, HALF), (2, EDGE), (2, HALF))
STRIP = (3, 2)
STEPS = ((-1, -1), (1, -1), (-1, 1), (1, 1), (0, -1), (0, 1), (-1, 0), (1, 0))


def kernel(
    n_gx, n_gy,
    owners_in, table_in, source_ref, region_ref, out_ref,
    owners_ref, table_ref, labels, store, shipped, group, holders, squeezed, whole_corr, wide,
    send_sem, recv_sem, in_sem, ready_sem, pace_sem,
):
    nx, ny, nz = out_ref.shape
    cx, cy, cz = nx // 2, ny // 2, nz // 2
    first, last = WIDE, WIDE + nx
    gx, gy = lax.axis_index("gx"), lax.axis_index("gy")
    planes = nx + 2 * WIDE
    source, iterate, cond, weight, diag2 = (
        store.at[pl.ds(k * planes, planes)] for k in range(5)
    )
    fields = (labels, source, iterate)
    all_y = n_gy * cy

    def exists(dx, dy):
        x, y = gx + dx, gy + dy
        return (x >= 0) & (x < n_gx) & (y >= 0) & (y < n_gy)

    near_slabs = [
        (dx, off) for off in reversed(range(n_gy)) for dx in (-1, 1, 0) if (dx, off) != (0, 0)
    ]

    nowhere = table_ref.shape[1]
    for i in range(planes):
        if i in (0, planes - 1):
            labels[i] = jnp.full((ny + 8, nz), nowhere, jnp.int32)
        else:
            labels[i, pl.ds(ny, 8), :] = jnp.full((8, nz), nowhere, jnp.int32)

    barrier = pltpu.get_barrier_semaphore()
    count = jnp.int32(0)
    for dx, off in near_slabs:
        if dx != 0 and off != 0:
            continue
        near = exists(dx, 0)

        @pl.when(near)
        def _():
            pl.semaphore_signal(
                barrier, inc=1, device_id=(gx + dx, lax.rem(gy + off, n_gy)), device_id_type=MESH
            )

        count = count + near.astype(jnp.int32)

    load_source = pltpu.make_async_copy(
        source_ref, source.at[pl.ds(first, nx), pl.ds(0, ny)], in_sem.at[0]
    )
    load_region = pltpu.make_async_copy(
        region_ref, labels.at[pl.ds(first, nx), pl.ds(0, ny)], in_sem.at[1]
    )
    load_table = pltpu.make_async_copy(table_in, table_ref, in_sem.at[2])
    load_owners = pltpu.make_async_copy(owners_in, owners_ref, in_sem.at[3])
    load_region.start()
    load_table.start()
    load_source.start()
    load_owners.start()

    def box(kind, dx, dy):
        if dx == 0:
            w, high = nx, HALF
        elif dy == 0:
            w, high = BESIDE[kind], ny
        else:
            w, high = CORNER[kind]
        plane = nx - w if dx > 0 else 0
        land = {0: first, -1: last, 1: first - w}[dx]
        row = ny - high if dy > 0 else 0
        to = {0: 0, -1: ny, 1: ny + 8 - high}[dy]
        return (plane, w, row, high), (land, w, to, high)

    def move(kind, dx, dy, here, there):
        plane, w, row, high = here
        land, _, to, _ = there
        return pltpu.make_async_remote_copy(
            src_ref=fields[kind].at[pl.ds(first + plane, w), pl.ds(row, high)],
            dst_ref=fields[kind].at[pl.ds(land, w), pl.ds(to, high)],
            send_sem=send_sem.at[0],
            recv_sem=recv_sem.at[
                5 if kind == REGION and dx * dy else 2 * kind + abs(dx) * (kind != ITERATE)
            ],
            device_id=(gx + dx, gy + dy),
            device_id_type=MESH,
        )

    def strips(kind, dx):
        far = STRIP[kind]
        plane, land = (nx - far, first - far) if dx > 0 else (far - 1, last + far - 1)
        for row in (0, ny - EDGE):
            yield move(kind, dx, 0, (plane, 1, row, EDGE), (land, 1, row, EDGE))

    def ship(dx):
        side = (1 - dx) // 2
        return pltpu.make_async_remote_copy(
            src_ref=shipped.at[2 + side],
            dst_ref=shipped.at[side],
            send_sem=send_sem.at[0],
            recv_sem=recv_sem.at[8],
            device_id=(gx + dx, gy),
            device_id_type=MESH,
        )

    def far(dx):
        return lax.rem(gx + (dx + 1) // 2, 4) == 0

    def to_group(sem):
        for off in range(1, n_gy):
            pl.semaphore_signal(
                sem, inc=1, device_id=(gx, lax.rem(gy + off, n_gy)), device_id_type=MESH
            )

    def send(kind, corners=(False, True), late=None):
        for dx, dy in STEPS:
            if (dx * dy != 0) not in corners:
                continue
            now = exists(dx, dy)
            if late is not None and dx != 0:
                now = now & (far(dx) == late)
            elif late:
                continue

            @pl.when(now)
            def _():
                move(kind, dx, dy, *box(kind, dx, dy)).start()
                if dy == 0 and kind != ITERATE:
                    for strip in strips(kind, dx):
                        strip.start()

    def by_neighbours(act):
        for a in (1, 2):
            for b in (1, 2) if n_gy > 2 else (1,):
                xs = exists(-1, 0).astype(jnp.int32) + exists(1, 0).astype(jnp.int32)
                ys = exists(0, -1).astype(jnp.int32) + exists(0, 1).astype(jnp.int32)

                @pl.when((xs == a) & (ys == b))
                def _():
                    act(a, b)

    def wait(ref, sem):
        pltpu.make_async_copy(ref, ref, sem).wait()

    def of_rows(n):
        high = next(r for r in (40, 32, 24, 16, 8, HALF) if n % r == 0 and r <= store.shape[1])
        return store.at[pl.ds(0, n // high), pl.ds(0, high)]

    def beside(kind, b):
        n = BESIDE[kind] * ny + b * CORNER[kind][0] * CORNER[kind][1]
        return n + (0 if kind == ITERATE else 2 * EDGE)

    def receive(kind, inner):
        def act(a, b):
            n = nx * b * HALF if inner else a * beside(kind, 0 if kind == REGION else b)
            if kind == ITERATE:
                n += nx * b * HALF
            wait(of_rows(n), recv_sem.at[2 * kind + (not inner and kind != ITERATE)])

        by_neighbours(act)

    def group_rows(a):
        return (a * n_gy + n_gy - 1) * cx * cy * cz // nz

    def finish(a, b):
        beside_x = a * (sum(beside(kind, b) for kind in range(3)) + ny)
        wait(of_rows(3 * nx * b * HALF + beside_x), send_sem.at[0])
        wait(of_rows(2 * group_rows(a) + 8 * a * cz // nz), send_sem.at[1])

    def gather(kind, dx, off):
        at = pl.ds(pl.multiple_of(all_y + gy * cy, 8), cy)
        to = pl.ds(pl.multiple_of((1 - dx) * all_y + gy * cy, 8), cy)
        return pltpu.make_async_remote_copy(
            src_ref=group.at[kind, :, at],
            dst_ref=group.at[kind, :, to],
            send_sem=send_sem.at[1],
            recv_sem=recv_sem.at[6 + kind],
            device_id=(gx + dx, lax.rem(gy + off, n_gy)),
            device_id_type=MESH,
        )

    def tell(dx):
        return pltpu.make_async_remote_copy(
            src_ref=holders.at[1],
            dst_ref=holders.at[1 - dx],
            send_sem=send_sem.at[1],
            recv_sem=recv_sem.at[6],
            device_id=(gx + dx, gy),
            device_id_type=MESH,
        )

    def gather_start(kind):
        for dx, off in near_slabs:
            @pl.when(exists(dx, 0))
            def _():
                gather(kind, dx, off).start()

    def gather_wait(kind):
        told = 0 if kind else 8 * cz // nz
        by_neighbours(lambda a, b: wait(
            of_rows(group_rows(a) + a * told), recv_sem.at[6 + kind]
        ))

    for dy in (-1, 1):
        @pl.when(jnp.logical_not(exists(0, -dy)))
        def _():
            at = pl.ds(ny if dy < 0 else ny + HALF, HALF)
            for ref in (source, iterate):
                ref[:, at, :] = jnp.zeros((planes, HALF, nz), jnp.float32)
    for dx in (-1, 1):
        @pl.when(jnp.logical_not(exists(-dx, 0)))
        def _():
            at = pl.ds(last if dx < 0 else 0, WIDE)
            labels[at] = jnp.full((WIDE, ny + 8, nz), nowhere, jnp.int32)
            for ref in (source, iterate):
                ref[at] = jnp.zeros((WIDE, ny + 8, nz), jnp.float32)
            shipped[(1 - dx) // 2] = jnp.zeros((ny, nz), jnp.float32)
            for kind in range(2):
                ref = group.at[kind, :, pl.ds((1 - dx) * all_y, all_y)]
                ref[...] = jnp.zeros(ref.shape, jnp.float32)
            ref = holders.at[1 - dx]
            ref[...] = jnp.zeros(ref.shape, jnp.float32)

    with jax.named_scope("wait_neighbours"):
        pl.semaphore_wait(barrier, count)
    with jax.named_scope("wait_own_region"):
        load_region.wait()
    send(REGION, (False,))
    to_group(ready_sem)
    load_source.wait()
    send(SOURCE, (False,), False)

    load_owners.wait()
    eight = lax.broadcasted_iota(jnp.int32, (8, cz), 0)
    held = jnp.zeros((8, cz), jnp.float32)
    for c in range(n_gy):
        held = jnp.where(eight == c, owners_ref[0, c].astype(jnp.float32), held)
    holders[1] = held
    for dx in (-1, 1):
        @pl.when(exists(dx, 0))
        def _():
            tell(dx).start()

    load_table.wait()
    regions = table_ref.shape[1]
    pair = jnp.concatenate([table_ref[...], jnp.zeros((1, 128 - regions), jnp.float32)], axis=1)
    table = jnp.broadcast_to(pair, (8, 128))

    def look_up(planes, tiles):
        for i in planes:
            for r in tiles:
                for c in range(0, nz, 128):
                    spot = labels[i, pl.ds(r, 8), pl.ds(c, 128)]
                    cond[i, pl.ds(r, 8), pl.ds(c, 128)] = jnp.take_along_axis(table, spot, axis=1)

    look_up(range(first, last), range(0, ny, 8))

    rows = ny + 8

    def blend(a, b, c, keep=rows):
        u = b + 0.5 * (a + c)
        u = u + 0.5 * (pltpu.roll(u, 1, 0) + pltpu.roll(u, rows - 1, 0))
        u = u[:keep]
        parts = [u[:, c:c + 128] for c in range(0, nz, 128)]
        up = [pltpu.roll(p, 1, 1) for p in parts]
        down = [pltpu.roll(p, 127, 1) for p in parts]
        mixed = []
        for j, p in enumerate(parts):
            low = jnp.where(lane128[:1] == 0, up[j - 1] if j else 0.0, up[j])
            high = jnp.where(lane128[:1] == 127, down[j + 1] if j + 1 < len(parts) else 0.0, down[j])
            mixed.append(p + 0.5 * (low + high))
        return jnp.concatenate(mixed, axis=1)

    lane128 = lax.broadcasted_iota(jnp.int32, (8, 128), 1)
    even = lax.rem(2 * lane128, jnp.int32(128))
    half_of = lane128 // 2

    def coarsen(pairs, kind):
        for i, pair_sum in enumerate(pairs):
            for r in range(0, ny, 8):
                halves = (pair_sum[r:r + 8, :128], pair_sum[r:r + 8, 128:])
                evens = [jnp.take_along_axis(h, even, axis=1) for h in halves]
                odds = [jnp.take_along_axis(h, even + 1, axis=1) for h in halves]
                squeezed[i, pl.ds(r, 8), :] = (
                    jnp.where(lane128 < 64, *evens) + jnp.where(lane128 < 64, *odds)
                )
            block = squeezed[i, pl.ds(0, cy, stride=2), :] + squeezed[i, pl.ds(1, cy, stride=2), :]
            group[kind, i, pl.ds(pl.multiple_of(all_y + gy * cy, 8), cy), :] = 0.125 * block

    for dx, i in ((1, last - EDGE), (-1, first + EDGE - 1)):
        mine = cond[i, pl.ds(0, ny), :]
        mixed = blend(cond[i - 1], cond[i], cond[i + 1], ny)
        shipped[2 + (1 - dx) // 2] = (
            RELAX_WEIGHT * source[i, pl.ds(0, ny), :] / (MASS_TERM + 6.0 * mine + mixed)
        )

        @pl.when(exists(dx, 0) & jnp.logical_not(far(dx)))
        def _():
            ship(dx).start()

    with jax.named_scope("wait_corners"):
        pl.semaphore_wait(ready_sem, n_gy - 1)
    send(REGION, (True,))
    send(SOURCE, (True,))
    coarsen(
        [cond[first + 2 * i, pl.ds(0, ny), :] + cond[first + 2 * i + 1, pl.ds(0, ny), :]
         for i in range(cx)],
        0,
    )

    row = lax.broadcasted_iota(jnp.int32, (rows, 1), 0)
    y = gy * ny + jnp.where(row < ny + HALF, row, row - rows)
    in_y = jnp.where((y >= 0) & (y < n_gy * ny), RELAX_WEIGHT, 0.0)

    def weigh(at):
        for i in at:
            mine = cond[i]
            mixed = blend(cond[i - 1], mine, cond[i + 1])
            x = gx * nx + (i - first)
            in_x = jnp.where((x >= 0) & (x < n_gx * nx), 1.0, 0.0)
            weight[i] = (in_y * in_x) / (MASS_TERM + 6.0 * mine + mixed)
            diag2[i] = MASS_TERM + 8.0 * mine + mixed

    with jax.named_scope("pace"):
        to_group(pace_sem)
        pl.semaphore_wait(pace_sem, n_gy - 1)
    send(SOURCE, (False,), True)
    for dx in (-1, 1):
        @pl.when(exists(dx, 0) & far(dx))
        def _():
            ship(dx).start()

    with jax.named_scope("wait_region_rows"):
        receive(REGION, True)
    look_up(range(first, last), (ny,))
    weigh(range(first + 1, last - 1))
    with jax.named_scope("wait_region_planes"):
        receive(REGION, False)
    edges = [*range(first - WIDE, first), *range(last, last + WIDE)]
    look_up(edges, range(0, ny, 8))
    with jax.named_scope("wait_region_corners"):
        by_neighbours(lambda a, b: wait(
            of_rows(a * b * CORNER[REGION][0] * CORNER[REGION][1]), recv_sem.at[5]
        ))
    look_up(edges, (ny,))
    weigh([first - 2, first - 1, first, last - 1, last, last + 1])
    with jax.named_scope("start_coarse_cond"):
        gather_start(0)
    def defect(i, values, flux, keep=rows):
        at = pl.ds(0, keep)
        lhs = cond[i, at] * blend(values[i - 1], values[i], values[i + 1], keep)
        rhs = blend(flux[i - 1], flux[i], flux[i + 1], keep)
        return source[i, at] - diag2[i, at] * values[i][:keep] + lhs + rhs

    values, flux, smooth = {}, {}, {}

    def first_sweep(at):
        for i in at:
            values[i] = weight[i] * source[i]
            if i in (first - EDGE, last + EDGE - 1):
                side = int(i > first)
                far = jnp.concatenate([shipped[side], jnp.zeros((8, nz), jnp.float32)])
                values[i] = jnp.where((row > 0) & (row < ny - 1), far, values[i])
            flux[i] = cond[i] * values[i]

    def second_sweep(at):
        for i in at:
            smooth[i] = values[i] + weight[i] * defect(i, values, flux)

    with jax.named_scope("wait_source_rows"):
        receive(SOURCE, True)
    first_sweep(range(first, last))
    second_sweep(range(first + 1, last - 1))
    with jax.named_scope("wait_source_planes"):
        receive(SOURCE, False)
    first_sweep((first - 1, last))
    second_sweep((first, last - 1))
    carried = {i: cond[i] * smooth[i] for i in range(first, last)}
    left = {i: defect(i, smooth, carried, ny) for i in range(first + 1, last - 1)}
    with jax.named_scope("wait_shipped"):
        by_neighbours(lambda a, b: wait(of_rows(a * ny), recv_sem.at[8]))
    first_sweep((first - 2, last + 1))
    second_sweep((first - 1, last))
    for i in (first - 1, last):
        carried[i] = cond[i] * smooth[i]
    for i in (first, last - 1):
        left[i] = defect(i, smooth, carried, ny)
    pairs = [left[first + 2 * i] + left[first + 2 * i + 1] for i in range(cx)]
    coarsen(pairs, 1)
    with jax.named_scope("start_coarse_res"):
        gather_start(1)
    for i in range(first, last):
        iterate[i, pl.ds(0, ny), :] = smooth[i][:ny]
    send(ITERATE)

    crow = lax.broadcasted_iota(jnp.int32, (all_y, cz), 0)
    clane = lax.broadcasted_iota(jnp.int32, (1, cz), 1)
    cz_low = jnp.where(clane == 0, 0.0, 0.5)
    cz_high = jnp.where(clane == cz - 1, 0.0, 0.5)

    def coarse_blend(planes, y_low, y_high):
        mixed = []
        for i, u in enumerate(planes):
            near = [planes[j] for j in (i - 1, i + 1) if 0 <= j < cx]
            u = u + 0.5 * functools.reduce(jnp.add, near) if near else u
            u = u + y_low * pltpu.roll(u, 1, 0) + y_high * pltpu.roll(u, all_y - 1, 0)
            mixed.append(u + cz_low * pltpu.roll(u, 1, 1) + cz_high * pltpu.roll(u, cz - 1, 1))
        return mixed

    def total(planes, c):
        whole = functools.reduce(jnp.add, [v[c * cy:(c + 1) * cy] for v in planes])
        return jnp.sum(whole, keepdims=True)

    with jax.named_scope("wait_coarse_cond"):
        gather_wait(0)
    slabs = []
    for g in range(3):
        held = [holders[g, pl.ds(c, 1), :] for c in range(n_gy)]
        same = lambda a, b: jnp.where(held[a] == held[b], 1.0, 0.0)
        y_low = jnp.where(crow == 0, 0.0, 0.5)
        y_high = jnp.where(crow == all_y - 1, 0.0, 0.5)
        for c in range(1, n_gy):
            tied = 0.5 * same(c - 1, c)
            y_low = jnp.where(crow == c * cy, tied, y_low)
            y_high = jnp.where(crow == c * cy - 1, tied, y_high)
        k = [group[0, i, pl.ds(g * all_y, all_y), :] for i in range(cx)]
        mixed = coarse_blend(k, y_low, y_high)
        diag = [MASS_TERM + 1.5 * a + 0.25 * b for a, b in zip(k, mixed)]
        step = [RELAX_WEIGHT / d for d in diag]
        ones = coarse_blend([jnp.ones((all_y, cz), jnp.float32)] * cx, y_low, y_high)
        slabs.append(dict(
            y_low=y_low, y_high=y_high, k=k, step=step,
            keep=[1.0 - s * (d + 0.5 * a) for s, d, a in zip(step, diag, k)],
            mine=[0.25 * s * a for s, a in zip(step, k)],
            theirs=[0.25 * s for s in step],
            drain=[MASS_TERM + 0.25 * a * (8.0 - b) for a, b in zip(k, ones)],
            same=[[same(a, b)[:, :1] for b in range(n_gy)] for a in range(n_gy)],
        ))
        s = slabs[-1]
        diag_sum = [total(diag, c) for c in range(n_gy)]
        for line in s["same"]:
            den = functools.reduce(jnp.add, [a * d for a, d in zip(line, diag_sum)])
            line[:] = [a / jnp.maximum(den, 1.0) for a in line]

    with jax.named_scope("wait_coarse_res"):
        gather_wait(1)
    e = []
    for g, s in enumerate(slabs):
        s["res"] = [group[1, i, pl.ds(g * all_y, all_y), :] for i in range(cx)]
        s["start"] = [a * b for a, b in zip(s["step"], s["res"])]
        e.append(s["start"])
    for _ in range(COARSE_SWEEPS - 1):
        for g, s in enumerate(slabs):
            straight = coarse_blend(e[g], s["y_low"], s["y_high"])
            carried = coarse_blend([a * v for a, v in zip(s["k"], e[g])], s["y_low"], s["y_high"])
            e[g] = [
                s["start"][i] + s["keep"][i] * e[g][i]
                + (s["mine"][i] * straight[i] + s["theirs"][i] * carried[i])
                for i in range(cx)
            ]
    keep_planes = ((0, cx - 1), *[(1, i) for i in range(cx)], (2, 0))
    ratios = []
    for g, s in enumerate(slabs):
        left = [r - d * v for r, d, v in zip(s["res"], s["drain"], e[g])]
        left = [total(left, c) for c in range(n_gy)]
        shares = []
        for c in range(n_gy):
            num = functools.reduce(jnp.add, [s["same"][c][b] * left[b] for b in range(n_gy)])
            shares.append(num)
        ratios.append(shares)
    for slot, (g, i) in enumerate(keep_planes):
        whole_corr[slot, pl.ds(0, 8), :] = jnp.zeros((8, cz), jnp.float32)
        whole_corr[slot, pl.ds(8, all_y), :] = e[g][i]
        whole_corr[slot, pl.ds(8 + all_y, 8), :] = jnp.zeros((8, cz), jnp.float32)

    sub = lax.broadcasted_iota(jnp.int32, (8, nz), 0)

    def of_column(g, column):
        found = jnp.zeros((1, 1), jnp.float32)
        for c in range(n_gy):
            found = jnp.where(column == c, ratios[g][c], found)
        return jnp.broadcast_to(found, (8, nz))

    shifts = [
        (of_column(g, gy), jnp.where(sub < HALF, of_column(g, gy + 1), of_column(g, gy - 1)))
        for g in range(3)
    ]
    for i, (g, _) in enumerate(keep_planes):
        mine = whole_corr[i, pl.ds(pl.multiple_of(8 + gy * cy, 8), cy), :]
        below = whole_corr[i, pl.ds(pl.multiple_of(gy * cy, 8), 8), :]
        above = whole_corr[i, pl.ds(pl.multiple_of(8 + gy * cy + cy, 8), 8), :]
        outer = jnp.where(
            sub[:, :cz] < HALF,
            jnp.broadcast_to(above[:1], (8, cz)),
            jnp.broadcast_to(below[7:], (8, cz)),
        )
        for part in range(2):
            at = half_of + 64 * part
            for r in range(0, cy, 8):
                tile = jnp.take_along_axis(mine[r:r + 8], at, axis=1) + shifts[g][0][:, :128]
                wide[i, part, pl.ds(2 * r, 8, stride=2), :] = tile
                wide[i, part, pl.ds(2 * r + 1, 8, stride=2), :] = tile
            wide[i, part, pl.ds(ny, 8), :] = (
                jnp.take_along_axis(outer, at, axis=1) + shifts[g][1][:, :128]
            )
    with jax.named_scope("wait_iterate_planes"):
        receive(ITERATE, False)
    values = {
        i: iterate[i] + jnp.concatenate([wide[(i - first + 2) // 2, part] for part in range(2)], axis=1)
        for i in range(first - 2, last + 2)
    }
    for sweep in range(POST_SWEEPS):
        reach = POST_SWEEPS - 1 - sweep
        keep = rows if reach else ny
        flux = {i: cond[i] * values[i] for i in values}
        values = {
            i: values[i][:keep] + weight[i, pl.ds(0, keep)] * defect(i, values, flux, keep)
            for i in range(first - reach, last + reach)
        }
    for i in range(nx):
        out_ref[i] = values[first + i][:ny]

    with jax.named_scope("wait_sends"):
        by_neighbours(finish)


def on_device(source, region, permeability, owners, *, n_gx, n_gy):
    nx, ny, nz = source.shape
    planes = nx + 2 * WIDE
    cx, all_y, cz = nx // 2, n_gy * ny // 2, nz // 2
    f32 = jnp.float32
    return pl.pallas_call(
        functools.partial(kernel, n_gx, n_gy),
        out_shape=jax.ShapeDtypeStruct(source.shape, f32),
        in_specs=[pl.BlockSpec(memory_space=pltpu.HBM)] * 4,
        out_specs=pl.BlockSpec(memory_space=pltpu.VMEM),
        scratch_shapes=[
            pltpu.SMEM((1, n_gy), jnp.int32),
            pltpu.VMEM((1, permeability.shape[0]), f32),
            pltpu.VMEM((planes, ny + 8, nz), jnp.int32),
            pltpu.VMEM((8 * planes, ny + 8, nz), f32),
            pltpu.VMEM((4, ny, nz), f32),
            pltpu.VMEM((2, cx, 3 * all_y, cz), f32),
            pltpu.VMEM((3, 8, cz), f32),
            pltpu.VMEM((cx, ny, cz), f32),
            pltpu.VMEM((cx + 2, all_y + 16, cz), f32),
            pltpu.VMEM((cx + 2, 2, ny + 8, cz), f32),
            pltpu.SemaphoreType.DMA((2,)),
            pltpu.SemaphoreType.DMA((9,)),
            pltpu.SemaphoreType.DMA((4,)),
            pltpu.SemaphoreType.REGULAR,
            pltpu.SemaphoreType.REGULAR,
        ],
        compiler_params=pltpu.CompilerParams(
            collective_id=0, has_side_effects=True, vmem_limit_bytes=56328192
        ),
    )(*[
        pltpu.with_memory_space_constraint(a, pltpu.HBM)
        for a in (owners, permeability[None, :], source, region)
    ])


def solution(mesh):
    placed = (P("gx", "gy", None), P("gx", "gy", None), P(), P("gx", None))
    body = functools.partial(on_device, n_gx=mesh.shape["gx"], n_gy=mesh.shape["gy"])
    return jax.shard_map(
        body, mesh=mesh, in_specs=placed, out_specs=P("gx", "gy", None), check_vma=False
    )
```

```python
import functools

import jax
import jax.numpy as jnp
from jax import lax
from jax.experimental import pallas as pl
from jax.experimental.pallas import tpu as pltpu
from jax.sharding import PartitionSpec as P

POST_SWEEPS = 2
COARSE_SWEEPS = 6
RELAX_WEIGHT = 0.6
MASS_TERM = 0.1

MESH = pl.DeviceIdType.MESH
WIDE = 3
HALF = 4
REGION, SOURCE, ITERATE = 0, 1, 2
EDGE = 2
BESIDE = (2, 1, 2)
CORNER = ((3, HALF), (2, EDGE), (2, HALF))
STRIP = (3, 2)
STEPS = ((-1, -1), (1, -1), (-1, 1), (1, 1), (0, -1), (0, 1), (-1, 0), (1, 0))


def kernel(
    n_gx, n_gy,
    owners_in, table_in, source_ref, region_ref, out_ref,
    owners_ref, table_ref, labels, store, shipped, group, holders, squeezed, whole_corr, wide,
    send_sem, recv_sem, in_sem, ready_sem, pace_sem,
):
    nx, ny, nz = out_ref.shape
    cx, cy, cz = nx // 2, ny // 2, nz // 2
    first, last = WIDE, WIDE + nx
    gx, gy = lax.axis_index("gx"), lax.axis_index("gy")
    planes = nx + 2 * WIDE
    source, iterate, cond, weight, diag2 = (
        store.at[pl.ds(k * planes, planes)] for k in range(5)
    )
    fields = (labels, source, iterate)
    all_y = n_gy * cy

    def exists(dx, dy):
        x, y = gx + dx, gy + dy
        return (x >= 0) & (x < n_gx) & (y >= 0) & (y < n_gy)

    near_slabs = [
        (dx, off) for off in reversed(range(n_gy)) for dx in (-1, 1, 0) if (dx, off) != (0, 0)
    ]

    nowhere = table_ref.shape[1]
    for i in range(planes):
        if i in (0, planes - 1):
            labels[i] = jnp.full((ny + 8, nz), nowhere, jnp.int32)
        else:
            labels[i, pl.ds(ny, 8), :] = jnp.full((8, nz), nowhere, jnp.int32)

    barrier = pltpu.get_barrier_semaphore()
    count = jnp.int32(0)
    for dx, off in near_slabs:
        if dx != 0 and off != 0:
            continue
        near = exists(dx, 0)

        @pl.when(near)
        def _():
            pl.semaphore_signal(
                barrier, inc=1, device_id=(gx + dx, lax.rem(gy + off, n_gy)), device_id_type=MESH
            )

        count = count + near.astype(jnp.int32)

    load_source = pltpu.make_async_copy(
        source_ref, source.at[pl.ds(first, nx), pl.ds(0, ny)], in_sem.at[0]
    )
    load_region = pltpu.make_async_copy(
        region_ref, labels.at[pl.ds(first, nx), pl.ds(0, ny)], in_sem.at[1]
    )
    load_table = pltpu.make_async_copy(table_in, table_ref, in_sem.at[2])
    load_owners = pltpu.make_async_copy(owners_in, owners_ref, in_sem.at[3])
    load_region.start()
    load_table.start()
    load_source.start()
    load_owners.start()

    def box(kind, dx, dy):
        if dx == 0:
            w, high = nx, HALF
        elif dy == 0:
            w, high = BESIDE[kind], ny
        else:
            w, high = CORNER[kind]
        plane = nx - w if dx > 0 else 0
        land = {0: first, -1: last, 1: first - w}[dx]
        row = ny - high if dy > 0 else 0
        to = {0: 0, -1: ny, 1: ny + 8 - high}[dy]
        return (plane, w, row, high), (land, w, to, high)

    def move(kind, dx, dy, here, there):
        plane, w, row, high = here
        land, _, to, _ = there
        return pltpu.make_async_remote_copy(
            src_ref=fields[kind].at[pl.ds(first + plane, w), pl.ds(row, high)],
            dst_ref=fields[kind].at[pl.ds(land, w), pl.ds(to, high)],
            send_sem=send_sem,
            recv_sem=in_sem.at[0] if kind == ITERATE else recv_sem.at[
                4 if kind == REGION and dx * dy else 2 * kind + abs(dx)
            ],
            device_id=(gx + dx, gy + dy),
            device_id_type=MESH,
        )

    def strips(kind, dx):
        far = STRIP[kind]
        plane, land = (nx - far, first - far) if dx > 0 else (far - 1, last + far - 1)
        for row in (0, ny - EDGE):
            yield move(kind, dx, 0, (plane, 1, row, EDGE), (land, 1, row, EDGE))

    def ship(dx):
        side = (1 - dx) // 2
        return pltpu.make_async_remote_copy(
            src_ref=shipped.at[2 + side],
            dst_ref=shipped.at[side],
            send_sem=send_sem,
            recv_sem=recv_sem.at[5],
            device_id=(gx + dx, gy),
            device_id_type=MESH,
        )

    def far(dx):
        return lax.rem(gx + (dx + 1) // 2, 4) == 0

    def to_group(sem):
        for off in range(1, n_gy):
            pl.semaphore_signal(
                sem, inc=1, device_id=(gx, lax.rem(gy + off, n_gy)), device_id_type=MESH
            )

    def send(kind, corners=(False, True), late=None):
        for dx, dy in STEPS:
            if (dx * dy != 0) not in corners:
                continue
            now = exists(dx, dy)
            if late is not None and dx != 0:
                now = now & (far(dx) == late)
            elif late:
                continue

            @pl.when(now)
            def _():
                move(kind, dx, dy, *box(kind, dx, dy)).start()
                if dy == 0 and kind != ITERATE:
                    for strip in strips(kind, dx):
                        strip.start()

    def by_neighbours(act):
        for a in (1, 2):
            for b in (1, 2) if n_gy > 2 else (1,):
                xs = exists(-1, 0).astype(jnp.int32) + exists(1, 0).astype(jnp.int32)
                ys = exists(0, -1).astype(jnp.int32) + exists(0, 1).astype(jnp.int32)

                @pl.when((xs == a) & (ys == b))
                def _():
                    act(a, b)

    def wait(ref, sem):
        pltpu.make_async_copy(ref, ref, sem).wait()

    def of_rows(n):
        high = next(r for r in (40, 32, 24, 16, 8, HALF) if n % r == 0 and r <= store.shape[1])
        return store.at[pl.ds(0, n // high), pl.ds(0, high)]

    def beside(kind, b):
        n = BESIDE[kind] * ny + b * CORNER[kind][0] * CORNER[kind][1]
        return n + (0 if kind == ITERATE else 2 * EDGE)

    def receive(kind, inner):
        def act(a, b):
            n = nx * b * HALF if inner else a * beside(kind, 0 if kind == REGION else b)
            if kind == ITERATE:
                n += nx * b * HALF
            wait(of_rows(n), in_sem.at[0] if kind == ITERATE else recv_sem.at[2 * kind + (not inner)])

        by_neighbours(act)

    def group_rows(a):
        return (a * n_gy + n_gy - 1) * cx * cy * cz // nz

    def finish(a, b):
        beside_x = a * (sum(beside(kind, b) for kind in range(3)) + ny)
        blocks = 2 * group_rows(a) + 8 * a * cz // nz
        wait(of_rows(3 * nx * b * HALF + beside_x + blocks), send_sem)

    def gather(kind, dx, off):
        at = pl.ds(pl.multiple_of(all_y + gy * cy, 8), cy)
        to = pl.ds(pl.multiple_of((1 - dx) * all_y + gy * cy, 8), cy)
        return pltpu.make_async_remote_copy(
            src_ref=group.at[kind, :, at],
            dst_ref=group.at[kind, :, to],
            send_sem=send_sem,
            recv_sem=in_sem.at[1] if kind else recv_sem.at[6],
            device_id=(gx + dx, lax.rem(gy + off, n_gy)),
            device_id_type=MESH,
        )

    def tell(dx):
        return pltpu.make_async_remote_copy(
            src_ref=holders.at[1],
            dst_ref=holders.at[1 - dx],
            send_sem=send_sem,
            recv_sem=recv_sem.at[6],
            device_id=(gx + dx, gy),
            device_id_type=MESH,
        )

    def gather_start(kind):
        for dx, off in near_slabs:
            @pl.when(exists(dx, 0))
            def _():
                gather(kind, dx, off).start()

    def gather_wait(kind):
        told = 0 if kind else 8 * cz // nz
        by_neighbours(lambda a, b: wait(
            of_rows(group_rows(a) + a * told), in_sem.at[1] if kind else recv_sem.at[6]
        ))

    for dy in (-1, 1):
        @pl.when(jnp.logical_not(exists(0, -dy)))
        def _():
            at = pl.ds(ny if dy < 0 else ny + HALF, HALF)
            for ref in (source, iterate):
                ref[:, at, :] = jnp.zeros((planes, HALF, nz), jnp.float32)
    for dx in (-1, 1):
        @pl.when(jnp.logical_not(exists(-dx, 0)))
        def _():
            at = pl.ds(last if dx < 0 else 0, WIDE)
            labels[at] = jnp.full((WIDE, ny + 8, nz), nowhere, jnp.int32)
            for ref in (source, iterate):
                ref[at] = jnp.zeros((WIDE, ny + 8, nz), jnp.float32)
            shipped[(1 - dx) // 2] = jnp.zeros((ny, nz), jnp.float32)
            for kind in range(2):
                ref = group.at[kind, :, pl.ds((1 - dx) * all_y, all_y)]
                ref[...] = jnp.zeros(ref.shape, jnp.float32)
            ref = holders.at[1 - dx]
            ref[...] = jnp.zeros(ref.shape, jnp.float32)

    with jax.named_scope("wait_neighbours"):
        pl.semaphore_wait(barrier, count)
    with jax.named_scope("wait_own_region"):
        load_region.wait()
    send(REGION, (False,))
    to_group(ready_sem)
    load_source.wait()
    send(SOURCE, (False,), False)

    load_owners.wait()
    eight = lax.broadcasted_iota(jnp.int32, (8, cz), 0)
    held = jnp.zeros((8, cz), jnp.float32)
    for c in range(n_gy):
        held = jnp.where(eight == c, owners_ref[0, c].astype(jnp.float32), held)
    holders[1] = held
    for dx in (-1, 1):
        @pl.when(exists(dx, 0))
        def _():
            tell(dx).start()

    load_table.wait()
    regions = table_ref.shape[1]
    pair = jnp.concatenate([table_ref[...], jnp.zeros((1, 128 - regions), jnp.float32)], axis=1)
    table = jnp.broadcast_to(pair, (8, 128))

    def look_up(planes, tiles):
        for i in planes:
            for r in tiles:
                for c in range(0, nz, 128):
                    spot = labels[i, pl.ds(r, 8), pl.ds(c, 128)]
                    cond[i, pl.ds(r, 8), pl.ds(c, 128)] = jnp.take_along_axis(table, spot, axis=1)

    look_up(range(first, last), range(0, ny, 8))

    rows = ny + 8

    def blend(a, b, c, keep=rows):
        u = b + 0.5 * (a + c)
        u = u + 0.5 * (pltpu.roll(u, 1, 0) + pltpu.roll(u, rows - 1, 0))
        u = u[:keep]
        parts = [u[:, c:c + 128] for c in range(0, nz, 128)]
        up = [pltpu.roll(p, 1, 1) for p in parts]
        down = [pltpu.roll(p, 127, 1) for p in parts]
        mixed = []
        for j, p in enumerate(parts):
            low = jnp.where(lane128[:1] == 0, up[j - 1] if j else 0.0, up[j])
            high = jnp.where(lane128[:1] == 127, down[j + 1] if j + 1 < len(parts) else 0.0, down[j])
            mixed.append(p + 0.5 * (low + high))
        return jnp.concatenate(mixed, axis=1)

    lane128 = lax.broadcasted_iota(jnp.int32, (8, 128), 1)
    even = lax.rem(2 * lane128, jnp.int32(128))
    half_of = lane128 // 2

    def coarsen(pairs, kind):
        for i, pair_sum in enumerate(pairs):
            for r in range(0, ny, 8):
                halves = (pair_sum[r:r + 8, :128], pair_sum[r:r + 8, 128:])
                evens = [jnp.take_along_axis(h, even, axis=1) for h in halves]
                odds = [jnp.take_along_axis(h, even + 1, axis=1) for h in halves]
                squeezed[i, pl.ds(r, 8), :] = (
                    jnp.where(lane128 < 64, *evens) + jnp.where(lane128 < 64, *odds)
                )
            block = squeezed[i, pl.ds(0, cy, stride=2), :] + squeezed[i, pl.ds(1, cy, stride=2), :]
            group[kind, i, pl.ds(pl.multiple_of(all_y + gy * cy, 8), cy), :] = 0.125 * block

    for dx, i in ((1, last - EDGE), (-1, first + EDGE - 1)):
        mine = cond[i, pl.ds(0, ny), :]
        mixed = blend(cond[i - 1], cond[i], cond[i + 1], ny)
        shipped[2 + (1 - dx) // 2] = (
            RELAX_WEIGHT * source[i, pl.ds(0, ny), :] / (MASS_TERM + 6.0 * mine + mixed)
        )

        @pl.when(exists(dx, 0) & jnp.logical_not(far(dx)))
        def _():
            ship(dx).start()

    with jax.named_scope("wait_corners"):
        pl.semaphore_wait(ready_sem, n_gy - 1)
    send(REGION, (True,))
    send(SOURCE, (True,))
    coarsen(
        [cond[first + 2 * i, pl.ds(0, ny), :] + cond[first + 2 * i + 1, pl.ds(0, ny), :]
         for i in range(cx)],
        0,
    )

    row = lax.broadcasted_iota(jnp.int32, (rows, 1), 0)
    y = gy * ny + jnp.where(row < ny + HALF, row, row - rows)
    in_y = jnp.where((y >= 0) & (y < n_gy * ny), RELAX_WEIGHT, 0.0)

    def weigh(at):
        for i in at:
            mine = cond[i]
            mixed = blend(cond[i - 1], mine, cond[i + 1])
            x = gx * nx + (i - first)
            in_x = jnp.where((x >= 0) & (x < n_gx * nx), 1.0, 0.0)
            weight[i] = (in_y * in_x) / (MASS_TERM + 6.0 * mine + mixed)
            diag2[i] = MASS_TERM + 8.0 * mine + mixed

    with jax.named_scope("pace"):
        to_group(pace_sem)
        pl.semaphore_wait(pace_sem, n_gy - 1)
    send(SOURCE, (False,), True)
    for dx in (-1, 1):
        @pl.when(exists(dx, 0) & far(dx))
        def _():
            ship(dx).start()

    with jax.named_scope("wait_region_rows"):
        receive(REGION, True)
    look_up(range(first, last), (ny,))
    weigh(range(first + 1, last - 1))
    with jax.named_scope("wait_region_planes"):
        receive(REGION, False)
    edges = [*range(first - WIDE, first), *range(last, last + WIDE)]
    look_up(edges, range(0, ny, 8))
    with jax.named_scope("wait_region_corners"):
        by_neighbours(lambda a, b: wait(
            of_rows(a * b * CORNER[REGION][0] * CORNER[REGION][1]), recv_sem.at[4]
        ))
    look_up(edges, (ny,))
    weigh([first - 2, first - 1, first, last - 1, last, last + 1])
    with jax.named_scope("start_coarse_cond"):
        gather_start(0)
    def defect(i, values, flux, keep=rows):
        at = pl.ds(0, keep)
        lhs = cond[i, at] * blend(values[i - 1], values[i], values[i + 1], keep)
        rhs = blend(flux[i - 1], flux[i], flux[i + 1], keep)
        return source[i, at] - diag2[i, at] * values[i][:keep] + lhs + rhs

    values, flux, smooth = {}, {}, {}

    def first_sweep(at):
        for i in at:
            values[i] = weight[i] * source[i]
            if i in (first - EDGE, last + EDGE - 1):
                side = int(i > first)
                far = jnp.concatenate([shipped[side], jnp.zeros((8, nz), jnp.float32)])
                values[i] = jnp.where((row > 0) & (row < ny - 1), far, values[i])
            flux[i] = cond[i] * values[i]

    def second_sweep(at):
        for i in at:
            smooth[i] = values[i] + weight[i] * defect(i, values, flux)

    with jax.named_scope("wait_source_rows"):
        receive(SOURCE, True)
    first_sweep(range(first, last))
    second_sweep(range(first + 1, last - 1))
    with jax.named_scope("wait_source_planes"):
        receive(SOURCE, False)
    first_sweep((first - 1, last))
    second_sweep((first, last - 1))
    carried = {i: cond[i] * smooth[i] for i in range(first, last)}
    left = {i: defect(i, smooth, carried, ny) for i in range(first + 1, last - 1)}
    with jax.named_scope("wait_shipped"):
        by_neighbours(lambda a, b: wait(of_rows(a * ny), recv_sem.at[5]))
    first_sweep((first - 2, last + 1))
    second_sweep((first - 1, last))
    for i in (first - 1, last):
        carried[i] = cond[i] * smooth[i]
    for i in (first, last - 1):
        left[i] = defect(i, smooth, carried, ny)
    pairs = [left[first + 2 * i] + left[first + 2 * i + 1] for i in range(cx)]
    coarsen(pairs, 1)
    with jax.named_scope("start_coarse_res"):
        gather_start(1)
    for i in range(first, last):
        iterate[i, pl.ds(0, ny), :] = smooth[i][:ny]
    send(ITERATE)

    crow = lax.broadcasted_iota(jnp.int32, (all_y, cz), 0)
    clane = lax.broadcasted_iota(jnp.int32, (1, cz), 1)
    cz_low = jnp.where(clane == 0, 0.0, 0.5)
    cz_high = jnp.where(clane == cz - 1, 0.0, 0.5)

    def coarse_blend(planes, y_low, y_high):
        mixed = []
        for i, u in enumerate(planes):
            near = [planes[j] for j in (i - 1, i + 1) if 0 <= j < cx]
            u = u + 0.5 * functools.reduce(jnp.add, near) if near else u
            u = u + y_low * pltpu.roll(u, 1, 0) + y_high * pltpu.roll(u, all_y - 1, 0)
            mixed.append(u + cz_low * pltpu.roll(u, 1, 1) + cz_high * pltpu.roll(u, cz - 1, 1))
        return mixed

    def total(planes, c):
        whole = functools.reduce(jnp.add, [v[c * cy:(c + 1) * cy] for v in planes])
        return jnp.sum(whole, keepdims=True)

    with jax.named_scope("wait_coarse_cond"):
        gather_wait(0)
    slabs = []
    for g in range(3):
        held = [holders[g, pl.ds(c, 1), :] for c in range(n_gy)]
        same = lambda a, b: jnp.where(held[a] == held[b], 1.0, 0.0)
        y_low = jnp.where(crow == 0, 0.0, 0.5)
        y_high = jnp.where(crow == all_y - 1, 0.0, 0.5)
        for c in range(1, n_gy):
            tied = 0.5 * same(c - 1, c)
            y_low = jnp.where(crow == c * cy, tied, y_low)
            y_high = jnp.where(crow == c * cy - 1, tied, y_high)
        k = [group[0, i, pl.ds(g * all_y, all_y), :] for i in range(cx)]
        mixed = coarse_blend(k, y_low, y_high)
        diag = [MASS_TERM + 1.5 * a + 0.25 * b for a, b in zip(k, mixed)]
        step = [RELAX_WEIGHT / d for d in diag]
        ones = coarse_blend([jnp.ones((all_y, cz), jnp.float32)] * cx, y_low, y_high)
        slabs.append(dict(
            y_low=y_low, y_high=y_high, k=k, step=step,
            keep=[1.0 - s * (d + 0.5 * a) for s, d, a in zip(step, diag, k)],
            mine=[0.25 * s * a for s, a in zip(step, k)],
            theirs=[0.25 * s for s in step],
            drain=[MASS_TERM + 0.25 * a * (8.0 - b) for a, b in zip(k, ones)],
            same=[[same(a, b)[:, :1] for b in range(n_gy)] for a in range(n_gy)],
        ))
        s = slabs[-1]
        diag_sum = [total(diag, c) for c in range(n_gy)]
        for line in s["same"]:
            den = functools.reduce(jnp.add, [a * d for a, d in zip(line, diag_sum)])
            line[:] = [a / jnp.maximum(den, 1.0) for a in line]

    with jax.named_scope("wait_coarse_res"):
        gather_wait(1)
    e = []
    for g, s in enumerate(slabs):
        s["res"] = [group[1, i, pl.ds(g * all_y, all_y), :] for i in range(cx)]
        s["start"] = [a * b for a, b in zip(s["step"], s["res"])]
        e.append(s["start"])
    for _ in range(COARSE_SWEEPS - 1):
        for g, s in enumerate(slabs):
            straight = coarse_blend(e[g], s["y_low"], s["y_high"])
            carried = coarse_blend([a * v for a, v in zip(s["k"], e[g])], s["y_low"], s["y_high"])
            e[g] = [
                s["start"][i] + s["keep"][i] * e[g][i]
                + (s["mine"][i] * straight[i] + s["theirs"][i] * carried[i])
                for i in range(cx)
            ]
    keep_planes = ((0, cx - 1), *[(1, i) for i in range(cx)], (2, 0))
    ratios = []
    for g, s in enumerate(slabs):
        left = [r - d * v for r, d, v in zip(s["res"], s["drain"], e[g])]
        left = [total(left, c) for c in range(n_gy)]
        shares = []
        for c in range(n_gy):
            num = functools.reduce(jnp.add, [s["same"][c][b] * left[b] for b in range(n_gy)])
            shares.append(num)
        ratios.append(shares)
    for slot, (g, i) in enumerate(keep_planes):
        whole_corr[slot, pl.ds(0, 8), :] = jnp.zeros((8, cz), jnp.float32)
        whole_corr[slot, pl.ds(8, all_y), :] = e[g][i]
        whole_corr[slot, pl.ds(8 + all_y, 8), :] = jnp.zeros((8, cz), jnp.float32)

    sub = lax.broadcasted_iota(jnp.int32, (8, nz), 0)

    def of_column(g, column):
        found = jnp.zeros((1, 1), jnp.float32)
        for c in range(n_gy):
            found = jnp.where(column == c, ratios[g][c], found)
        return jnp.broadcast_to(found, (8, nz))

    shifts = [
        (of_column(g, gy), jnp.where(sub < HALF, of_column(g, gy + 1), of_column(g, gy - 1)))
        for g in range(3)
    ]
    for i, (g, _) in enumerate(keep_planes):
        mine = whole_corr[i, pl.ds(pl.multiple_of(8 + gy * cy, 8), cy), :]
        below = whole_corr[i, pl.ds(pl.multiple_of(gy * cy, 8), 8), :]
        above = whole_corr[i, pl.ds(pl.multiple_of(8 + gy * cy + cy, 8), 8), :]
        outer = jnp.where(
            sub[:, :cz] < HALF,
            jnp.broadcast_to(above[:1], (8, cz)),
            jnp.broadcast_to(below[7:], (8, cz)),
        )
        for part in range(2):
            at = half_of + 64 * part
            for r in range(0, cy, 8):
                tile = jnp.take_along_axis(mine[r:r + 8], at, axis=1) + shifts[g][0][:, :128]
                wide[i, part, pl.ds(2 * r, 8, stride=2), :] = tile
                wide[i, part, pl.ds(2 * r + 1, 8, stride=2), :] = tile
            wide[i, part, pl.ds(ny, 8), :] = (
                jnp.take_along_axis(outer, at, axis=1) + shifts[g][1][:, :128]
            )
    with jax.named_scope("wait_iterate_planes"):
        receive(ITERATE, False)
    values = {
        i: iterate[i] + jnp.concatenate([wide[(i - first + 2) // 2, part] for part in range(2)], axis=1)
        for i in range(first - 2, last + 2)
    }
    for sweep in range(POST_SWEEPS):
        reach = POST_SWEEPS - 1 - sweep
        keep = rows if reach else ny
        flux = {i: cond[i] * values[i] for i in values}
        values = {
            i: values[i][:keep] + weight[i, pl.ds(0, keep)] * defect(i, values, flux, keep)
            for i in range(first - reach, last + reach)
        }
    for i in range(nx):
        out_ref[i] = values[first + i][:ny]

    with jax.named_scope("wait_sends"):
        by_neighbours(finish)


def on_device(source, region, permeability, owners, *, n_gx, n_gy):
    nx, ny, nz = source.shape
    planes = nx + 2 * WIDE
    cx, all_y, cz = nx // 2, n_gy * ny // 2, nz // 2
    f32 = jnp.float32
    return pl.pallas_call(
        functools.partial(kernel, n_gx, n_gy),
        out_shape=jax.ShapeDtypeStruct(source.shape, f32),
        in_specs=[pl.BlockSpec(memory_space=pltpu.HBM)] * 4,
        out_specs=pl.BlockSpec(memory_space=pltpu.VMEM),
        scratch_shapes=[
            pltpu.SMEM((1, n_gy), jnp.int32),
            pltpu.VMEM((1, permeability.shape[0]), f32),
            pltpu.VMEM((planes, ny + 8, nz), jnp.int32),
            pltpu.VMEM((15 * planes, ny + 8, nz), f32),
            pltpu.VMEM((4, ny, nz), f32),
            pltpu.VMEM((2, cx, 3 * all_y, cz), f32),
            pltpu.VMEM((3, 8, cz), f32),
            pltpu.VMEM((cx, ny, cz), f32),
            pltpu.VMEM((cx + 2, all_y + 16, cz), f32),
            pltpu.VMEM((cx + 2, 2, ny + 8, cz), f32),
            pltpu.SemaphoreType.DMA,
            pltpu.SemaphoreType.DMA((7,)),
            pltpu.SemaphoreType.DMA((4,)),
            pltpu.SemaphoreType.REGULAR,
            pltpu.SemaphoreType.REGULAR,
        ],
        compiler_params=pltpu.CompilerParams(
            collective_id=0, has_side_effects=True, vmem_limit_bytes=56328192
        ),
    )(*[
        pltpu.with_memory_space_constraint(a, pltpu.HBM)
        for a in (owners, permeability[None, :], source, region)
    ])


def solution(mesh):
    placed = (P("gx", "gy", None), P("gx", "gy", None), P(), P("gx", None))
    body = functools.partial(on_device, n_gx=mesh.shape["gx"], n_gy=mesh.shape["gy"])
    return jax.shard_map(
        body, mesh=mesh, in_specs=placed, out_specs=P("gx", "gy", None), check_vma=False
    )
```
